32 devices in a mesh: pb: 8 (over z, y), ka: 4 (over x, core).
Axes of the slice: x: 2, y: 2, z: 4, core: 2. Of those that a mesh axis runs over, the one named last changes fastest.
Arguments:
- tokens: bfloat16 [16384, 768], P(('pb', 'ka')), may hold values from -6 to 6
- lengths: int32 [8, 2], P('pb'), may hold values from 0 to 2048, as said below
- block_place: int32 [8, 16], P('pb'), may hold values from 0 to 15, as said below
- qkv_weight: bfloat16 [768, 2304], P(('pb', 'ka')), may hold values from -0.21875 to 0.21875
- out_weight: bfloat16 [768, 768], P(('pb', 'ka')), may hold values from -2.5 to 2.5
- up_weight: bfloat16 [768, 3072], P(('pb', 'ka')), may hold values from -0.21875 to 0.21875
- down_weight: bfloat16 [3072, 768], P(('pb', 'ka')), may hold values from -0.109375 to 0.109375
- attn_gain: bfloat16 [768], P(('pb', 'ka')), may hold values from 0.5 to 1.5
- mlp_gain: bfloat16 [768], P(('pb', 'ka')), may hold values from 0.5 to 1.5
- cotangent: bfloat16 [16384, 768], P(('pb', 'ka')), may hold values from -6 to 6
Outputs:
- mixed: bfloat16 [16384, 768], P(('pb', 'ka'))
- tokens_grad: bfloat16 [16384, 768], P(('pb', 'ka'))
- grad_qkv: float32 [768, 2304], P(('pb', 'ka'))
- grad_out: float32 [768, 768], P(('pb', 'ka'))
- grad_up: float32 [768, 3072], P(('pb', 'ka'))
- grad_down: float32 [3072, 768], P(('pb', 'ka'))
- grad_attn_gain: float32 [768], P(('pb', 'ka'))
- grad_mlp_gain: float32 [768], P(('pb', 'ka'))
The draws below stay inside these ranges and needn't reach their ends.
Inputs may be any that keep to these rules, and one draw needn't show every extreme that they name: Row g lists the lengths of the sequences of group g: the nonzero entries come first, are equal, each is 1024 times a power of two, and they sum to 2048; in every draw some group holds one sequence of 2048 tokens. `block_place`: row g is a permutation of 0 to 15. Entry k * 4 + t names the block of 128 positions held in slot t of the k-th device of ka. For each t, the blocks t * (4) up to t * 4 + 16 // 4 - 1 fill slot t of the devices of ka, one on each.
All inputs are finite; a program needn't handle non-finite values.
Results may differ from the reference program's by a relative error of at most 0.018.
Values may be sent and summed in bfloat16 or wider, within the bound.
No kernel may reach another device: no remote copies, remote signals or barrier semaphores. Data moves between devices by JAX's collectives and lax.ppermute only.
A program may use at most 192 MiB of HBM per device.

```python
import functools
import math
import jax
import jax.numpy as jnp
from jax import lax

D = 768
HEADS = 12
HEAD_DIM = 64
FF = 3072
BLK = 128
QBLK = 512
SEQ_UNIT = 1024
ROW = 2048
BUCKETS = 8
TOKENS = 16384
NSEQ = 2
SLOTS = 4
NBLK = 16


def draw_lengths(key, part):
    key = jax.random.fold_in(key, 11)
    unit_count = ROW // SEQ_UNIT
    levels = unit_count.bit_length() - 1
    level_key, chosen_key = jax.random.split(key)
    row_level = jax.random.randint(level_key, (BUCKETS,), 0, levels + 1)
    chosen = jax.random.randint(chosen_key, (), 0, BUCKETS)
    row_level = jnp.where(jnp.arange(BUCKETS) == chosen, levels, row_level).astype(jnp.int32)
    part_units = jnp.left_shift(jnp.int32(1), row_level)
    seq_count = jnp.right_shift(jnp.int32(unit_count), row_level)
    slot_ids = jnp.arange(NSEQ, dtype=jnp.int32)
    return jnp.where(slot_ids[None, :] < seq_count[:, None], (part_units * SEQ_UNIT)[:, None], 0).astype(jnp.int32)


def draw_block_place(key, part):
    key = jax.random.fold_in(key, 23)
    spread = NBLK // SLOTS
    group_keys = jax.random.split(key, BUCKETS * SLOTS)
    shuffled = jax.vmap(lambda one_key: jax.random.permutation(one_key, spread))(group_keys)
    member = shuffled.reshape(BUCKETS, SLOTS, spread).transpose(0, 2, 1)
    base = jnp.arange(SLOTS, dtype=jnp.int32) * spread
    return (member + base[None, None, :]).reshape(BUCKETS, NBLK).astype(jnp.int32)


def spiked(drawn, stream_key, source, target, blocks, factor):
    def block_of(dim):
        return (jnp.arange(drawn.shape[dim]) // (drawn.shape[dim] // blocks)).reshape((-1,) + (1,) * (drawn.ndim - 1 - dim))

    first = jax.random.permutation(stream_key, blocks)[block_of(target)]
    far = (block_of(target) + blocks // 2) % blocks
    return jnp.where((block_of(source) == first) | (block_of(source) == far), factor * drawn, drawn)


def steps_of(stream_key, dims, shards, least, top_value):
    gain, own = 1.0, jax.random.fold_in(stream_key, 6)
    for dim, shards_of in shards:
        steps = jnp.exp(jax.random.uniform(jax.random.fold_in(own, dim), (shards_of,), jnp.float32, least / len(shards), top_value / len(shards)))
        gain = gain * jnp.repeat(steps, dims[dim] // shards_of).reshape([-1 if axis == dim else 1 for axis in range(len(dims))])
    return gain


def normal_values(rng, dims, scale, most, shards=(), kind=jnp.bfloat16):
    values = jax.random.normal(rng, dims, jnp.float32) * scale
    if len(shards) > 0:
        values = steps_of(rng, dims, shards, -0.22, 0.18) * values
    return jnp.clip(values, min=-most, max=most).astype(kind)


def noise_with(own_key, shape, deviation, most, cuts, heavy, kind=jnp.bfloat16):
    array = deviation * jax.random.normal(own_key, shape, jnp.float32)
    if cuts:
        array = array * steps_of(own_key, shape, cuts, -0.22, 0.18)
    return jnp.clip(spiked(array, jax.random.fold_in(own_key, 3), *heavy), -most, most).astype(kind)


def setup_inputs(seed: int = 0) -> dict:
    arg_keys = jax.random.split(jax.random.key(seed), 11)
    return {
        "tokens": noise_with(arg_keys[0], (TOKENS, D), 1.0, 6.0, ((0, 32),), (0, 1, 32, 2.75)),
        "lengths": draw_lengths(jax.random.fold_in(arg_keys[10], 71), 0),
        "block_place": draw_block_place(jax.random.fold_in(arg_keys[10], 71), 0),
        "qkv_weight": normal_values(arg_keys[3], (D, 3 * D), D ** -0.5, 0.21875, ((0, 32),)),
        "out_weight": normal_values(arg_keys[4], (D, D), (D // 128) ** -0.5, 2.5, ((0, 32),)),
        "up_weight": normal_values(arg_keys[5], (D, FF), D ** -0.5, 0.21875, ((0, 32),)),
        "down_weight": normal_values(arg_keys[6], (FF, D), FF ** -0.5, 0.109375, ((0, 32),)),
        "attn_gain": jnp.clip(1.0 + 0.1 * jax.random.normal(arg_keys[7], (D,), jnp.float32), 0.5, 1.5).astype(jnp.bfloat16),
        "mlp_gain": jnp.clip(1.0 + 0.1 * jax.random.normal(arg_keys[8], (D,), jnp.float32), 0.5, 1.5).astype(jnp.bfloat16),
        "cotangent": normal_values(arg_keys[9], (TOKENS, D), 1.0, 6.0, ((0, 32),)),
    }


@jax.custom_vjp
def low(v):
    return lax.optimization_barrier(v.astype(jnp.bfloat16)).astype(jnp.float32)

@jax.custom_vjp
def low_back(v):
    return v

def low_keep(v):
    return (low(v), None)

def low_pass(kept, grad):
    return (grad,)

def back_keep(v):
    return (v, None)

def back_low(kept, grad):
    return (low(grad),)
low.defvjp(low_keep, low_pass)
low_back.defvjp(back_keep, back_low)
highest = lax.Precision.HIGHEST
epsilon = 1e-05

def norm_rows(values, gain_vec):
    row_mean = lax.optimization_barrier(jnp.mean(values, axis=-1, keepdims=True))
    centered = values - row_mean
    row_var = lax.optimization_barrier(jnp.mean(centered * centered, axis=-1, keepdims=True))
    return centered * lax.rsqrt(row_var + epsilon) * gain_vec

def gelu_tanh(values):
    return jax.nn.gelu(values, approximate=True)

def row_layout(lengths_row, place_row):
    offsets = jnp.arange(BLK, dtype=jnp.int32)
    positions = (place_row[:, None] * BLK + offsets[None, :]).reshape(-1).astype(jnp.int32)
    doc_ends = jnp.cumsum(lengths_row).astype(jnp.int32)
    documents = lax.optimization_barrier(jnp.sum((positions[:, None] >= doc_ends[None, :]).astype(jnp.int32), axis=1)).astype(jnp.int32)
    return (positions, documents)

def row_attention(queries, keys_all, values_all, positions, documents):
    score_scale = HEAD_DIM ** (-0.5)
    block_rows = math.gcd(QBLK, ROW)

    def one_block(block_id):
        begin = (block_id * block_rows).astype(jnp.int32)
        query_rows = lax.dynamic_slice_in_dim(queries, begin, block_rows, 0)
        query_pos = lax.dynamic_slice_in_dim(positions, begin, block_rows, 0)
        query_doc = lax.dynamic_slice_in_dim(documents, begin, block_rows, 0)
        scores = low_back(jnp.einsum('qhd,khd->hqk', query_rows, keys_all, precision=highest) * score_scale)
        visible = ((query_doc[:, None] == documents[None, :]) & (positions[None, :] <= query_pos[:, None]))[None]
        magnitude = jnp.sqrt(scores * scores + 1.0)
        masked = jnp.where(visible, magnitude, -1000000000.0)
        peak = lax.optimization_barrier(jnp.max(masked, axis=-1, keepdims=True))
        raised = jnp.exp(masked - peak)
        shares = raised / lax.optimization_barrier(jnp.sum(raised, axis=-1, keepdims=True))
        mixing = low(shares * scores / magnitude)
        return jnp.einsum('hqk,khd->qhd', mixing, values_all, precision=highest)
    blocks = lax.map(jax.checkpoint(one_block), jnp.arange(ROW // block_rows, dtype=jnp.int32))
    return blocks.reshape(ROW, D)

def layer(positions, documents, inputs, qkv_weight, out_weight, up_weight, down_weight, attn_gain, mlp_gain):
    normed_one = low(norm_rows(inputs, attn_gain))
    projected = low_back(low(jnp.dot(normed_one, qkv_weight, precision=highest)))
    shaped = projected.reshape(BUCKETS, ROW, 3, HEADS, HEAD_DIM)

    def one_row(running, row_items):
        row_proj, row_pos, row_doc = row_items
        return (running, row_attention(row_proj[:, 0], row_proj[:, 1], row_proj[:, 2], row_pos, row_doc))
    _, attended = lax.scan(one_row, jnp.zeros((), jnp.float32), (shaped, positions, documents))
    attended = low_back(low(attended.reshape(TOKENS, D)))
    residual = inputs + low_back(jnp.dot(attended, out_weight, precision=highest))
    normed_two = low(norm_rows(residual, mlp_gain))
    hidden_pre = low_back(jnp.dot(normed_two, up_weight, precision=highest))
    hidden_act = low(gelu_tanh(hidden_pre))
    return residual + jnp.dot(hidden_act, down_weight, precision=highest)

def reference(tokens, lengths, block_place, qkv_weight, out_weight, up_weight, down_weight, attn_gain, mlp_gain, cotangent):
    positions, documents = jax.vmap(row_layout)(lengths, block_place)
    forward = functools.partial(layer, positions, documents)
    layer_out, pullback = jax.vjp(forward, tokens.astype(jnp.float32), qkv_weight.astype(jnp.float32), out_weight.astype(jnp.float32), up_weight.astype(jnp.float32), down_weight.astype(jnp.float32), attn_gain.astype(jnp.float32), mlp_gain.astype(jnp.float32))
    grads = pullback(cotangent.astype(jnp.float32))
    return (layer_out.astype(jnp.bfloat16), grads[0].astype(jnp.bfloat16), grads[1], grads[2], grads[3], grads[4], grads[5], grads[6])
```

```python
import functools
import math

import jax
import jax.numpy as jnp
from jax import lax
from jax.experimental import pallas as pl
from jax.experimental.pallas import tpu as pltpu
from jax.sharding import PartitionSpec as P

HEADS = 12
HEAD_DIM = 64
BLK = 128
TILE = 256
epsilon = 1e-05
f32 = jnp.float32
bf16 = jnp.bfloat16


class Grid:
    def __init__(self, nb, nk):
        nhi = math.gcd(4, nb)
        nc = math.gcd(2, nk)
        self.sizes = {"hi": nhi, "lo": nb // nhi, "x": nk // nc, "c": nc}
        self.nb, self.nk = nb, nk
        pb, ka = lax.axis_index("pb"), lax.axis_index("ka")
        self.pb, self.ka = pb, ka
        self.at = {"hi": pb // self.sizes["lo"], "lo": pb % self.sizes["lo"], "x": ka // nc, "c": ka % nc}

    def fetch(self, value, **steps):
        n = self.sizes
        pairs = []
        for hi in range(n["hi"]):
            for lo in range(n["lo"]):
                for x in range(n["x"]):
                    for c in range(n["c"]):
                        here = {"hi": hi, "lo": lo, "x": x, "c": c}
                        there = {d: (here[d] + steps.get(d, 0)) % n[d] for d in here}
                        flat = [((p["hi"] * n["lo"] + p["lo"]) * n["x"] + p["x"]) * n["c"] + p["c"] for p in (there, here)]
                        pairs.append(tuple(flat))
        return lax.ppermute(value, ("pb", "ka"), pairs)

    def gather(self, value, dim):
        return jnp.stack([value] + [self.fetch(value, **{dim: r}) for r in range(1, self.sizes[dim])])

    def rolled(self, stacked, axis, dim):
        n = self.sizes[dim]
        if n == 1:
            return stacked
        twice = jnp.concatenate([stacked, lax.slice_in_dim(stacked, 0, n - 1, axis=axis)], axis=axis)
        return lax.dynamic_slice_in_dim(twice, (n - self.at[dim]) % n, n, axis=axis)

    def reduce(self, parts, axis, dim, last=False):
        n, me = self.sizes[dim], self.at[dim]
        total = lax.dynamic_index_in_dim(parts, me, axis, keepdims=False).astype(f32)
        for r in range(1, n):
            sent = lax.dynamic_index_in_dim(parts, (me - r) % n, axis, keepdims=False)
            total = total + self.fetch(sent, **{dim: r}).astype(f32)
        return total if last else total.astype(parts.dtype)


def place_kernel(counts, rows, offs_ref, *refs):
    ins, out_ref, sems = refs[: len(counts)], refs[len(counts)], refs[len(counts) + 1]
    copies = []
    for ref, count in zip(ins, counts):
        for i in range(count):
            at = pl.multiple_of(offs_ref[len(copies)], rows)
            copies.append(pltpu.make_async_copy(ref.at[i], out_ref.at[pl.ds(at, rows), :], sems.at[len(copies)]))
    for copy in copies:
        copy.start()
    for copy in copies:
        copy.wait()


def place(stacks, offsets):
    rows, cols = stacks[0].shape[1:]
    counts = [s.shape[0] for s in stacks]
    total = sum(counts)
    return pl.pallas_call(
        functools.partial(place_kernel, counts, rows),
        out_shape=jax.ShapeDtypeStruct((total * rows, cols), stacks[0].dtype),
        in_specs=[pl.BlockSpec(memory_space=pltpu.SMEM)] + [pl.BlockSpec(memory_space=pl.ANY)] * len(stacks),
        out_specs=pl.BlockSpec(memory_space=pl.ANY),
        scratch_shapes=[pltpu.SemaphoreType.DMA((total,))],
        cost_estimate=pl.CostEstimate(flops=0, bytes_accessed=4 * total * rows * cols, transcendentals=0),
    )(offsets.astype(jnp.int32), *stacks)


def gather_rows(grid, piece, order):
    stack = piece[None]
    steps = [dict()]
    stacks = []
    for dim in order:
        got = [grid.fetch(stack, **{dim: r}) for r in range(1, grid.sizes[dim])]
        steps = steps + [{**s, dim: r} for r in range(1, grid.sizes[dim]) for s in steps]
        if dim == order[-1]:
            stacks = [stack] + got
        else:
            stack = jnp.concatenate([stack] + got, axis=0)
    dims = [d for d in ("hi", "lo", "x") if d in order]
    rows = piece.shape[0]
    index = []
    for s in steps:
        at = 0
        for d in dims:
            at = at * grid.sizes[d] + (grid.at[d] + s.get(d, 0)) % grid.sizes[d]
        index.append(at)
    index = jnp.stack(index)
    if rows % 16 == 0:
        return place(stacks, index * rows)
    sizes = [grid.sizes[d] for d in reversed(order)]
    out = jnp.concatenate(stacks, axis=0).reshape(sizes + list(piece.shape))
    for axis, dim in enumerate(reversed(order)):
        out = grid.rolled(out, axis, dim)
    turn = [list(reversed(order)).index(d) for d in dims]
    return jnp.transpose(out, turn + [len(sizes), len(sizes) + 1]).reshape(-1, piece.shape[1])


def reduce_rows(grid, parts, order):
    dims = [d for d in ("hi", "lo", "x") if d in order]
    sizes = [grid.sizes[d] for d in dims]
    rows = parts.shape[0] // math.prod(sizes)
    parts = parts.reshape(sizes + [rows, parts.shape[1]])
    for dim in order:
        parts = grid.reduce(parts, dims.index(dim), dim, last=dim == order[-1])
        dims.remove(dim)
    return parts


def lane_tile(at, size):
    return pl.ds(pl.multiple_of(at, BLK), size)


def tile_scores(keys, queries):
    scores = jnp.dot(keys, queries, preferred_element_type=f32)
    square = scores * scores + 1.0
    return scores, square, lax.rsqrt(square)


def seen_tile(tile):
    return lax.broadcasted_iota(jnp.int32, (tile, tile), 0) <= lax.broadcasted_iota(jnp.int32, (tile, tile), 1)


def forward_kernel(heads, tile, meta_ref, qkv_ref, out_ref, att_ref, lse_ref, sorted_ref, keys_ref):
    row_len = qkv_ref.shape[1]
    width = heads * HEAD_DIM
    blocks = row_len // BLK
    per_device = out_ref.shape[2] // BLK
    for b in range(blocks):
        sorted_ref[:, b * BLK : (b + 1) * BLK] = qkv_ref[: 3 * width, lane_tile(meta_ref[b] * BLK, BLK)]
    for h in range(heads):
        keys_ref[h] = sorted_ref[width + h * HEAD_DIM : width + (h + 1) * HEAD_DIM, :].astype(f32).T.astype(bf16)
    doc_tiles = meta_ref[blocks] // tile
    seen = seen_tile(tile)
    lse_ref[...] = jnp.zeros_like(lse_ref)

    def one_query_tile(i, _):
        first = (i // doc_tiles) * doc_tiles

        def step(j, carry, diagonal):
            new = []
            for h in range(heads):
                peak, total, acc = carry[h]
                keys = keys_ref[h, pl.ds(pl.multiple_of(j * tile, tile), tile), :]
                queries = sorted_ref[h * HEAD_DIM : (h + 1) * HEAD_DIM, lane_tile(i * tile, tile)]
                scores, square, inverse = tile_scores(keys, queries)
                size = square * inverse
                if diagonal:
                    size = jnp.where(seen, size, -1e30)
                top = jnp.maximum(peak, jnp.max(size, axis=0, keepdims=True))
                shares = jnp.exp(size - top)
                fade = jnp.exp(peak - top)
                total = total * fade + jnp.sum(shares, axis=0, keepdims=True)
                mixing = (shares * (scores * inverse)).astype(bf16)
                values = sorted_ref[2 * width + h * HEAD_DIM : 2 * width + (h + 1) * HEAD_DIM, lane_tile(j * tile, tile)]
                acc = acc * fade + jnp.dot(values, mixing, preferred_element_type=f32)
                new.append((top, total, acc))
            return tuple(new)

        start = tuple(
            (jnp.ones((1, tile), f32), jnp.zeros((1, tile), f32), jnp.zeros((HEAD_DIM, tile), f32)) for _ in range(heads)
        )
        carry = lax.fori_loop(first, i, lambda j, c: step(j, c, False), start)
        carry = step(i, carry, True)
        for h in range(heads):
            peak, total, acc = carry[h]
            result = acc / total
            att_ref[h * HEAD_DIM : (h + 1) * HEAD_DIM, lane_tile(i * tile, tile)] = result
            lse_ref[h : h + 1, lane_tile(i * tile, tile)] = peak + jnp.log(total)
            low = result.astype(bf16)
            for part in range(tile // BLK):
                place_at = meta_ref[i * (tile // BLK) + part]
                out_ref[
                    place_at // per_device, h * HEAD_DIM : (h + 1) * HEAD_DIM, lane_tile((place_at % per_device) * BLK, BLK)
                ] = low[:, part * BLK : (part + 1) * BLK]
        return 0

    lax.fori_loop(0, row_len // tile, one_query_tile, 0)


def forward_attention(meta, qkv, heads, devices):
    row_len = qkv.shape[1]
    width = heads * HEAD_DIM
    tile = min(TILE, row_len)
    whole = pl.BlockSpec(memory_space=pltpu.VMEM)
    return pl.pallas_call(
        functools.partial(forward_kernel, heads, tile),
        out_shape=(
            jax.ShapeDtypeStruct((devices, width, row_len // devices), bf16),
            jax.ShapeDtypeStruct((width, row_len), f32),
            jax.ShapeDtypeStruct((8, row_len), f32),
        ),
        in_specs=[pl.BlockSpec(memory_space=pltpu.SMEM), whole],
        out_specs=(whole, whole, whole),
        scratch_shapes=[pltpu.VMEM((3 * width, row_len), bf16), pltpu.VMEM((heads, row_len, HEAD_DIM), bf16)],
        compiler_params=pltpu.CompilerParams(vmem_limit_bytes=40 * 2**20),
        cost_estimate=pl.CostEstimate(
            flops=2 * row_len * row_len * width, bytes_accessed=16 * row_len * width, transcendentals=heads * row_len * row_len
        ),
    )(meta, qkv)


def backward_kernel(
    heads, tile, meta_ref, qkv_ref, up_ref, att_ref, lse_ref, grad_ref, sorted_ref, ups_ref, nat_ref, delta_ref, dq_ref, dkv_ref
):
    row_len = qkv_ref.shape[1]
    width = heads * HEAD_DIM
    blocks = row_len // BLK
    per_device = up_ref.shape[2] // BLK
    for b in range(blocks):
        spot = slice(b * BLK, (b + 1) * BLK)
        sorted_ref[:, spot] = qkv_ref[: 3 * width, lane_tile(meta_ref[b] * BLK, BLK)]
        ups_ref[:, spot] = up_ref[meta_ref[b] // per_device, :, lane_tile((meta_ref[b] % per_device) * BLK, BLK)]
    delta_ref[...] = jnp.zeros_like(delta_ref)
    for h in range(heads):
        rows = slice(h * HEAD_DIM, (h + 1) * HEAD_DIM)
        for part in range(3):
            nat_ref[part * heads + h] = (
                sorted_ref[part * width + h * HEAD_DIM : part * width + (h + 1) * HEAD_DIM, :].astype(f32).T.astype(bf16)
            )
        upstream = ups_ref[rows, :].astype(f32)
        nat_ref[3 * heads + h] = upstream.T.astype(bf16)
        delta_ref[h : h + 1, :] = jnp.sum(upstream * att_ref[rows, :], axis=0, keepdims=True)
    dq_ref[...] = jnp.zeros_like(dq_ref)
    doc_tiles = meta_ref[blocks] // tile
    seen = seen_tile(tile)

    def one_key_tile(j, _):
        last = (j // doc_tiles + 1) * doc_tiles
        key_rows = pl.ds(pl.multiple_of(j * tile, tile), tile)

        def step(i, carry, diagonal):
            new = []
            at = lane_tile(i * tile, tile)
            query_rows = pl.ds(pl.multiple_of(i * tile, tile), tile)
            for h in range(heads):
                grad_keys, grad_values = carry[h]
                rows = slice(h * HEAD_DIM, (h + 1) * HEAD_DIM)
                scores, square, inverse = tile_scores(nat_ref[heads + h, key_rows, :], sorted_ref[rows, at])
                shares = jnp.exp(square * inverse - lse_ref[h : h + 1, at])
                if diagonal:
                    shares = jnp.where(seen, shares, 0.0)
                effect = jnp.dot(nat_ref[2 * heads + h, key_rows, :], ups_ref[rows, at], preferred_element_type=f32)
                sign = scores * inverse
                square_inverse = inverse * inverse
                grad = shares * (
                    effect * (1.0 - square_inverse + square_inverse * inverse) - delta_ref[h : h + 1, at] * sign
                )
                grad = grad.astype(bf16)
                mixing = (shares * sign).astype(bf16)
                grad_keys = grad_keys + jnp.dot(grad, nat_ref[h, query_rows, :], preferred_element_type=f32)
                grad_values = grad_values + jnp.dot(mixing, nat_ref[3 * heads + h, query_rows, :], preferred_element_type=f32)
                keys_t = sorted_ref[width + h * HEAD_DIM : width + (h + 1) * HEAD_DIM, lane_tile(j * tile, tile)]
                dq_ref[rows, at] += jnp.dot(keys_t, grad, preferred_element_type=f32)
                new.append((grad_keys, grad_values))
            return tuple(new)

        start = tuple((jnp.zeros((tile, HEAD_DIM), f32), jnp.zeros((tile, HEAD_DIM), f32)) for _ in range(heads))
        carry = step(j, start, True)
        carry = lax.fori_loop(j + 1, last, lambda i, c: step(i, c, False), carry)
        both = jnp.concatenate([c[0] for c in carry] + [c[1] for c in carry], axis=1).astype(bf16)
        dkv_ref[key_rows, :] = both
        return 0

    lax.fori_loop(0, row_len // tile, one_key_tile, 0)
    scale = HEAD_DIM**-0.5
    for b in range(blocks):
        spot = pl.ds(pl.multiple_of(meta_ref[b] * BLK, BLK), BLK)
        dq = (dq_ref[:, b * BLK : (b + 1) * BLK] * scale).T.astype(bf16)
        grad_ref[spot, :] = jnp.concatenate([dq, dkv_ref[b * BLK : (b + 1) * BLK, :]], axis=1)


def backward_attention(meta, qkv, upstream, att, lse, heads):
    row_len = qkv.shape[1]
    width = heads * HEAD_DIM
    tile = min(TILE, row_len)
    whole = pl.BlockSpec(memory_space=pltpu.VMEM)
    return pl.pallas_call(
        functools.partial(backward_kernel, heads, tile),
        out_shape=jax.ShapeDtypeStruct((row_len, 3 * width), bf16),
        in_specs=[pl.BlockSpec(memory_space=pltpu.SMEM)] + [whole] * 4,
        out_specs=whole,
        scratch_shapes=[
            pltpu.VMEM((3 * width, row_len), bf16),
            pltpu.VMEM((width, row_len), bf16),
            pltpu.VMEM((4 * heads, row_len, HEAD_DIM), bf16),
            pltpu.VMEM((8, row_len), f32),
            pltpu.VMEM((width, row_len), f32),
            pltpu.VMEM((row_len, 2 * width), bf16),
        ],
        compiler_params=pltpu.CompilerParams(vmem_limit_bytes=48 * 2**20),
        cost_estimate=pl.CostEstimate(
            flops=5 * row_len * row_len * width, bytes_accessed=20 * row_len * width, transcendentals=heads * row_len * row_len
        ),
    )(meta, qkv, upstream, att, lse)


def norm_parts(values):
    centered = values - jnp.mean(values, axis=-1, keepdims=True)
    inverse = lax.rsqrt(jnp.mean(centered * centered, axis=-1, keepdims=True) + epsilon)
    return centered * inverse, inverse


def norm_back(normed, inverse, gain, grad):
    c = grad * gain
    return (c - jnp.mean(c, axis=-1, keepdims=True) - normed * jnp.mean(c * normed, axis=-1, keepdims=True)) * inverse


def mm(a, b, dims):
    return lax.dot_general(a, b, ((dims[:1], dims[1:]), ((), ())), preferred_element_type=f32)


def body(
    tokens,
    lengths,
    block_place,
    qkv_weight,
    out_weight,
    up_weight,
    down_weight,
    attn_gain,
    mlp_gain,
    cotangent,
):
    nb, nk = lax.axis_size("pb"), lax.axis_size("ka")
    grid = Grid(nb, nk)
    nx, nc = grid.sizes["x"], grid.sizes["c"]
    x_at, c_at = grid.at["x"], grid.at["c"]
    tok_rows, model = tokens.shape
    shard = qkv_weight.shape[0]
    chips = nb * nx
    heads = -(-HEADS // nk)
    width = heads * HEAD_DIM
    lanes = -(-(3 * width + 2) // BLK) * BLK
    rels = [(xr, cr) for xr in range(nx) for cr in range(nc)]

    def ka_of(xr, cr):
        return ((x_at + xr) % nx) * nc + (c_at + cr) % nc

    def exchange(parts):
        got = [parts(grid.ka)]
        for xr, cr in rels[1:]:
            got.append(grid.fetch(parts(ka_of(-xr, -cr)), x=xr, c=cr))
        return got

    def head_groups(weight):
        split = weight.reshape(weight.shape[0], 3, HEADS, HEAD_DIM)
        if heads * nk != HEADS:
            split = jnp.pad(split, ((0, 0), (0, 0), (0, heads * nk - HEADS), (0, 0)))
        return jnp.transpose(split.reshape(-1, 3, nk, width), (2, 0, 1, 3)).reshape(nk, -1, 3 * width)

    gains = jnp.stack([attn_gain, mlp_gain], axis=1)
    gains = jnp.pad(gains, ((0, 0), (0, lanes - 3 * width - 2)))
    own_qkv = jnp.concatenate([head_groups(qkv_weight), jnp.broadcast_to(gains[None], (nk,) + gains.shape)], axis=2)
    got = exchange(lambda ka: lax.dynamic_index_in_dim(own_qkv, ka, 0, keepdims=False))
    group_qkv = jnp.stack(got).reshape(nx, nc, shard, lanes)
    group_qkv = grid.rolled(grid.rolled(group_qkv, 0, "x"), 1, "c").reshape(nk * shard, lanes)
    full_qkv = gather_rows(grid, group_qkv, ("lo", "hi"))

    by_x = [tokens] + [grid.fetch(tokens, x=r) for r in range(1, nx)]
    row_tokens = jnp.concatenate([p for t in by_x for p in ([t] + [grid.fetch(t, c=r) for r in range(1, nc)])], axis=0)
    row_len = row_tokens.shape[0]

    def core_part(weight):
        mine = lax.dynamic_index_in_dim(weight, c_at, 0, keepdims=False)
        got = [mine] + [
            grid.fetch(lax.dynamic_index_in_dim(weight, (c_at - r) % nc, 0, keepdims=False), c=r) for r in range(1, nc)
        ]
        return grid.rolled(jnp.stack(got), 0, "c").reshape(nc * weight.shape[1], weight.shape[2])

    strip = down_weight.shape[0]
    up_split = jnp.transpose(up_weight.reshape(shard, chips, nc, strip), (2, 0, 1, 3)).reshape(nc, shard, chips * strip)
    out_split = jnp.transpose(out_weight.reshape(shard, nc, model // nc), (1, 0, 2))
    up_out = core_part(jnp.concatenate([up_split, out_split], axis=2))
    full_down = gather_rows(grid, down_weight, ("hi", "x", "lo"))
    full_up_out = gather_rows(grid, up_out, ("hi", "lo", "x"))
    full_up = full_up_out[:, : chips * strip]
    out_own = full_up_out[:, chips * strip :]
    full_out = jnp.concatenate([out_own] + [grid.fetch(out_own, c=r) for r in range(1, nc)], axis=1)
    full_out = grid.rolled(full_out.reshape(model, nc, model // nc), 1, "c").reshape(model, model)
    cots = jnp.concatenate([cotangent] + [grid.fetch(cotangent, c=r) for r in range(1, nc)], axis=0)

    slots = tok_rows // BLK
    holder = jnp.argsort(block_place[0]).astype(jnp.int32)
    holder_ka, holder_slot = holder // slots, holder % slots
    rel = ((holder_ka // nc - x_at) % nx) * nc + (holder_ka % nc - c_at) % nc
    meta = jnp.concatenate([rel * slots + holder_slot, lengths[0, :1]]).astype(jnp.int32)

    gain_one = full_qkv[:, 3 * width].astype(f32)
    gain_two = full_qkv[:, 3 * width + 1].astype(f32)
    head_qkv = full_qkv[:, : 3 * width]
    inputs = tokens.astype(f32)
    normed_row, _ = norm_parts(row_tokens.astype(f32))
    h1 = (normed_row * gain_one).astype(bf16)
    scale = jnp.where(jnp.arange(3 * width) < width, HEAD_DIM**-0.5, 1.0).astype(f32)
    qkv = (mm(head_qkv, h1, (0, 1)) * scale[:, None]).astype(bf16)
    att_parts, att_row, lse = forward_attention(meta, qkv, heads, nk)

    def abs_heads(parts):
        both = jnp.stack(parts).reshape((nx, nc) + parts[0].shape)
        both = grid.rolled(grid.rolled(both, 0, "x"), 1, "c")
        return both.reshape((nk * parts[0].shape[0],) + parts[0].shape[1:])

    got = [att_parts[0]]
    for xr, cr in rels[1:]:
        got.append(grid.fetch(att_parts[((-xr) % nx) * nc + (-cr) % nc], x=xr, c=cr))
    att = abs_heads(got)[: HEADS * HEAD_DIM]

    residual = inputs + mm(att, full_out, (0, 0))
    normed_two, inverse_two = norm_parts(residual)
    h2 = (normed_two * gain_two).astype(bf16)
    h2s = jnp.concatenate([h2] + [grid.fetch(h2, c=r) for r in range(1, nc)], axis=0)

    def core_sum(part):
        pieces = part.reshape((nc, tok_rows) + part.shape[1:])
        total = pieces[0]
        for r in range(1, nc):
            total = total + grid.fetch(pieces[(nc - r) % nc].astype(bf16), c=r).astype(f32)
        return total

    hidden_pre = mm(h2s, full_up, (1, 0))
    hidden_act, gelu_back = jax.vjp(lambda v: jax.nn.gelu(v, approximate=True), hidden_pre)
    hidden_low = hidden_act.astype(bf16)
    (grad_pre,) = gelu_back(mm(cots, full_down, (1, 1)))
    grad_pre = grad_pre.astype(bf16)
    grad_h2 = core_sum(mm(grad_pre, full_up, (1, 1)))
    grad_down = mm(hidden_low, cots, (0, 0)).astype(bf16)
    grad_up = mm(h2s, grad_pre, (0, 0)).astype(bf16)
    mixed = (residual + core_sum(mm(hidden_low, full_down, (1, 0)))).astype(bf16)

    grad_residual = cotangent.astype(f32) + norm_back(normed_two, inverse_two, gain_two, grad_h2)
    grad_res_low = grad_residual.astype(bf16)
    grad_att = mm(full_out, grad_res_low, (1, 1)).astype(bf16)
    if heads * nk != HEADS:
        grad_att = jnp.pad(grad_att, ((0, (heads * nk - HEADS) * HEAD_DIM), (0, 0)))
    grad_att = grad_att.reshape(nk, width, tok_rows)
    upstream = jnp.stack(exchange(lambda ka: lax.dynamic_index_in_dim(grad_att, ka, 0, keepdims=False)))
    grad_out = mm(att, grad_res_low, (1, 0)).astype(bf16)

    grad_qkv_rows = backward_attention(meta, qkv, upstream, att_row, lse, heads)
    grad_qkv = mm(h1, grad_qkv_rows, (0, 0)).astype(bf16)
    grad_h1 = mm(grad_qkv_rows, head_qkv, (1, 1)).astype(bf16).reshape(nx, nc, tok_rows, model)

    half = grad_h1[:, 0].astype(f32)
    for r in range(1, nc):
        half = half + grid.fetch(grad_h1[:, (nc - r) % nc], c=r).astype(f32)
    half = half.astype(bf16)
    grad_normed_one = half[0].astype(f32)
    for r in range(1, nx):
        grad_normed_one = grad_normed_one + grid.fetch(half[(nx - r) % nx], x=r).astype(f32)
    normed_one, inverse_one = norm_parts(inputs)
    tokens_grad = (grad_residual + norm_back(normed_one, inverse_one, gain_one, grad_normed_one)).astype(bf16)

    def from_core_parts(part):
        pieces = part.reshape(nc, part.shape[0] // nc, part.shape[1])
        got = [lax.dynamic_index_in_dim(pieces, c_at, 0, keepdims=False)]
        for r in range(1, nc):
            got.append(grid.fetch(lax.dynamic_index_in_dim(pieces, (c_at - r) % nc, 0, keepdims=False), c=r))
        return grid.rolled(jnp.stack(got), 0, "c")

    sum_down = reduce_rows(grid, grad_down, ("lo", "x", "hi"))
    sum_up = from_core_parts(reduce_rows(grid, grad_up, ("x", "lo", "hi")))
    sum_up = jnp.transpose(sum_up.reshape(nc, shard, chips, strip), (1, 2, 0, 3)).reshape(shard, -1)
    core_out = grid.reduce(grad_out.reshape(model, nc, model // nc), 1, "c")
    sum_out = from_core_parts(reduce_rows(grid, core_out, ("x", "lo", "hi")))
    sum_out = jnp.transpose(sum_out, (1, 0, 2)).reshape(shard, model)
    group_grad = reduce_rows(grid, grad_qkv, ("lo", "hi")).reshape(nk, shard, 3 * width)
    got = exchange(lambda ka: lax.dynamic_index_in_dim(group_grad, ka, 0, keepdims=False))
    sum_qkv = jnp.stack(got).reshape(nx, nc, shard, 3, width)
    sum_qkv = grid.rolled(grid.rolled(sum_qkv, 0, "x"), 1, "c").reshape(nk, shard, 3, width)
    sum_qkv = jnp.transpose(sum_qkv, (1, 2, 0, 3)).reshape(shard, 3, nk * width)[:, :, : HEADS * HEAD_DIM]
    sum_qkv = sum_qkv.reshape(shard, 3 * HEADS * HEAD_DIM)

    grad_gain_one = jnp.sum(sum_qkv * qkv_weight.astype(f32), axis=1) / attn_gain.astype(f32)
    grad_gain_two = jnp.sum(sum_up * up_weight.astype(f32), axis=1) / mlp_gain.astype(f32)
    return (mixed, tokens_grad, sum_qkv, sum_out, sum_up, sum_down, grad_gain_one, grad_gain_two)


def solution(mesh):
    rows = P(("pb", "ka"), None)
    flat = P(("pb", "ka"))
    group = P("pb", None)
    return jax.shard_map(
        body,
        mesh=mesh,
        in_specs=(rows, group, group, rows, rows, rows, rows, flat, flat, rows),
        out_specs=(rows, rows, rows, rows, rows, rows, flat, flat),
        check_vma=False,
    )
```

```python
import functools
import math

import jax
import jax.numpy as jnp
from jax import lax
from jax.experimental import pallas as pl
from jax.experimental.pallas import tpu as pltpu
from jax.sharding import PartitionSpec as P

HEADS = 12
HEAD_DIM = 64
BLK = 128
SEQ_UNIT = 1024
epsilon = 1e-05
f32 = jnp.float32
bf16 = jnp.bfloat16


class Grid:
    def __init__(self, nb, nk):
        nhi = math.gcd(4, nb)
        nc = math.gcd(2, nk)
        self.sizes = {"hi": nhi, "lo": nb // nhi, "x": nk // nc, "c": nc}
        self.nb, self.nk = nb, nk
        pb, ka = lax.axis_index("pb"), lax.axis_index("ka")
        self.pb, self.ka = pb, ka
        self.at = {"hi": pb // self.sizes["lo"], "lo": pb % self.sizes["lo"], "x": ka // nc, "c": ka % nc}

    def fetch(self, value, flip=0, **steps):
        n = self.sizes
        pairs = []
        for hi in range(n["hi"]):
            for lo in range(n["lo"]):
                for x in range(n["x"]):
                    for c in range(n["c"]):
                        here = {"hi": hi, "lo": lo, "x": x, "c": c}
                        there = {d: here[d] ^ steps[d] if flip and d in steps else (here[d] + steps.get(d, 0)) % n[d] for d in here}
                        flat = [((p["hi"] * n["lo"] + p["lo"]) * n["x"] + p["x"]) * n["c"] + p["c"] for p in (there, here)]
                        pairs.append(tuple(flat))
        return lax.ppermute(value, ("pb", "ka"), pairs)

    def gather(self, value, dim):
        return jnp.stack([value] + [self.fetch(value, **{dim: r}) for r in range(1, self.sizes[dim])])

    def in_order(self, pieces, dim):
        n, me = self.sizes[dim], self.at[dim]
        if n == 1:
            return pieces
        if n == 2:
            return [jnp.where(me == 0, pieces[0], pieces[1]), jnp.where(me == 0, pieces[1], pieces[0])]
        stacked = jnp.stack(pieces)
        return [lax.dynamic_index_in_dim(stacked, (i - me) % n, 0, keepdims=False) for i in range(n)]

    def group_in_order(self, pieces):
        nx, nc = self.sizes["x"], self.sizes["c"]
        by_x = [self.in_order(pieces[i * nc : (i + 1) * nc], "c") for i in range(nx)]
        by_c = [self.in_order([row[c] for row in by_x], "x") for c in range(nc)]
        return [by_c[c][x] for x in range(nx) for c in range(nc)]

    def split(self, parts, axis, dim):
        n, me = self.sizes[dim], self.at[dim]
        own = lax.dynamic_index_in_dim(parts, me, axis, keepdims=False)
        return own, [lax.dynamic_index_in_dim(parts, (me - r) % n, axis, keepdims=False) for r in range(1, n)]

    def halve(self, parts, dim, bit):
        mine = (self.at[dim] >> bit) % 2
        parts = parts.reshape((2, -1) + parts.shape[1:])
        kept = lax.dynamic_index_in_dim(parts, mine, 0, keepdims=False)
        return kept, lax.dynamic_index_in_dim(parts, 1 - mine, 0, keepdims=False)

    def swap(self, value, dim, bit):
        return self.fetch(value, 1, **{dim: 1 << bit})

    def send(self, sends, dim):
        return [self.fetch(sent, **{dim: r + 1}) for r, sent in enumerate(sends)]


def added(own, received, last=False):
    total = own.astype(f32)
    for one in received:
        total = total + one.astype(f32)
    return total if last else total.astype(own.dtype)


def together(*values):
    return lax.optimization_barrier(values)


def place_kernel(counts, rows, offs_ref, *refs):
    ins, out_ref, sems = refs[: len(counts)], refs[len(counts)], refs[len(counts) + 1]
    copies = []
    for ref, count in zip(ins, counts):
        for i in range(count):
            at = pl.multiple_of(offs_ref[len(copies)], rows)
            copies.append(pltpu.make_async_copy(ref.at[i], out_ref.at[pl.ds(at, rows), :], sems.at[len(copies)]))
    for copy in copies:
        copy.start()
    for copy in copies:
        copy.wait()


def place(stacks, offsets):
    rows, cols = stacks[0].shape[1:]
    counts = [s.shape[0] for s in stacks]
    total = sum(counts)
    return pl.pallas_call(
        functools.partial(place_kernel, counts, rows),
        out_shape=jax.ShapeDtypeStruct((total * rows, cols), stacks[0].dtype),
        in_specs=[pl.BlockSpec(memory_space=pltpu.SMEM)] + [pl.BlockSpec(memory_space=pl.ANY)] * len(stacks),
        out_specs=pl.BlockSpec(memory_space=pltpu.VMEM),
        scratch_shapes=[pltpu.SemaphoreType.DMA((total,))],
        compiler_params=pltpu.CompilerParams(vmem_limit_bytes=16 * 2**20),
        cost_estimate=pl.CostEstimate(flops=10**6, bytes_accessed=10**5, transcendentals=0),
    )(offsets.astype(jnp.int32), *stacks)


def tie(value, *before):
    return lax.optimization_barrier((value,) + before)[0]


def gather_rows(grid, piece, order, gates=None, begun=None, done=("hi",)):
    if begun is None:
        stack, steps = piece[None], [dict()]
    else:
        stack, steps = begun, [dict()]
        for dim in done:
            steps = steps + [{**s, dim: r} for r in range(1, grid.sizes[dim]) for s in steps]
        piece = stack[0]
    stacks = []
    received = {}
    for dim in order:
        if gates and dim in gates:
            stack = tie(stack, *gates[dim])
        got = [grid.fetch(stack, **{dim: r}) for r in range(1, grid.sizes[dim])]
        received[dim] = got
        steps = steps + [{**s, dim: r} for r in range(1, grid.sizes[dim]) for s in steps]
        if dim == order[-1]:
            stacks = [stack] + got
        else:
            stack = jnp.concatenate([stack] + got, axis=0)
    dims = [d for d in ("hi", "lo", "x") if d in order or (begun is not None and d in done)]
    rows = piece.shape[0]
    index = []
    for s in steps:
        at = 0
        for d in dims:
            at = at * grid.sizes[d] + (grid.at[d] + s.get(d, 0)) % grid.sizes[d]
        index.append(at)
    index = jnp.stack(index)
    if gates and "place" in gates:
        stacks, _ = together(stacks, gates["place"])
    if rows % 16 == 0:
        return place(stacks, index * rows), received
    order_back = jnp.argsort(index)
    out = jnp.concatenate(stacks, axis=0)
    out = jnp.concatenate([lax.dynamic_index_in_dim(out, order_back[i], 0, keepdims=False) for i in range(len(steps))], axis=0)
    return out, received


def lane_tile(at, size):
    return pl.ds(pl.multiple_of(at, BLK), size)


def head_rows(sets, kind, head):
    at = 0
    for one in sets:
        if head in one:
            return slice(at + (kind * len(one) + one.index(head)) * HEAD_DIM, at + (kind * len(one) + one.index(head) + 1) * HEAD_DIM)
        at += 3 * len(one) * HEAD_DIM


def pipeline(work, first, second, third):
    held = {}
    for t in range(len(work) + 2):
        if t < len(work):
            held[t] = first(work[t])
        if 1 <= t <= len(work):
            held[t - 1] = second(work[t - 1], held[t - 1])
        if t >= 2:
            third(work[t - 2], held.pop(t - 2))


def spans_to(begin, end, chunk):
    spans = []
    while begin < end:
        size = min(chunk, end - begin)
        spans.append((begin, size, begin + size == end))
        begin += size
    return spans


def forward_kernel(sets, tile, chunk, unit, meta_ref, qkv_ref, out_ref, att_ref, lse_ref, sorted_ref, keys_ref):
    heads = sum(len(one) for one in sets)
    row_len = qkv_ref.shape[1]
    blocks = row_len // BLK
    per_device = out_ref.shape[2] // BLK
    for b in range(blocks):
        sorted_ref[:, b * BLK : (b + 1) * BLK] = qkv_ref[:, lane_tile(meta_ref[b] * BLK, BLK)]
    for h in range(heads):
        keys_ref[h] = sorted_ref[head_rows(sets, 1, h), :].astype(f32).T.astype(bf16)
    doc_units = meta_ref[blocks] // unit
    seen = lax.broadcasted_iota(jnp.int32, (tile, tile), 0) <= lax.broadcasted_iota(jnp.int32, (tile, tile), 1)
    lse_ref[...] = jnp.zeros_like(lse_ref)
    for i in range(row_len // tile):
        lanes = slice(i * tile, (i + 1) * tile)
        queries = [sorted_ref[head_rows(sets, 0, h), lanes] for h in range(heads)]

        def run(spans, carry):
            carry = list(carry)

            def first(item):
                h, begin, size, _ = item
                return jnp.dot(keys_ref[h, pl.ds(begin, size), :], queries[h], preferred_element_type=f32)

            def second(item, scores):
                h, _, size, diagonal = item
                peak, total, acc = carry[h]
                square = scores * scores + 1.0
                inverse = lax.rsqrt(square)
                reach = square * inverse
                if diagonal:
                    low = jnp.where(seen, reach[size - tile :], -1e30)
                    reach = low if size == tile else jnp.concatenate([reach[: size - tile], low], axis=0)
                top = jnp.maximum(peak, jnp.max(reach, axis=0, keepdims=True))
                shares = jnp.exp(reach - top)
                fade = jnp.exp(peak - top)
                total = total * fade + jnp.sum(shares, axis=0, keepdims=True)
                carry[h] = (top, total, acc)
                return (shares * (scores * inverse)).astype(bf16), fade

            def third(item, kept):
                h, begin, size, _ = item
                mixing, fade = kept
                top, total, acc = carry[h]
                values = sorted_ref[head_rows(sets, 2, h), pl.ds(begin, size)]
                carry[h] = (top, total, acc * fade + jnp.dot(values, mixing, preferred_element_type=f32))

            pipeline([(h,) + span for span in spans for h in range(heads)], first, second, third)
            return tuple(carry)

        here = i * tile // unit
        start = (jnp.ones((1, tile), f32), jnp.zeros((1, tile), f32), jnp.zeros((HEAD_DIM, tile), f32))
        carry = run(spans_to(here * unit, (i + 1) * tile, chunk), (start,) * heads)
        if here > 0:

            def earlier(k, carry):
                base = pl.multiple_of(k * unit, unit)
                return run([(base + o, chunk, False) for o in range(0, unit, chunk)], carry)

            carry = lax.fori_loop(here // doc_units * doc_units, here, earlier, carry)
        for h in range(heads):
            peak, total, acc = carry[h]
            rows = slice(h * HEAD_DIM, (h + 1) * HEAD_DIM)
            result = acc / total
            att_ref[rows, lanes] = result
            lse_ref[h : h + 1, lanes] = peak + jnp.log(total)
            low = result.astype(bf16)
            for part in range(tile // BLK):
                spot = meta_ref[i * (tile // BLK) + part]
                out_ref[spot // per_device, rows, lane_tile((spot % per_device) * BLK, BLK)] = low[:, part * BLK : (part + 1) * BLK]


def forward_attention(meta, qkv, sets, devices):
    row_len = qkv.shape[1]
    heads = sum(len(one) for one in sets)
    width = heads * HEAD_DIM
    whole = pl.BlockSpec(memory_space=pltpu.VMEM)
    return pl.pallas_call(
        functools.partial(forward_kernel, sets, 256, 512, SEQ_UNIT),
        out_shape=(
            jax.ShapeDtypeStruct((devices, width, row_len // devices), bf16),
            jax.ShapeDtypeStruct((width, row_len), f32),
            jax.ShapeDtypeStruct((8, row_len), f32),
        ),
        in_specs=[pl.BlockSpec(memory_space=pltpu.SMEM), whole],
        out_specs=(whole, whole, whole),
        scratch_shapes=[pltpu.VMEM((3 * width, row_len), bf16), pltpu.VMEM((heads, row_len, HEAD_DIM), bf16)],
        compiler_params=pltpu.CompilerParams(vmem_limit_bytes=40 * 2**20),
        cost_estimate=pl.CostEstimate(
            flops=10**6, bytes_accessed=10**5, transcendentals=0),
    )(meta, qkv)


def backward_kernel(
    sets, which, tile, chunk, unit, meta_ref, qkv_ref, up_ref, att_ref, lse_ref, grad_ref, sorted_ref, ups_ref, nat_ref, stat_ref, dq_ref, dkv_ref
):
    heads = sets[which]
    count = len(heads)
    row_len = qkv_ref.shape[1]
    width = count * HEAD_DIM
    blocks = row_len // BLK
    per_device = up_ref.shape[2] // BLK
    base_row = head_rows(sets, 0, heads[0]).start
    ups_rows = slice(heads[0] * HEAD_DIM, (heads[-1] + 1) * HEAD_DIM)
    for b in range(blocks):
        spot = slice(b * BLK, (b + 1) * BLK)
        sorted_ref[:, spot] = qkv_ref[base_row : base_row + 3 * width, lane_tile(meta_ref[b] * BLK, BLK)]
        ups_ref[:, spot] = up_ref[meta_ref[b] // per_device, ups_rows, lane_tile((meta_ref[b] % per_device) * BLK, BLK)]
    own = [slice(h * HEAD_DIM, (h + 1) * HEAD_DIM) for h in range(3 * count)]
    for h in range(count):
        for part in range(2):
            nat_ref[part * count + h] = sorted_ref[own[part * count + h], :].astype(f32).T.astype(bf16)
        upstream = ups_ref[own[h], :].astype(f32)
        nat_ref[2 * count + h] = upstream.T.astype(bf16)
        att = att_ref[heads[h] * HEAD_DIM : (heads[h] + 1) * HEAD_DIM, :]
        delta = jnp.sum(upstream * att, axis=0, keepdims=True)
        stats = [lse_ref[heads[h] : heads[h] + 1, :], delta, jnp.zeros((6, row_len), f32)]
        stat_ref[h] = jnp.concatenate(stats, axis=0).T
    dkv_ref[...] = jnp.zeros_like(dkv_ref)
    doc_units = meta_ref[blocks] // unit
    seen = lax.broadcasted_iota(jnp.int32, (tile, tile), 0) >= lax.broadcasted_iota(jnp.int32, (tile, tile), 1)
    for i in range(row_len // tile):
        at = slice(i * tile, (i + 1) * tile)

        def run(spans, carry):
            carry = list(carry)

            def first(item):
                h, begin, size, _ = item
                lanes = pl.ds(begin, size)
                scores = jnp.dot(nat_ref[h, at, :], sorted_ref[own[count + h], lanes], preferred_element_type=f32)
                effect = jnp.dot(nat_ref[2 * count + h, at, :], sorted_ref[own[2 * count + h], lanes], preferred_element_type=f32)
                return scores, effect

            def second(item, kept):
                h, _, size, diagonal = item
                scores, effect = kept
                square = scores * scores + 1.0
                inverse = lax.rsqrt(square)
                shares = jnp.exp(square * inverse - stat_ref[h, at, 0:1])
                if diagonal:
                    low = jnp.where(seen, shares[:, size - tile :], 0.0)
                    shares = low if size == tile else jnp.concatenate([shares[:, : size - tile], low], axis=1)
                sign = scores * inverse
                twice = inverse * inverse
                grad = shares * (effect * (1.0 - twice + twice * inverse) - stat_ref[h, at, 1:2] * sign)
                return grad.astype(bf16), (shares * sign).astype(bf16)

            def third(item, kept):
                h, begin, size, _ = item
                grad, mixing = kept
                lanes = pl.ds(begin, size)
                carry[h] = carry[h] + jnp.dot(grad, nat_ref[count + h, pl.ds(begin, size), :], preferred_element_type=f32)
                dkv_ref[own[h], lanes] += jnp.dot(sorted_ref[own[h], at], grad, preferred_element_type=f32)
                dkv_ref[own[count + h], lanes] += jnp.dot(ups_ref[own[h], at], mixing, preferred_element_type=f32)

            pipeline([(h,) + span for span in spans for h in range(count)], first, second, third)
            return tuple(carry)

        here = i * tile // unit
        carry = run(spans_to(here * unit, (i + 1) * tile, chunk), (jnp.zeros((tile, HEAD_DIM), f32),) * count)
        if here > 0:

            def earlier(k, carry):
                base = pl.multiple_of(k * unit, unit)
                return run([(base + o, chunk, False) for o in range(0, unit, chunk)], carry)

            carry = lax.fori_loop(here // doc_units * doc_units, here, earlier, carry)
        dq_ref[at, :] = carry[0] if count == 1 else jnp.concatenate(carry, axis=1)
    scale = HEAD_DIM**-0.5
    for b in range(blocks):
        here = slice(b * BLK, (b + 1) * BLK)
        both = jnp.concatenate([dq_ref[here, :] * scale, dkv_ref[:, here].T], axis=1)
        grad_ref[pl.ds(pl.multiple_of(meta_ref[b] * BLK, BLK), BLK), :] = both.astype(bf16)


def backward_attention(meta, qkv, upstream, att, lse, sets, which):
    row_len = qkv.shape[1]
    count = len(sets[which])
    width = count * HEAD_DIM
    whole = pl.BlockSpec(memory_space=pltpu.VMEM)
    return pl.pallas_call(
        functools.partial(backward_kernel, sets, which, 256, 256, SEQ_UNIT),
        out_shape=jax.ShapeDtypeStruct((row_len, 3 * width), bf16),
        in_specs=[pl.BlockSpec(memory_space=pltpu.SMEM)] + [whole] * 4,
        out_specs=whole,
        scratch_shapes=[
            pltpu.VMEM((3 * width, row_len), bf16),
            pltpu.VMEM((width, row_len), bf16),
            pltpu.VMEM((3 * count, row_len, HEAD_DIM), bf16),
            pltpu.VMEM((count, row_len, 8), f32),
            pltpu.VMEM((row_len, width), f32),
            pltpu.VMEM((2 * width, row_len), f32),
        ],
        compiler_params=pltpu.CompilerParams(vmem_limit_bytes=48 * 2**20),
        cost_estimate=pl.CostEstimate(
            flops=10**6, bytes_accessed=10**5, transcendentals=0),
    )(meta, qkv, upstream, att, lse)


def project_kernel(sets, gain_lane, count, *refs):
    weight_ref, h1_ref, qkv_ref, turned_ref, gain_ref = refs[count:]
    columns = qkv_ref.shape[0]

    @pl.when(pl.program_id(0) == 0)
    def _():
        turned = weight_ref[...].astype(f32).T
        gain_ref[...] = turned[gain_lane : gain_lane + 8]
        turned = turned[:columns]
        for one in sets:
            begin = head_rows(sets, 0, one[0]).start
            end = begin + len(one) * HEAD_DIM
            stop = begin + 3 * len(one) * HEAD_DIM
            turned_ref[begin:end] = (turned[begin:end] * HEAD_DIM**-0.5).astype(bf16)
            turned_ref[end:stop] = turned[end:stop].astype(bf16)

    for i in range(count):

        @pl.when(pl.program_id(0) == i)
        def _(tokens_ref=refs[i]):
            values = tokens_ref[...].astype(f32)
            centered = values - jnp.mean(values, axis=-1, keepdims=True)
            inverse = lax.rsqrt(jnp.mean(centered * centered, axis=-1, keepdims=True) + epsilon)
            h1 = (centered * inverse * gain_ref[0:1]).T.astype(bf16)
            h1_ref[...] = h1
            qkv_ref[...] = jnp.dot(turned_ref[...], h1, preferred_element_type=f32).astype(bf16)


def project(pieces, weight, sets):
    step, model = pieces[0].shape
    count = len(pieces)
    row_len = count * step
    columns = 3 * HEAD_DIM * sum(len(one) for one in sets)
    return pl.pallas_call(
        functools.partial(project_kernel, sets, columns, count),
        grid=(count,),
        out_shape=(jax.ShapeDtypeStruct((model, row_len), bf16), jax.ShapeDtypeStruct((columns, row_len), bf16)),
        in_specs=[pl.BlockSpec((step, model), lambda i: (0, 0))] * count + [pl.BlockSpec(weight.shape, lambda i: (0, 0))],
        out_specs=(pl.BlockSpec((model, step), lambda i: (0, i)), pl.BlockSpec((columns, step), lambda i: (0, i))),
        scratch_shapes=[pltpu.VMEM((columns, model), bf16), pltpu.VMEM((8, model), f32)],
        compiler_params=pltpu.CompilerParams(vmem_limit_bytes=40 * 2**20),
        cost_estimate=pl.CostEstimate(flops=10**6, bytes_accessed=10**5, transcendentals=0),
    )(*pieces, weight)


def rows_kernel(count, strides, me_ref, left_ref, right_ref, *refs):
    outs, total_ref = refs[:-1], refs[-1]
    total_ref[...] = jnp.dot(left_ref[...], right_ref[...], preferred_element_type=f32)
    outer, inner = strides
    rows = outs[0].shape[-2]
    for r in range(count):
        entry = (me_ref[0] + count - r) % count
        for a in range(outer):
            for b in range(inner):
                at = pl.multiple_of(((a * count + entry) * inner + b) * rows, 8)
                outs[r][a, b] = total_ref[pl.ds(at, rows), :].astype(bf16)


def split_product(grid, left, right, dim, with_x=False):
    rows_all, cols = left.shape[0], right.shape[1]
    outer = grid.sizes["hi"] if dim == "lo" else grid.nb
    inner = grid.sizes["x"] if dim == "lo" and with_x else 1
    count = grid.sizes[dim]
    rows = rows_all // (outer * inner * count)
    whole = pl.BlockSpec(memory_space=pltpu.VMEM)
    outs = pl.pallas_call(
        functools.partial(rows_kernel, count, (outer, inner)),
        out_shape=tuple(jax.ShapeDtypeStruct((outer, inner, rows, cols), bf16) for _ in range(count)),
        in_specs=[pl.BlockSpec(memory_space=pltpu.SMEM), whole, whole],
        out_specs=(whole,) * count,
        scratch_shapes=[pltpu.VMEM((rows_all, cols), f32)],
        compiler_params=pltpu.CompilerParams(vmem_limit_bytes=48 * 2**20),
        cost_estimate=pl.CostEstimate(flops=10**6, bytes_accessed=10**5, transcendentals=0),
    )(grid.at[dim].reshape(1).astype(jnp.int32), left, right)
    if inner == 1:
        outs = [one.reshape(outer, rows, cols) for one in outs]
    return outs[0], list(outs[1:])


def back_kernel(bounds, count, *refs):
    parts, weight_ref, outs = refs[:count], refs[count], refs[count + 1 :]
    pieces, rows = outs[0].shape[0], outs[0].shape[1]
    for x in range(pieces):
        for c, out_ref in enumerate(outs):
            here = slice((x * len(outs) + c) * rows, (x * len(outs) + c + 1) * rows)
            total = 0.0
            for i in range(count):
                weight = weight_ref[:, bounds[i] : bounds[i + 1]]
                total = total + lax.dot_general(parts[i][here, :], weight, (((1,), (1,)), ((), ())), preferred_element_type=f32)
            out_ref[x] = total.astype(bf16)


def back_project(grid, parts, weight, bounds):
    nx, nc = grid.sizes["x"], grid.sizes["c"]
    rows = parts[0].shape[0] // (nx * nc)
    whole = pl.BlockSpec(memory_space=pltpu.VMEM)
    return pl.pallas_call(
        functools.partial(back_kernel, bounds, len(parts)),
        out_shape=tuple(jax.ShapeDtypeStruct((nx, rows, weight.shape[0]), bf16) for _ in range(nc)),
        in_specs=[whole] * (len(parts) + 1),
        out_specs=(whole,) * nc,
        compiler_params=pltpu.CompilerParams(vmem_limit_bytes=48 * 2**20),
        cost_estimate=pl.CostEstimate(flops=10**6, bytes_accessed=10**5, transcendentals=0),
    )(*parts, weight)


def norm_parts(values):
    centered = values - jnp.mean(values, axis=-1, keepdims=True)
    inverse = lax.rsqrt(jnp.mean(centered * centered, axis=-1, keepdims=True) + epsilon)
    return centered * inverse, inverse


def norm_back(normed, inverse, gain, grad):
    c = grad * gain
    return (c - jnp.mean(c, axis=-1, keepdims=True) - normed * jnp.mean(c * normed, axis=-1, keepdims=True)) * inverse


def mm(a, b, dims):
    return lax.dot_general(a, b, ((dims[:1], dims[1:]), ((), ())), preferred_element_type=f32)


def body(
    tokens,
    lengths,
    block_place,
    qkv_weight,
    out_weight,
    up_weight,
    down_weight,
    attn_gain,
    mlp_gain,
    cotangent,
):
    nb, nk = lax.axis_size("pb"), lax.axis_size("ka")
    grid = Grid(nb, nk)
    nx, nc = grid.sizes["x"], grid.sizes["c"]
    x_at, c_at = grid.at["x"], grid.at["c"]
    tok_rows, model = tokens.shape
    shard = qkv_weight.shape[0]
    chips = nb * nx
    heads = -(-HEADS // nk)
    width = heads * HEAD_DIM
    lanes = -(-(3 * width + 2) // BLK) * BLK
    rels = [(xr, cr) for xr in range(nx) for cr in range(nc)]

    def ka_of(xr, cr):
        return ((x_at + xr) % nx) * nc + (c_at + cr) % nc

    def exchange(parts):
        got = [parts(grid.ka)]
        for xr, cr in rels[1:]:
            got.append(grid.fetch(parts(ka_of(-xr, -cr)), x=xr, c=cr))
        return got

    cut = max(1, heads - 1)
    sets = [tuple(range(cut)), tuple(range(cut, heads))] if heads > 1 else [(0,)]
    bounds = [0]
    for one in sets:
        bounds.append(bounds[-1] + 3 * len(one) * HEAD_DIM)

    def head_groups(weight):
        split = weight.reshape(weight.shape[0], 3, HEADS, HEAD_DIM)
        if heads * nk != HEADS:
            split = jnp.pad(split, ((0, 0), (0, 0), (0, heads * nk - HEADS), (0, 0)))
        split = split.reshape(-1, 3, nk, heads, HEAD_DIM)
        chosen = [split[:, :, :, one[0] : one[-1] + 1].transpose(2, 0, 1, 3, 4).reshape(nk, weight.shape[0], -1) for one in sets]
        return jnp.concatenate(chosen, axis=2)

    gains = jnp.stack([attn_gain, mlp_gain], axis=1)
    gains = jnp.pad(gains, ((0, 0), (0, lanes - 3 * width - 2)))
    own_qkv = jnp.concatenate([head_groups(qkv_weight), jnp.broadcast_to(gains[None], (nk,) + gains.shape)], axis=2)
    got = exchange(lambda ka: lax.dynamic_index_in_dim(own_qkv, ka, 0, keepdims=False))
    group_qkv = jnp.concatenate(grid.group_in_order(got), axis=0)

    first_tokens = tie(tokens, *got)
    by_x = [tokens] + [grid.fetch(first_tokens, x=r) for r in range(1, nx)]
    got_hi = [grid.fetch(group_qkv[None], hi=r) for r in range(1, grid.sizes["hi"])]
    stack = tie(jnp.stack(by_x), *got_hi)
    by_c = [by_x] + [list(grid.fetch(stack, c=r)) for r in range(1, nc)]
    row_tokens = [by_c[c][x] for x in range(nx) for c in range(nc)]
    full_qkv, _ = gather_rows(grid, None, ("lo",), {"place": row_tokens}, jnp.concatenate([group_qkv[None]] + got_hi, axis=0))

    full_out = lax.all_gather(tie(out_weight, *got_hi), ("pb", "ka"), axis=0, tiled=True)

    strip = down_weight.shape[0]
    up_split = jnp.transpose(up_weight.reshape(shard, chips, nc, strip), (2, 0, 1, 3)).reshape(nc, shard, chips * strip)
    own, sends = grid.split(up_split, 0, "c")
    up_part = jnp.concatenate(grid.in_order([own] + grid.send(sends, "c"), "c"), axis=0)
    folds = chips * strip // model
    up_part = jnp.concatenate([up_part[:, i * model : (i + 1) * model] for i in range(folds)], axis=0)
    both = tie(jnp.concatenate([up_part, down_weight], axis=0), *got_hi, *by_x)
    both = grid.gather(both, "hi")

    slots = tok_rows // BLK
    holder = jnp.argsort(block_place[0]).astype(jnp.int32)
    holder_ka, holder_slot = holder // slots, holder % slots
    rel = ((holder_ka // nc - x_at) % nx) * nc + (holder_ka % nc - c_at) % nc
    meta = jnp.concatenate([rel * slots + holder_slot, lengths[0, :1]]).astype(jnp.int32)

    gain_one = full_qkv[:, 3 * width].astype(f32)
    gain_two = full_qkv[:, 3 * width + 1].astype(f32)
    inputs = tokens.astype(f32)
    h1, qkv = project(row_tokens, full_qkv, sets)
    row_len = h1.shape[1]
    both = tie(both, qkv)
    up_rows = up_part.shape[0]
    up_stack, down_stack = both[:, :up_rows], both[:, up_rows:]
    up_stack = jnp.concatenate([up_stack] + [grid.fetch(up_stack, lo=r) for r in range(1, grid.sizes["lo"])], axis=0)
    down_stack = jnp.concatenate([down_stack] + [grid.fetch(down_stack, x=r) for r in range(1, nx)], axis=0)
    att_parts, att_row, lse = forward_attention(meta, tie(qkv, both), sets, nk)
    att_parts, up_stack, down_stack = together(att_parts, up_stack, down_stack)
    full_up, _ = gather_rows(grid, None, ("x",), begun=up_stack, done=("hi", "lo"))
    full_up = jnp.transpose(full_up.reshape(chips, folds, nc * shard, model), (0, 2, 1, 3)).reshape(model, folds * model)
    full_down, _ = gather_rows(grid, None, ("lo",), begun=down_stack, done=("hi", "x"))

    got = [att_parts[0]]
    for xr, cr in rels[1:]:
        got.append(grid.fetch(att_parts[((-xr) % nx) * nc + (-cr) % nc], x=xr, c=cr))
    att = jnp.concatenate(grid.group_in_order(got), axis=0)[: HEADS * HEAD_DIM]

    late_cot = tie(cotangent, att_parts)
    cots = jnp.concatenate([cotangent] + [grid.fetch(late_cot, c=r) for r in range(1, nc)], axis=0)
    residual = inputs + mm(att, full_out, (0, 0))
    normed_two, inverse_two = norm_parts(residual)
    h2 = (normed_two * gain_two).astype(bf16)
    h2s = jnp.concatenate([h2] + [grid.fetch(h2, c=r) for r in range(1, nc)], axis=0)

    def core_sum(part):
        pieces = part.reshape((nc, tok_rows) + part.shape[1:])
        total = pieces[0]
        for r in range(1, nc):
            total = total + grid.fetch(pieces[(nc - r) % nc].astype(bf16), c=r).astype(f32)
        return total

    hidden_pre = mm(h2s, full_up, (1, 0))
    hidden_act, gelu_back = jax.vjp(lambda v: jax.nn.gelu(v, approximate=True), hidden_pre)
    hidden_low = hidden_act.astype(bf16)
    (grad_pre,) = gelu_back(mm(cots, full_down, (1, 1)))
    grad_pre = grad_pre.astype(bf16)
    grad_h2 = core_sum(mm(grad_pre, full_up, (1, 1)))
    grad_up = mm(h2s, grad_pre, (0, 0)).astype(bf16)
    grad_residual = cotangent.astype(f32) + norm_back(normed_two, inverse_two, gain_two, grad_h2)
    grad_res_low = grad_residual.astype(bf16)
    grad_att = mm(full_out, grad_res_low, (1, 1)).astype(bf16)
    if heads * nk != HEADS:
        grad_att = jnp.pad(grad_att, ((0, (heads * nk - HEADS) * HEAD_DIM), (0, 0)))
    grad_att = grad_att.reshape(nk, width, tok_rows)
    upstream = jnp.stack(exchange(lambda ka: lax.dynamic_index_in_dim(grad_att, ka, 0, keepdims=False)))
    grad_down = mm(hidden_low, cots, (0, 0)).astype(bf16)
    grad_out = mm(att, grad_res_low, (1, 0)).astype(bf16)
    mixed = (residual + core_sum(mm(hidden_low, full_down, (1, 0)))).astype(bf16)

    n = grid.sizes

    def placed(grad):
        return grad.reshape(n["hi"], n["lo"], n["x"], -1, grad.shape[1])

    up_own, up_send = grid.split(placed(grad_up), 1, "lo")
    up_got = grid.send(up_send, "lo")
    sum_out = lax.psum_scatter(grad_out, ("pb", "ka"), scatter_dimension=0, tiled=True)
    down_own, down_send = grid.split(placed(grad_down), 2, "x")
    down_send, _ = together(down_send, upstream)
    down_got = grid.send(down_send, "x")

    parts, qkv_rest, qkv_got = [], [], []
    last = len(sets) - 1
    for which in range(len(sets)):
        part = backward_attention(meta, qkv, upstream, att_row, lse, sets, which)
        if which == last:
            part, down_got, qkv_got = together(part, down_got, qkv_got)
        parts.append(part)
        own, sends = split_product(grid, h1, part, "lo")
        qkv_rest.append(own)
        if which < last:
            qkv_got.append(grid.send(sends, "lo"))
        if which == 0:
            up_own, up_send = grid.split(added(up_own, up_got), 0, "hi")
            up_got = grid.send(up_send, "hi")
            upstream, *_ = together(upstream, *sends, *up_send)

    qkv_got.append(grid.send(sends, "lo"))
    down_own, down_send = grid.split(added(down_own, down_got), 1, "lo")
    down_send, _ = together(down_send, sends)
    down_got = grid.send(down_send, "lo")
    grad_h1 = back_project(grid, parts, full_qkv, bounds)
    h1_send = [grad_h1[(nc - r) % nc] for r in range(1, nc)]

    sums = [added(own, got) for own, got in zip(qkv_rest, qkv_got)]
    by_kind = []
    for kind in range(3):
        for i, one in enumerate(sets):
            begin = kind * len(one) * HEAD_DIM
            by_kind.append(sums[i][:, :, begin : begin + len(one) * HEAD_DIM])
    qkv_own, qkv_send = grid.split(jnp.concatenate(by_kind, axis=2), 0, "hi")
    up_got, qkv_send, h1_send = together(up_got, qkv_send, h1_send)
    up_own, up_send = grid.split(added(up_own, up_got), 0, "x")
    qkv_got = grid.send(qkv_send, "hi")
    h1_got = grid.send(h1_send, "c")
    up_got = grid.send(up_send, "x")
    h1_own = added(grad_h1[0], h1_got)
    h1_send = [h1_own[(nx - r) % nx] for r in range(1, nx)]
    up_own, up_send = grid.split(added(up_own, up_got, True).reshape(nc, shard, -1), 0, "c")
    h1_send, up_send = together(h1_send, up_send)
    h1_got = grid.send(h1_send, "x")
    up_got = grid.send(up_send, "c")

    down_own, down_send = grid.split(added(down_own, down_got), 0, "hi")
    group_grad = added(qkv_own, qkv_got, True).reshape(nx, nc, shard, 3 * width)
    group_grad, down_send, up_got = together(group_grad, down_send, up_got)
    group_own, group_send = grid.split(group_grad, 0, "x")
    by_x = grid.in_order([group_own] + grid.send(group_send, "x"), "x")
    down_got = grid.send(down_send, "hi")
    group_own, group_send = grid.split(jnp.stack(by_x), 1, "c")
    by_c = grid.in_order([group_own] + grid.send(group_send, "c"), "c")
    got = [by_c[c][x] for x in range(nx) for c in range(nc)]
    sum_up = grid.in_order([up_own] + up_got, "c")

    kept = min(nk * width, HEADS * HEAD_DIM)
    sum_qkv = []
    for kind in range(3):
        for i, one in enumerate(got):
            size = min(width, kept - i * width)
            if size > 0:
                sum_qkv.append(one[:, kind * width : kind * width + size])
    sum_qkv = jnp.concatenate(sum_qkv, axis=1)
    sum_up = jnp.stack([one.reshape(shard, chips, strip) for one in sum_up], axis=2).reshape(shard, -1)
    sum_down = added(down_own, down_got, True)
    normed_one, inverse_one = norm_parts(inputs)
    tokens_grad = added(h1_own[0], h1_got, True)
    tokens_grad = (grad_residual + norm_back(normed_one, inverse_one, gain_one, tokens_grad)).astype(bf16)

    grad_gain_one = jnp.sum(sum_qkv * qkv_weight.astype(f32), axis=1) / attn_gain.astype(f32)
    grad_gain_two = jnp.sum(sum_up * up_weight.astype(f32), axis=1) / mlp_gain.astype(f32)
    sum_out = tie(sum_out, tokens_grad).astype(f32)
    return (mixed, tokens_grad, sum_qkv, sum_out, sum_up, sum_down, grad_gain_one, grad_gain_two)


def solution(mesh):
    rows = P(("pb", "ka"), None)
    flat = P(("pb", "ka"))
    group = P("pb", None)
    return jax.shard_map(
        body,
        mesh=mesh,
        in_specs=(rows, group, group, rows, rows, rows, rows, flat, flat, rows),
        out_specs=(rows, rows, rows, rows, rows, rows, flat, flat),
        check_vma=False,
    )
```

```python
import functools
import math

import jax
import jax.numpy as jnp
from jax import lax
from jax.experimental import pallas as pl
from jax.experimental.pallas import tpu as pltpu
from jax.sharding import PartitionSpec as P

HEADS = 12
HEAD_DIM = 64
BLK = 128
SEQ_UNIT = 1024
epsilon = 1e-05
f32 = jnp.float32
bf16 = jnp.bfloat16


class Grid:
    def __init__(self, nb, nk):
        nhi = math.gcd(4, nb)
        nc = math.gcd(2, nk)
        self.sizes = {"hi": nhi, "lo": nb // nhi, "x": nk // nc, "c": nc}
        self.nb, self.nk = nb, nk
        pb, ka = lax.axis_index("pb"), lax.axis_index("ka")
        self.pb, self.ka = pb, ka
        self.at = {"hi": pb // self.sizes["lo"], "lo": pb % self.sizes["lo"], "x": ka // nc, "c": ka % nc}

    def fetch(self, value, flip=0, **steps):
        n = self.sizes
        pairs = []
        for hi in range(n["hi"]):
            for lo in range(n["lo"]):
                for x in range(n["x"]):
                    for c in range(n["c"]):
                        here = {"hi": hi, "lo": lo, "x": x, "c": c}
                        there = {d: here[d] ^ steps[d] if flip and d in steps else (here[d] + steps.get(d, 0)) % n[d] for d in here}
                        flat = [((p["hi"] * n["lo"] + p["lo"]) * n["x"] + p["x"]) * n["c"] + p["c"] for p in (there, here)]
                        pairs.append(tuple(flat))
        return lax.ppermute(value, ("pb", "ka"), pairs)

    def gather(self, value, dim):
        return jnp.stack([value] + [self.fetch(value, **{dim: r}) for r in range(1, self.sizes[dim])])

    def in_order(self, pieces, dim):
        n, me = self.sizes[dim], self.at[dim]
        if n == 1:
            return pieces
        if n == 2:
            return [jnp.where(me == 0, pieces[0], pieces[1]), jnp.where(me == 0, pieces[1], pieces[0])]
        stacked = jnp.stack(pieces)
        return [lax.dynamic_index_in_dim(stacked, (i - me) % n, 0, keepdims=False) for i in range(n)]

    def group_in_order(self, pieces):
        nx, nc = self.sizes["x"], self.sizes["c"]
        by_x = [self.in_order(pieces[i * nc : (i + 1) * nc], "c") for i in range(nx)]
        by_c = [self.in_order([row[c] for row in by_x], "x") for c in range(nc)]
        return [by_c[c][x] for x in range(nx) for c in range(nc)]

    def split(self, parts, axis, dim):
        n, me = self.sizes[dim], self.at[dim]
        own = lax.dynamic_index_in_dim(parts, me, axis, keepdims=False)
        return own, [lax.dynamic_index_in_dim(parts, (me - r) % n, axis, keepdims=False) for r in range(1, n)]

    def halve(self, parts, dim, bit):
        mine = (self.at[dim] >> bit) % 2
        parts = parts.reshape((-1, 2) + parts.shape[1:])
        kept = lax.dynamic_index_in_dim(parts, mine, 1, keepdims=False)
        return kept, lax.dynamic_index_in_dim(parts, 1 - mine, 1, keepdims=False)

    def swap(self, value, dim, bit):
        return self.fetch(value, 1, **{dim: 1 << bit})

    def send(self, sends, dim):
        return [self.fetch(sent, **{dim: r + 1}) for r, sent in enumerate(sends)]


def added(own, received, last=False):
    total = own.astype(f32)
    for one in received:
        total = total + one.astype(f32)
    return total if last else total.astype(own.dtype)


def together(*values):
    return lax.optimization_barrier(values)


def place_kernel(counts, rows, offs_ref, *refs):
    ins, out_ref, sems = refs[: len(counts)], refs[len(counts)], refs[len(counts) + 1]
    copies = []
    for ref, count in zip(ins, counts):
        for i in range(count):
            at = pl.multiple_of(offs_ref[len(copies)], rows)
            copies.append(pltpu.make_async_copy(ref.at[i], out_ref.at[pl.ds(at, rows), :], sems.at[len(copies)]))
    for copy in copies:
        copy.start()
    for copy in copies:
        copy.wait()


def place(stacks, offsets):
    rows, cols = stacks[0].shape[1:]
    counts = [s.shape[0] for s in stacks]
    total = sum(counts)
    return pl.pallas_call(
        functools.partial(place_kernel, counts, rows),
        out_shape=jax.ShapeDtypeStruct((total * rows, cols), stacks[0].dtype),
        in_specs=[pl.BlockSpec(memory_space=pltpu.SMEM)] + [pl.BlockSpec(memory_space=pl.ANY)] * len(stacks),
        out_specs=pl.BlockSpec(memory_space=pltpu.VMEM),
        scratch_shapes=[pltpu.SemaphoreType.DMA((total,))],
        compiler_params=pltpu.CompilerParams(vmem_limit_bytes=16 * 2**20),
        cost_estimate=pl.CostEstimate(flops=10**6, bytes_accessed=10**5, transcendentals=0),
    )(offsets.astype(jnp.int32), *stacks)


def tie(value, *before):
    return lax.optimization_barrier((value,) + before)[0]


def put_in_place(stacks, index):
    rows = stacks[0].shape[1]
    if rows % 16 == 0:
        return place(stacks, index * rows)
    order = jnp.argsort(index)
    out = jnp.concatenate(stacks, axis=0)
    return jnp.concatenate([lax.dynamic_index_in_dim(out, order[i], 0, keepdims=False) for i in range(index.shape[0])], axis=0)


def gather_rows(grid, piece, order, gates=None, begun=None, done=("hi",), raw=False):
    if begun is None:
        stack, steps = piece[None], [dict()]
    else:
        stack, steps = begun, [dict()]
        for dim in done:
            steps = steps + [{**s, dim: r} for r in range(1, grid.sizes[dim]) for s in steps]
        piece = stack[0]
    stacks = []
    received = {}
    for dim in order:
        if gates and dim in gates:
            stack = tie(stack, *gates[dim])
        got = [grid.fetch(stack, **{dim: r}) for r in range(1, grid.sizes[dim])]
        received[dim] = got
        steps = steps + [{**s, dim: r} for r in range(1, grid.sizes[dim]) for s in steps]
        if dim == order[-1]:
            stacks = [stack] + got
        else:
            stack = jnp.concatenate([stack] + got, axis=0)
    dims = [d for d in ("hi", "lo", "x") if d in order or (begun is not None and d in done)]
    rows = piece.shape[0]
    index = []
    for s in steps:
        at = 0
        for d in dims:
            at = at * grid.sizes[d] + (grid.at[d] + s.get(d, 0)) % grid.sizes[d]
        index.append(at)
    index = jnp.stack(index).astype(jnp.int32)
    if begun is not None and len(order) == 1 and raw:
        return stacks, index
    if gates and "place" in gates:
        stacks, _ = together(stacks, gates["place"])
    return put_in_place(stacks, index), received


def lane_tile(at, size):
    return pl.ds(pl.multiple_of(at, BLK), size)


def head_rows(sets, kind, head):
    at = 0
    for one in sets:
        if head in one:
            return slice(at + (kind * len(one) + one.index(head)) * HEAD_DIM, at + (kind * len(one) + one.index(head) + 1) * HEAD_DIM)
        at += 3 * len(one) * HEAD_DIM


def pipeline(work, first, second, third):
    held = {}
    for t in range(len(work) + 2):
        if t < len(work):
            held[t] = first(work[t])
        if 1 <= t <= len(work):
            held[t - 1] = second(work[t - 1], held[t - 1])
        if t >= 2:
            third(work[t - 2], held.pop(t - 2))


def spans_to(begin, end, chunk):
    spans = []
    while begin < end:
        size = min(chunk, end - begin)
        spans.append((begin, size, begin + size == end))
        begin += size
    return spans


def forward_kernel(sets, tile, chunk, unit, meta_ref, qkv_ref, out_ref, att_ref, lse_ref, sorted_ref, keys_ref):
    heads = sum(len(one) for one in sets)
    row_len = qkv_ref.shape[1]
    blocks = row_len // BLK
    per_device = out_ref.shape[2] // BLK
    for b in range(blocks):
        sorted_ref[:, b * BLK : (b + 1) * BLK] = qkv_ref[:, lane_tile(meta_ref[b] * BLK, BLK)]
    for h in range(heads):
        keys_ref[h] = sorted_ref[head_rows(sets, 1, h), :].astype(f32).T.astype(bf16)
    doc_units = meta_ref[blocks] // unit
    seen = lax.broadcasted_iota(jnp.int32, (tile, tile), 0) <= lax.broadcasted_iota(jnp.int32, (tile, tile), 1)
    lse_ref[...] = jnp.zeros_like(lse_ref)
    for i in range(row_len // tile):
        lanes = slice(i * tile, (i + 1) * tile)
        queries = [sorted_ref[head_rows(sets, 0, h), lanes] for h in range(heads)]

        def run(spans, carry):
            carry = list(carry)

            def first(item):
                h, begin, size, _ = item
                return jnp.dot(keys_ref[h, pl.ds(begin, size), :], queries[h], preferred_element_type=f32)

            def second(item, scores):
                h, _, size, diagonal = item
                peak, total, acc = carry[h]
                square = scores * scores + 1.0
                inverse = lax.rsqrt(square)
                reach = square * inverse
                if diagonal:
                    low = jnp.where(seen, reach[size - tile :], -1e30)
                    reach = low if size == tile else jnp.concatenate([reach[: size - tile], low], axis=0)
                top = jnp.maximum(peak, jnp.max(reach, axis=0, keepdims=True))
                shares = jnp.exp(reach - top)
                fade = jnp.exp(peak - top)
                total = total * fade + jnp.sum(shares, axis=0, keepdims=True)
                carry[h] = (top, total, acc)
                return (shares * (scores * inverse)).astype(bf16), fade

            def third(item, kept):
                h, begin, size, _ = item
                mixing, fade = kept
                top, total, acc = carry[h]
                values = sorted_ref[head_rows(sets, 2, h), pl.ds(begin, size)]
                carry[h] = (top, total, acc * fade + jnp.dot(values, mixing, preferred_element_type=f32))

            pipeline([(h,) + span for span in spans for h in range(heads)], first, second, third)
            return tuple(carry)

        here = i * tile // unit
        start = (jnp.ones((1, tile), f32), jnp.zeros((1, tile), f32), jnp.zeros((HEAD_DIM, tile), f32))
        carry = run(spans_to(here * unit, (i + 1) * tile, chunk), (start,) * heads)
        if here > 0:

            def earlier(k, carry):
                base = pl.multiple_of(k * unit, unit)
                return run([(base + o, chunk, False) for o in range(0, unit, chunk)], carry)

            carry = lax.fori_loop(here // doc_units * doc_units, here, earlier, carry)
        for h in range(heads):
            peak, total, acc = carry[h]
            rows = slice(h * HEAD_DIM, (h + 1) * HEAD_DIM)
            result = acc / total
            att_ref[rows, lanes] = result
            lse_ref[h : h + 1, lanes] = peak + jnp.log(total)
            low = result.astype(bf16)
            for part in range(tile // BLK):
                spot = meta_ref[i * (tile // BLK) + part]
                out_ref[spot // per_device, rows, lane_tile((spot % per_device) * BLK, BLK)] = low[:, part * BLK : (part + 1) * BLK]


def forward_attention(meta, qkv, sets, devices):
    row_len = qkv.shape[1]
    heads = sum(len(one) for one in sets)
    width = heads * HEAD_DIM
    whole = pl.BlockSpec(memory_space=pltpu.VMEM)
    return pl.pallas_call(
        functools.partial(forward_kernel, sets, 256, 512, SEQ_UNIT),
        out_shape=(
            jax.ShapeDtypeStruct((devices, width, row_len // devices), bf16),
            jax.ShapeDtypeStruct((width, row_len), f32),
            jax.ShapeDtypeStruct((8, row_len), f32),
        ),
        in_specs=[pl.BlockSpec(memory_space=pltpu.SMEM), whole],
        out_specs=(whole, whole, whole),
        scratch_shapes=[pltpu.VMEM((3 * width, row_len), bf16), pltpu.VMEM((heads, row_len, HEAD_DIM), bf16)],
        compiler_params=pltpu.CompilerParams(vmem_limit_bytes=40 * 2**20),
        cost_estimate=pl.CostEstimate(flops=7 * 10**9 * heads, bytes_accessed=10**6, transcendentals=0),
    )(meta, qkv)


def backward_kernel(
    sets, which, tile, chunk, unit, meta_ref, qkv_ref, up_ref, att_ref, lse_ref, grad_ref, sorted_ref, ups_ref, nat_ref, stat_ref, dq_ref, dkv_ref
):
    heads = sets[which]
    count = len(heads)
    row_len = qkv_ref.shape[1]
    width = count * HEAD_DIM
    blocks = row_len // BLK
    per_device = up_ref.shape[2] // BLK
    base_row = head_rows(sets, 0, heads[0]).start
    ups_rows = slice(heads[0] * HEAD_DIM, (heads[-1] + 1) * HEAD_DIM)
    for b in range(blocks):
        spot = slice(b * BLK, (b + 1) * BLK)
        sorted_ref[:, spot] = qkv_ref[base_row : base_row + 3 * width, lane_tile(meta_ref[b] * BLK, BLK)]
        ups_ref[:, spot] = up_ref[meta_ref[b] // per_device, ups_rows, lane_tile((meta_ref[b] % per_device) * BLK, BLK)]
    own = [slice(h * HEAD_DIM, (h + 1) * HEAD_DIM) for h in range(3 * count)]
    for h in range(count):
        for part in range(2):
            nat_ref[part * count + h] = sorted_ref[own[part * count + h], :].astype(f32).T.astype(bf16)
        upstream = ups_ref[own[h], :].astype(f32)
        nat_ref[2 * count + h] = upstream.T.astype(bf16)
        att = att_ref[heads[h] * HEAD_DIM : (heads[h] + 1) * HEAD_DIM, :]
        delta = jnp.sum(upstream * att, axis=0, keepdims=True)
        stats = [lse_ref[heads[h] : heads[h] + 1, :], delta, jnp.zeros((6, row_len), f32)]
        stat_ref[h] = jnp.concatenate(stats, axis=0).T
    dkv_ref[...] = jnp.zeros_like(dkv_ref)
    doc_units = meta_ref[blocks] // unit
    seen = lax.broadcasted_iota(jnp.int32, (tile, tile), 0) >= lax.broadcasted_iota(jnp.int32, (tile, tile), 1)
    for i in range(row_len // tile):
        at = slice(i * tile, (i + 1) * tile)

        def run(spans, carry):
            carry = list(carry)

            def first(item):
                h, begin, size, _ = item
                lanes = pl.ds(begin, size)
                scores = jnp.dot(nat_ref[h, at, :], sorted_ref[own[count + h], lanes], preferred_element_type=f32)
                effect = jnp.dot(nat_ref[2 * count + h, at, :], sorted_ref[own[2 * count + h], lanes], preferred_element_type=f32)
                return scores, effect

            def second(item, kept):
                h, _, size, diagonal = item
                scores, effect = kept
                square = scores * scores + 1.0
                inverse = lax.rsqrt(square)
                shares = jnp.exp(square * inverse - stat_ref[h, at, 0:1])
                if diagonal:
                    low = jnp.where(seen, shares[:, size - tile :], 0.0)
                    shares = low if size == tile else jnp.concatenate([shares[:, : size - tile], low], axis=1)
                sign = scores * inverse
                twice = inverse * inverse
                grad = shares * (effect * (1.0 - twice + twice * inverse) - stat_ref[h, at, 1:2] * sign)
                return grad.astype(bf16), (shares * sign).astype(bf16)

            def third(item, kept):
                h, begin, size, _ = item
                grad, mixing = kept
                lanes = pl.ds(begin, size)
                carry[h] = carry[h] + jnp.dot(grad, nat_ref[count + h, pl.ds(begin, size), :], preferred_element_type=f32)
                dkv_ref[own[h], lanes] += jnp.dot(sorted_ref[own[h], at], grad, preferred_element_type=f32)
                dkv_ref[own[count + h], lanes] += jnp.dot(ups_ref[own[h], at], mixing, preferred_element_type=f32)

            pipeline([(h,) + span for span in spans for h in range(count)], first, second, third)
            return tuple(carry)

        here = i * tile // unit
        carry = run(spans_to(here * unit, (i + 1) * tile, chunk), (jnp.zeros((tile, HEAD_DIM), f32),) * count)
        if here > 0:

            def earlier(k, carry):
                base = pl.multiple_of(k * unit, unit)
                return run([(base + o, chunk, False) for o in range(0, unit, chunk)], carry)

            carry = lax.fori_loop(here // doc_units * doc_units, here, earlier, carry)
        dq_ref[at, :] = carry[0] if count == 1 else jnp.concatenate(carry, axis=1)
    scale = HEAD_DIM**-0.5
    for b in range(blocks):
        here = slice(b * BLK, (b + 1) * BLK)
        both = jnp.concatenate([dq_ref[here, :] * scale, dkv_ref[:, here].T], axis=1)
        grad_ref[pl.ds(pl.multiple_of(meta_ref[b] * BLK, BLK), BLK), :] = both.astype(bf16)


def backward_attention(meta, qkv, upstream, att, lse, sets, which):
    row_len = qkv.shape[1]
    count = len(sets[which])
    width = count * HEAD_DIM
    whole = pl.BlockSpec(memory_space=pltpu.VMEM)
    return pl.pallas_call(
        functools.partial(backward_kernel, sets, which, 256, 256, SEQ_UNIT),
        out_shape=jax.ShapeDtypeStruct((row_len, 3 * width), bf16),
        in_specs=[pl.BlockSpec(memory_space=pltpu.SMEM)] + [whole] * 4,
        out_specs=whole,
        scratch_shapes=[
            pltpu.VMEM((3 * width, row_len), bf16),
            pltpu.VMEM((width, row_len), bf16),
            pltpu.VMEM((3 * count, row_len, HEAD_DIM), bf16),
            pltpu.VMEM((count, row_len, 8), f32),
            pltpu.VMEM((row_len, width), f32),
            pltpu.VMEM((2 * width, row_len), f32),
        ],
        compiler_params=pltpu.CompilerParams(vmem_limit_bytes=48 * 2**20),
        cost_estimate=pl.CostEstimate(flops=13 * 10**9 * count if which == 0 else 10**6, bytes_accessed=10**5, transcendentals=0),
    )(meta, qkv, upstream, att, lse)


def project_kernel(sets, gain_lane, count, *refs):
    weight_ref, h1_ref, qkv_ref, turned_ref, gain_ref = refs[count:]
    columns = qkv_ref.shape[0]

    @pl.when(pl.program_id(0) == 0)
    def _():
        turned = weight_ref[...].astype(f32).T
        gain_ref[...] = turned[gain_lane : gain_lane + 8]
        turned = turned[:columns]
        for one in sets:
            begin = head_rows(sets, 0, one[0]).start
            end = begin + len(one) * HEAD_DIM
            stop = begin + 3 * len(one) * HEAD_DIM
            turned_ref[begin:end] = (turned[begin:end] * HEAD_DIM**-0.5).astype(bf16)
            turned_ref[end:stop] = turned[end:stop].astype(bf16)

    for i in range(count):

        @pl.when(pl.program_id(0) == i)
        def _(tokens_ref=refs[i]):
            values = tokens_ref[...].astype(f32)
            centered = values - jnp.mean(values, axis=-1, keepdims=True)
            inverse = lax.rsqrt(jnp.mean(centered * centered, axis=-1, keepdims=True) + epsilon)
            h1 = (centered * inverse * gain_ref[0:1]).T.astype(bf16)
            h1_ref[...] = h1
            qkv_ref[...] = jnp.dot(turned_ref[...], h1, preferred_element_type=f32).astype(bf16)


def project(pieces, weight, sets):
    step, model = pieces[0].shape
    count = len(pieces)
    row_len = count * step
    columns = 3 * HEAD_DIM * sum(len(one) for one in sets)
    return pl.pallas_call(
        functools.partial(project_kernel, sets, columns, count),
        grid=(count,),
        out_shape=(jax.ShapeDtypeStruct((model, row_len), bf16), jax.ShapeDtypeStruct((columns, row_len), bf16)),
        in_specs=[pl.BlockSpec((step, model), lambda i: (0, 0))] * count + [pl.BlockSpec(weight.shape, lambda i: (0, 0))],
        out_specs=(pl.BlockSpec((model, step), lambda i: (0, i)), pl.BlockSpec((columns, step), lambda i: (0, i))),
        scratch_shapes=[pltpu.VMEM((columns, model), bf16), pltpu.VMEM((8, model), f32)],
        compiler_params=pltpu.CompilerParams(vmem_limit_bytes=40 * 2**20),
        cost_estimate=pl.CostEstimate(flops=10**6, bytes_accessed=10**5, transcendentals=0),
    )(*pieces, weight)


def rows_kernel(count, strides, more, me_ref, left_ref, right_ref, *refs):
    outs, total_ref = refs[:-1], refs[-1]
    cols = right_ref.shape[1]
    total_ref[:, :cols] = jnp.dot(left_ref[...], right_ref[...], preferred_element_type=f32)
    if more:
        total_ref[:, cols:] = refs[0][...].astype(f32)
        outs = outs[1:]
    outer = strides
    rows = outs[0].shape[-2]
    for r in range(count):
        entry = (me_ref[0] + count - r) % count
        for a in range(outer):
            at = pl.multiple_of((a * count + entry) * rows, 8)
            outs[r][a] = total_ref[pl.ds(at, rows), :].astype(bf16)


def split_product(grid, left, right, dim, more=None):
    rows_all, cols = left.shape[0], right.shape[1]
    operands = [left, right]
    if more is not None:
        operands.append(more)
        cols += more.shape[1]
    outer, count = grid.sizes["hi"], grid.sizes[dim]
    rows = rows_all // (outer * count)
    whole = pl.BlockSpec(memory_space=pltpu.VMEM)
    outs = pl.pallas_call(
        functools.partial(rows_kernel, count, outer, more is not None),
        out_shape=tuple(jax.ShapeDtypeStruct((outer, rows, cols), bf16) for _ in range(count)),
        in_specs=[pl.BlockSpec(memory_space=pltpu.SMEM)] + [whole] * len(operands),
        out_specs=(whole,) * count,
        scratch_shapes=[pltpu.VMEM((rows_all, cols), f32)],
        compiler_params=pltpu.CompilerParams(vmem_limit_bytes=48 * 2**20),
        cost_estimate=pl.CostEstimate(flops=10**6, bytes_accessed=10**5, transcendentals=0),
    )(grid.at[dim].reshape(1).astype(jnp.int32), *operands)
    return outs[0], list(outs[1:])


def back_kernel(bounds, count, *refs):
    parts, weight_ref, outs = refs[:count], refs[count], refs[count + 1 :]
    pieces, rows = outs[0].shape[0], outs[0].shape[1]
    for x in range(pieces):
        for c, out_ref in enumerate(outs):
            here = slice((x * len(outs) + c) * rows, (x * len(outs) + c + 1) * rows)
            total = 0.0
            for i in range(count):
                weight = weight_ref[:, bounds[i] : bounds[i + 1]]
                total = total + lax.dot_general(parts[i][here, :], weight, (((1,), (1,)), ((), ())), preferred_element_type=f32)
            out_ref[x] = total.astype(bf16)


def back_project(grid, parts, weight, bounds):
    nx, nc = grid.sizes["x"], grid.sizes["c"]
    rows = parts[0].shape[0] // (nx * nc)
    whole = pl.BlockSpec(memory_space=pltpu.VMEM)
    return pl.pallas_call(
        functools.partial(back_kernel, bounds, len(parts)),
        out_shape=tuple(jax.ShapeDtypeStruct((nx, rows, weight.shape[0]), bf16) for _ in range(nc)),
        in_specs=[whole] * (len(parts) + 1),
        out_specs=(whole,) * nc,
        compiler_params=pltpu.CompilerParams(vmem_limit_bytes=48 * 2**20),
        cost_estimate=pl.CostEstimate(flops=10**6, bytes_accessed=10**5, transcendentals=0),
    )(*parts, weight)


def hidden_kernel(counts, folds, up_at, down_at, *refs):
    up_refs, down_refs = refs[: counts[0]], refs[counts[0] : counts[0] + counts[1]]
    rest = refs[counts[0] + counts[1] :]
    h2_refs, cot_refs = rest[:2], rest[2:4]
    act_ref, pre_ref, own_ref, sent_ref, up_ref, down_ref, up_sem, down_sem = rest[4:]
    model = up_ref.shape[0]
    rows = up_refs[0].shape[1] // folds
    strip = down_refs[0].shape[1]
    copies, later = [], []
    for ref in up_refs:
        for i in range(ref.shape[0]):
            at = pl.multiple_of(up_at[len(copies) // folds] * rows, rows)
            for f in range(folds):
                piece = ref.at[i, pl.ds(f * rows, rows), :]
                spot = up_ref.at[pl.ds(at, rows), pl.ds(f * model, model)]
                copies.append(pltpu.make_async_copy(piece, spot, up_sem.at[len(copies)]))
    for ref in down_refs:
        for i in range(ref.shape[0]):
            at = pl.multiple_of(down_at[len(later)] * strip, strip)
            later.append(pltpu.make_async_copy(ref.at[i], down_ref.at[pl.ds(at, strip), :], down_sem.at[len(later)]))
    for copy in copies + later:
        copy.start()
    for copy in copies + later:
        copy.wait()
    half = h2_refs[0].shape[0]
    hidden = up_ref.shape[1]
    width = 256
    root = (2.0 / math.pi) ** 0.5

    def first(item):
        i, at = item
        pre = jnp.dot(h2_refs[i][...], up_ref[:, at : at + width], preferred_element_type=f32)
        back = lax.dot_general(cot_refs[i][...], down_ref[at : at + width, :], (((1,), (1,)), ((), ())), preferred_element_type=f32)
        return pre, back

    def second(item, kept):
        i, at = item
        pre, back = kept
        square = pre * pre
        slope = jnp.tanh(pre * (root + root * 0.044715 * square))
        side = 0.5 + 0.5 * slope
        act_ref[i * half : (i + 1) * half, at : at + width] = (pre * side).astype(bf16)
        steep = side + (0.5 * pre) * (1.0 - slope * slope) * (root + 3 * root * 0.044715 * square)
        pre_ref[i * half : (i + 1) * half, at : at + width] = (steep * back).astype(bf16)

    pipeline([(i, at) for i in range(2) for at in range(0, hidden, width)], first, second, lambda item, kept: None)
    for i, ref in enumerate((own_ref, sent_ref)):
        for at in range(0, half, 256):
            left = pre_ref[i * half + at : i * half + at + 256, :]
            total = lax.dot_general(left, up_ref[...], (((1,), (1,)), ((), ())), preferred_element_type=f32)
            ref[at : at + 256, :] = total.astype(ref.dtype)


def hidden_layer(up_stacks, up_at, down_stacks, down_at, h2_pair, cot_pair, folds):
    half, model = h2_pair[0].shape
    up_count, down_count = sum(one.shape[0] for one in up_stacks), sum(one.shape[0] for one in down_stacks)
    hidden = folds * model
    whole, smem, far = (pl.BlockSpec(memory_space=m) for m in (pltpu.VMEM, pltpu.SMEM, pl.ANY))
    return pl.pallas_call(
        functools.partial(hidden_kernel, (len(up_stacks), len(down_stacks)), folds),
        out_shape=(
            jax.ShapeDtypeStruct((2 * half, hidden), bf16),
            jax.ShapeDtypeStruct((2 * half, hidden), bf16),
            jax.ShapeDtypeStruct((half, model), f32),
            jax.ShapeDtypeStruct((half, model), bf16),
        ),
        in_specs=[smem, smem] + [far] * (len(up_stacks) + len(down_stacks)) + [whole] * 4,
        out_specs=(whole,) * 4,
        scratch_shapes=[
            pltpu.VMEM((model, hidden), bf16),
            pltpu.VMEM((hidden, model), bf16),
            pltpu.SemaphoreType.DMA((up_count * folds,)),
            pltpu.SemaphoreType.DMA((down_count,)),
        ],
        compiler_params=pltpu.CompilerParams(vmem_limit_bytes=50 * 2**20),
        cost_estimate=pl.CostEstimate(flops=14 * 10**9, bytes_accessed=10**6, transcendentals=0),
    )(up_at, down_at, *up_stacks, *down_stacks, *h2_pair, *cot_pair)


def norm_parts(values):
    centered = values - jnp.mean(values, axis=-1, keepdims=True)
    inverse = lax.rsqrt(jnp.mean(centered * centered, axis=-1, keepdims=True) + epsilon)
    return centered * inverse, inverse


def norm_back(normed, inverse, gain, grad):
    c = grad * gain
    return (c - jnp.mean(c, axis=-1, keepdims=True) - normed * jnp.mean(c * normed, axis=-1, keepdims=True)) * inverse


def mm(a, b, dims):
    return lax.dot_general(a, b, ((dims[:1], dims[1:]), ((), ())), preferred_element_type=f32)


def body(
    tokens,
    lengths,
    block_place,
    qkv_weight,
    out_weight,
    up_weight,
    down_weight,
    attn_gain,
    mlp_gain,
    cotangent,
):
    nb, nk = lax.axis_size("pb"), lax.axis_size("ka")
    grid = Grid(nb, nk)
    nx, nc = grid.sizes["x"], grid.sizes["c"]
    x_at, c_at = grid.at["x"], grid.at["c"]
    tok_rows, model = tokens.shape
    shard = qkv_weight.shape[0]
    chips = nb * nx
    heads = -(-HEADS // nk)
    width = heads * HEAD_DIM
    lanes = -(-(3 * width + 2) // BLK) * BLK
    rels = [(xr, cr) for xr in range(nx) for cr in range(nc)]

    def ka_of(xr, cr):
        return ((x_at + xr) % nx) * nc + (c_at + cr) % nc

    def exchange(parts):
        got = [parts(grid.ka)]
        for xr, cr in rels[1:]:
            got.append(grid.fetch(parts(ka_of(-xr, -cr)), x=xr, c=cr))
        return got

    cut = max(1, heads - 1)
    sets = [tuple(range(cut)), tuple(range(cut, heads))] if heads > 1 else [(0,)]
    bounds = [0]
    for one in sets:
        bounds.append(bounds[-1] + 3 * len(one) * HEAD_DIM)

    def head_groups(weight):
        split = weight.reshape(weight.shape[0], 3, HEADS, HEAD_DIM)
        if heads * nk != HEADS:
            split = jnp.pad(split, ((0, 0), (0, 0), (0, heads * nk - HEADS), (0, 0)))
        split = split.reshape(-1, 3, nk, heads, HEAD_DIM)
        chosen = [split[:, :, :, one[0] : one[-1] + 1].transpose(2, 0, 1, 3, 4).reshape(nk, weight.shape[0], -1) for one in sets]
        return jnp.concatenate(chosen, axis=2)

    gains = jnp.stack([attn_gain, mlp_gain], axis=1)
    gains = jnp.pad(gains, ((0, 0), (0, lanes - 3 * width - 2)))
    own_qkv = jnp.concatenate([head_groups(qkv_weight), jnp.broadcast_to(gains[None], (nk,) + gains.shape)], axis=2)
    got = exchange(lambda ka: lax.dynamic_index_in_dim(own_qkv, ka, 0, keepdims=False))
    group_qkv = jnp.concatenate(grid.group_in_order(got), axis=0)

    first_tokens = tie(tokens, *got)
    by_x = [tokens] + [grid.fetch(first_tokens, x=r) for r in range(1, nx)]
    strip = down_weight.shape[0]
    up_split = jnp.transpose(up_weight.reshape(shard, chips, nc, strip), (2, 0, 1, 3)).reshape(nc, shard, chips * strip)
    own, sends = grid.split(up_split, 0, "c")
    up_part = jnp.concatenate(grid.in_order([own] + grid.send(sends, "c"), "c"), axis=0)
    folds = chips * strip // model
    up_part = jnp.concatenate([up_part[:, i * model : (i + 1) * model] for i in range(folds)], axis=0)
    both = jnp.concatenate([up_part, down_weight], axis=0)
    group_qkv, both = together(group_qkv, both)
    got_hi = [grid.fetch(group_qkv[None], hi=r) for r in range(1, grid.sizes["hi"])]
    stack = tie(jnp.stack(by_x), *got_hi)
    by_c = [by_x] + [list(grid.fetch(stack, c=r)) for r in range(1, nc)]
    row_tokens = [by_c[c][x] for x in range(nx) for c in range(nc)]
    qkv_stack = jnp.concatenate([group_qkv[None]] + got_hi, axis=0)
    full_qkv, _ = gather_rows(grid, None, ("lo",), {"place": row_tokens}, qkv_stack)

    full_out = lax.all_gather(tie(out_weight, *got_hi), ("pb", "ka"), axis=0, tiled=True)

    both = tie(both, qkv_stack, *row_tokens)
    both = grid.gather(both, "hi")

    slots = tok_rows // BLK
    holder = jnp.argsort(block_place[0]).astype(jnp.int32)
    holder_ka, holder_slot = holder // slots, holder % slots
    rel = ((holder_ka // nc - x_at) % nx) * nc + (holder_ka % nc - c_at) % nc
    meta = jnp.concatenate([rel * slots + holder_slot, lengths[0, :1]]).astype(jnp.int32)

    gain_one = full_qkv[:, 3 * width].astype(f32)
    gain_two = full_qkv[:, 3 * width + 1].astype(f32)
    inputs = tokens.astype(f32)
    h1, qkv = project(row_tokens, full_qkv, sets)
    row_len = h1.shape[1]
    up_rows = up_part.shape[0]
    up_stack, down_stack, _ = together(both[:, :up_rows], both[:, up_rows:], qkv)
    qkv = tie(qkv, up_stack, down_stack)
    up_stack = [up_stack] + [grid.fetch(up_stack, x=r) for r in range(1, nx)]
    down_stack = [down_stack] + [grid.fetch(down_stack, lo=r) for r in range(1, grid.sizes["lo"])]
    att_parts, att_row, lse = forward_attention(meta, qkv, sets, nk)
    att_parts, up_stack, down_stack = together(att_parts, up_stack, down_stack)
    up_stack, down_stack = jnp.concatenate(up_stack, axis=0), jnp.concatenate(down_stack, axis=0)
    up_stacks, up_at = gather_rows(grid, None, ("lo",), begun=up_stack, done=("hi", "x"), raw=True)
    down_stacks, down_at = gather_rows(grid, None, ("x",), begun=down_stack, done=("hi", "lo"), raw=True)
    got = [att_parts[0]]
    for xr, cr in rels[1:]:
        got.append(grid.fetch(att_parts[((-xr) % nx) * nc + (-cr) % nc], x=xr, c=cr))
    att = jnp.concatenate(grid.group_in_order(got), axis=0)[: HEADS * HEAD_DIM]

    late_cot = tie(cotangent, att_parts)
    cot_pair = [cotangent] + [grid.fetch(late_cot, c=r) for r in range(1, nc)]
    cots = jnp.concatenate(cot_pair, axis=0)
    att = tie(att, up_stack, down_stack)
    residual = inputs + mm(att, full_out, (0, 0))
    normed_two, inverse_two = norm_parts(residual)
    h2 = (normed_two * gain_two).astype(bf16)
    h2_pair = [h2] + [grid.fetch(h2, c=r) for r in range(1, nc)]
    h2s = jnp.concatenate(h2_pair, axis=0)

    def core_sum(part):
        pieces = part.reshape((nc, tok_rows) + part.shape[1:])
        total = pieces[0]
        for r in range(1, nc):
            total = total + grid.fetch(pieces[(nc - r) % nc].astype(bf16), c=r).astype(f32)
        return total

    if nc == 2 and strip % 16 == 0 and (nc * shard) % 16 == 0 and tok_rows % 256 == 0:
        hidden_low, grad_pre, grad_h2, grad_sent = hidden_layer(up_stacks, up_at, down_stacks, down_at, h2_pair, cot_pair, folds)
        grad_h2 = added(grad_h2, [grid.fetch(grad_sent, c=1)], True)
    else:
        full_up = put_in_place(up_stacks, up_at).reshape(chips, folds, nc * shard, model)
        full_up = jnp.transpose(full_up, (0, 2, 1, 3)).reshape(model, folds * model)
        hidden_act, gelu_back = jax.vjp(lambda v: jax.nn.gelu(v, approximate=True), mm(h2s, full_up, (1, 0)))
        hidden_low = hidden_act.astype(bf16)
        (grad_pre,) = gelu_back(mm(cots, put_in_place(down_stacks, down_at), (1, 1)))
        grad_pre = grad_pre.astype(bf16)
        grad_h2 = core_sum(mm(grad_pre, full_up, (1, 1)))
    grad_up = mm(h2s, grad_pre, (0, 0)).astype(bf16)
    grad_residual = cotangent.astype(f32) + norm_back(normed_two, inverse_two, gain_two, grad_h2)
    grad_res_low = grad_residual.astype(bf16)
    grad_att = mm(full_out, grad_res_low, (1, 1)).astype(bf16)
    if heads * nk != HEADS:
        grad_att = jnp.pad(grad_att, ((0, (heads * nk - HEADS) * HEAD_DIM), (0, 0)))
    grad_att = grad_att.reshape(nk, width, tok_rows)
    upstream = jnp.stack(exchange(lambda ka: lax.dynamic_index_in_dim(grad_att, ka, 0, keepdims=False)))
    late_low, late_res, _ = together(hidden_low, grad_res_low, grad_att)
    grad_down = mm(late_low, cots, (0, 0)).astype(bf16)
    grad_out = mm(att, late_res, (1, 0)).astype(bf16)

    n = grid.sizes

    def placed(grad):
        return grad.reshape(n["hi"], n["lo"], n["x"], -1, grad.shape[1])

    up_own, up_send = grid.split(placed(grad_up), 1, "lo")
    up_got = grid.send(up_send, "lo")
    down_own, down_send = grid.split(placed(grad_down), 2, "x")
    out_own, out_send = grid.split(grad_out.reshape(model, nc, model // nc), 1, "c")
    out_sum = added(out_own, grid.send(out_send, "c"))
    upstream, out_sum, down_send = together(upstream, out_sum, down_send)
    out_own, out_send = grid.split(out_sum.reshape(model, nx, model // nk), 1, "x")
    out_got = grid.send(out_send, "x")
    down_got = grid.send(down_send, "x")

    parts, qkv_rest, qkv_got = [], [], []
    last = len(sets) - 1
    for which in range(len(sets)):
        part = backward_attention(meta, qkv, upstream, att_row, lse, sets, which)
        if which == last:
            part, qkv_got, up_got = together(part, qkv_got, up_got)
        if which == 0:
            part, up_got, out_got = together(part, up_got, out_got)
            out_sum = added(out_own, out_got)
        parts.append(part)
        own, sends = split_product(grid, h1, part, "lo", out_sum if which == 0 else None)
        qkv_rest.append(own)
        qkv_got.append(grid.send(sends, "lo"))
        if which == 0:
            up_own, up_send = grid.halve(added(up_own, up_got), "hi", 0)
            up_got = [grid.swap(up_send, "hi", 0)]
            upstream, down_got, *_ = together(upstream, down_got, up_send, *sends)

    up_own, up_send = grid.halve(added(up_own, up_got), "hi", 1)
    down_own, down_send = grid.split(added(down_own, down_got), 1, "lo")
    up_got = [grid.swap(up_send, "hi", 1)]
    down_got = grid.send(down_send, "lo")
    late_part, *_ = together(parts[-1], *sends)
    grad_h1 = back_project(grid, parts[:-1] + [late_part], full_qkv, bounds)
    h1_got = grid.send([grad_h1[(nc - r) % nc] for r in range(1, nc)], "c")

    qkv_got, h1_got = together(qkv_got, h1_got)
    sums = [added(own, got) for own, got in zip(qkv_rest, qkv_got)]
    by_kind = []
    for kind in range(3):
        for i, one in enumerate(sets):
            begin = kind * len(one) * HEAD_DIM
            by_kind.append(sums[i][:, :, begin : begin + len(one) * HEAD_DIM])
    by_kind.append(sums[0][:, :, 3 * len(sets[0]) * HEAD_DIM :])
    qkv_own, qkv_send = grid.halve(jnp.concatenate(by_kind, axis=2), "hi", 0)
    qkv_got = [grid.swap(qkv_send, "hi", 0)]
    h1_own = added(grad_h1[0], h1_got)
    h1_got = grid.send([h1_own[(nx - r) % nx] for r in range(1, nx)], "x")

    qkv_got, up_got, down_got = together(qkv_got, up_got, down_got)
    qkv_own, qkv_send = grid.halve(added(qkv_own, qkv_got), "hi", 1)
    qkv_got = [grid.swap(qkv_send, "hi", 1)]
    up_own, up_send = grid.split(added(up_own, up_got)[0], 0, "x")
    up_got = grid.send(up_send, "x")
    down_own, down_send = grid.halve(added(down_own, down_got), "hi", 0)
    down_got = [grid.swap(down_send, "hi", 0)]

    low, stacks, _ = together(hidden_low, down_stacks, qkv_send)
    mixed = mm(low, put_in_place(stacks, down_at), (1, 0)).reshape(nc, tok_rows, model)
    mixed_got = [grid.fetch(mixed[(nc - r) % nc].astype(bf16), c=r) for r in range(1, nc)]
    mixed = (residual + added(mixed[0], mixed_got, True)).astype(bf16)

    qkv_got, h1_got, up_got, down_got = together(qkv_got, h1_got, up_got, down_got)
    group_grad = added(qkv_own, qkv_got, True).reshape(nx, nc, shard, -1)
    group_own, group_send = grid.split(group_grad, 0, "x")
    group_got = grid.send(group_send, "x")
    up_own, up_send = grid.split(added(up_own, up_got, True).reshape(nc, shard, -1), 0, "c")
    up_got = grid.send(up_send, "c")
    down_own, down_send = grid.halve(added(down_own, down_got), "hi", 1)
    down_got = [grid.swap(down_send, "hi", 1)]

    group_got, up_got = together(group_got, up_got)
    by_x = grid.in_order([group_own] + group_got, "x")
    group_own, group_send = grid.split(jnp.stack(by_x), 1, "c")
    by_c = grid.in_order([group_own] + grid.send(group_send, "c"), "c")
    got = [by_c[c][x] for x in range(nx) for c in range(nc)]
    sum_up = grid.in_order([up_own] + up_got, "c")

    sum_out = jnp.concatenate([got[x * nc + c][:, 3 * width :] for c in range(nc) for x in range(nx)], axis=1)
    kept = min(nk * width, HEADS * HEAD_DIM)
    sum_qkv = []
    for kind in range(3):
        for i, one in enumerate(got):
            size = min(width, kept - i * width)
            if size > 0:
                sum_qkv.append(one[:, kind * width : kind * width + size])
    sum_qkv = jnp.concatenate(sum_qkv, axis=1)
    sum_up = jnp.stack([one.reshape(shard, chips, strip) for one in sum_up], axis=2).reshape(shard, -1)
    sum_down = added(down_own, down_got, True)[0]
    normed_one, inverse_one = norm_parts(inputs)
    tokens_grad = added(h1_own[0], h1_got, True)
    tokens_grad = (grad_residual + norm_back(normed_one, inverse_one, gain_one, tokens_grad)).astype(bf16)

    grad_gain_one = jnp.sum(sum_qkv * qkv_weight.astype(f32), axis=1) / attn_gain.astype(f32)
    grad_gain_two = jnp.sum(sum_up * up_weight.astype(f32), axis=1) / mlp_gain.astype(f32)
    return (mixed, tokens_grad, sum_qkv, sum_out, sum_up, sum_down, grad_gain_one, grad_gain_two)


def solution(mesh):
    rows = P(("pb", "ka"), None)
    flat = P(("pb", "ka"))
    group = P("pb", None)
    return jax.shard_map(
        body,
        mesh=mesh,
        in_specs=(rows, group, group, rows, rows, rows, rows, flat, flat, rows),
        out_specs=(rows, rows, rows, rows, rows, rows, flat, flat),
        check_vma=False,
    )
```

```python
import functools
import math

import jax
import jax.numpy as jnp
from jax import lax
from jax.experimental import pallas as pl
from jax.experimental.pallas import tpu as pltpu
from jax.sharding import PartitionSpec as P

HEADS = 12
HEAD_DIM = 64
BLK = 128
SEQ_UNIT = 1024
epsilon = 1e-05
f32 = jnp.float32
bf16 = jnp.bfloat16


class Grid:
    def __init__(self, nb, nk):
        nhi = math.gcd(4, nb)
        nc = math.gcd(2, nk)
        self.sizes = {"hi": nhi, "lo": nb // nhi, "x": nk // nc, "c": nc}
        self.nb, self.nk = nb, nk
        pb, ka = lax.axis_index("pb"), lax.axis_index("ka")
        self.pb, self.ka = pb, ka
        self.at = {"hi": pb // self.sizes["lo"], "lo": pb % self.sizes["lo"], "x": ka // nc, "c": ka % nc}

    def fetch(self, value, flip=0, **steps):
        n = self.sizes
        pairs = []
        for hi in range(n["hi"]):
            for lo in range(n["lo"]):
                for x in range(n["x"]):
                    for c in range(n["c"]):
                        here = {"hi": hi, "lo": lo, "x": x, "c": c}
                        there = {d: here[d] ^ steps[d] if flip and d in steps else (here[d] + steps.get(d, 0)) % n[d] for d in here}
                        flat = [((p["hi"] * n["lo"] + p["lo"]) * n["x"] + p["x"]) * n["c"] + p["c"] for p in (there, here)]
                        pairs.append(tuple(flat))
        return lax.ppermute(value, ("pb", "ka"), pairs)

    def gather(self, value, dim):
        return jnp.stack([value] + [self.fetch(value, **{dim: r}) for r in range(1, self.sizes[dim])])

    def in_order(self, pieces, dim):
        n, me = self.sizes[dim], self.at[dim]
        if n == 1:
            return pieces
        if n == 2:
            return [jnp.where(me == 0, pieces[0], pieces[1]), jnp.where(me == 0, pieces[1], pieces[0])]
        stacked = jnp.stack(pieces)
        return [lax.dynamic_index_in_dim(stacked, (i - me) % n, 0, keepdims=False) for i in range(n)]

    def group_in_order(self, pieces):
        nx, nc = self.sizes["x"], self.sizes["c"]
        by_x = [self.in_order(pieces[i * nc : (i + 1) * nc], "c") for i in range(nx)]
        by_c = [self.in_order([row[c] for row in by_x], "x") for c in range(nc)]
        return [by_c[c][x] for x in range(nx) for c in range(nc)]

    def split(self, parts, axis, dim):
        n, me = self.sizes[dim], self.at[dim]
        own = lax.dynamic_index_in_dim(parts, me, axis, keepdims=False)
        return own, [lax.dynamic_index_in_dim(parts, (me - r) % n, axis, keepdims=False) for r in range(1, n)]

    def halve(self, parts, dim, bit):
        mine = (self.at[dim] >> bit) % 2
        parts = parts.reshape((-1, 2) + parts.shape[1:])
        kept = lax.dynamic_index_in_dim(parts, mine, 1, keepdims=False)
        return kept, lax.dynamic_index_in_dim(parts, 1 - mine, 1, keepdims=False)

    def swap(self, value, dim, bit):
        return self.fetch(value, 1, **{dim: 1 << bit})

    def send(self, sends, dim):
        return [self.fetch(sent, **{dim: r + 1}) for r, sent in enumerate(sends)]


def added(own, received, last=False):
    total = own.astype(f32)
    for one in received:
        total = total + one.astype(f32)
    return total if last else total.astype(own.dtype)


def together(*values):
    return lax.optimization_barrier(values)


def place_kernel(counts, rows, offs_ref, *refs):
    ins, out_ref, sems = refs[: len(counts)], refs[len(counts)], refs[len(counts) + 1]
    copies = []
    for ref, count in zip(ins, counts):
        for i in range(count):
            at = pl.multiple_of(offs_ref[len(copies)], rows)
            copies.append(pltpu.make_async_copy(ref.at[i], out_ref.at[pl.ds(at, rows), :], sems.at[len(copies)]))
    for copy in copies:
        copy.start()
    for copy in copies:
        copy.wait()


def place(stacks, offsets):
    rows, cols = stacks[0].shape[1:]
    counts = [s.shape[0] for s in stacks]
    total = sum(counts)
    return pl.pallas_call(
        functools.partial(place_kernel, counts, rows),
        out_shape=jax.ShapeDtypeStruct((total * rows, cols), stacks[0].dtype),
        in_specs=[pl.BlockSpec(memory_space=pltpu.SMEM)] + [pl.BlockSpec(memory_space=pl.ANY)] * len(stacks),
        out_specs=pl.BlockSpec(memory_space=pltpu.VMEM),
        scratch_shapes=[pltpu.SemaphoreType.DMA((total,))],
        compiler_params=pltpu.CompilerParams(vmem_limit_bytes=16 * 2**20),
        cost_estimate=pl.CostEstimate(flops=10**6, bytes_accessed=10**5, transcendentals=0),
    )(offsets.astype(jnp.int32), *stacks)


def tie(value, *before):
    return lax.optimization_barrier((value,) + before)[0]


def put_in_place(stacks, index):
    rows = stacks[0].shape[1]
    if rows % 16 == 0:
        return place(stacks, index * rows)
    order = jnp.argsort(index)
    out = jnp.concatenate(stacks, axis=0)
    return jnp.concatenate([lax.dynamic_index_in_dim(out, order[i], 0, keepdims=False) for i in range(index.shape[0])], axis=0)


def gather_rows(grid, piece, order, gates=None, begun=None, done=("hi",), raw=False):
    if begun is None:
        stack, steps = piece[None], [dict()]
    else:
        stack, steps = begun, [dict()]
        for dim in done:
            steps = steps + [{**s, dim: r} for r in range(1, grid.sizes[dim]) for s in steps]
        piece = stack[0]
    stacks = []
    received = {}
    for dim in order:
        if gates and dim in gates:
            stack = tie(stack, *gates[dim])
        got = [grid.fetch(stack, **{dim: r}) for r in range(1, grid.sizes[dim])]
        received[dim] = got
        steps = steps + [{**s, dim: r} for r in range(1, grid.sizes[dim]) for s in steps]
        if dim == order[-1]:
            stacks = [stack] + got
        else:
            stack = jnp.concatenate([stack] + got, axis=0)
    dims = [d for d in ("hi", "lo", "x") if d in order or (begun is not None and d in done)]
    rows = piece.shape[0]
    index = []
    for s in steps:
        at = 0
        for d in dims:
            at = at * grid.sizes[d] + (grid.at[d] + s.get(d, 0)) % grid.sizes[d]
        index.append(at)
    index = jnp.stack(index).astype(jnp.int32)
    if begun is not None and len(order) == 1 and raw:
        return stacks, index
    if gates and "place" in gates:
        stacks, _ = together(stacks, gates["place"])
    return put_in_place(stacks, index), received


def lane_tile(at, size):
    return pl.ds(pl.multiple_of(at, BLK), size)


def head_rows(sets, kind, head):
    at = 0
    for one in sets:
        if head in one:
            return slice(at + (kind * len(one) + one.index(head)) * HEAD_DIM, at + (kind * len(one) + one.index(head) + 1) * HEAD_DIM)
        at += 3 * len(one) * HEAD_DIM


def pipeline(work, first, second, third):
    held = {}
    for t in range(len(work) + 2):
        if t < len(work):
            held[t] = first(work[t])
        if 1 <= t <= len(work):
            held[t - 1] = second(work[t - 1], held[t - 1])
        if t >= 2:
            third(work[t - 2], held.pop(t - 2))


def spans_to(begin, end, chunk):
    spans = []
    while begin < end:
        size = min(chunk, end - begin)
        spans.append((begin, size, begin + size == end))
        begin += size
    return spans


def forward_kernel(sets, tile, chunk, unit, meta_ref, qkv_ref, out_ref, att_ref, lse_ref, sorted_ref, keys_ref):
    heads = sum(len(one) for one in sets)
    row_len = qkv_ref.shape[1]
    blocks = row_len // BLK
    per_device = out_ref.shape[2] // BLK
    for b in range(blocks):
        sorted_ref[:, b * BLK : (b + 1) * BLK] = qkv_ref[:, lane_tile(meta_ref[b] * BLK, BLK)]
    for h in range(heads):
        keys_ref[h] = sorted_ref[head_rows(sets, 1, h), :].astype(f32).T.astype(bf16)
    doc_units = jnp.maximum(meta_ref[blocks] // unit, 1)
    seen = lax.broadcasted_iota(jnp.int32, (tile, tile), 0) <= lax.broadcasted_iota(jnp.int32, (tile, tile), 1)
    lse_ref[...] = jnp.zeros_like(lse_ref)
    for i in range(row_len // tile):
        lanes = slice(i * tile, (i + 1) * tile)
        queries = [sorted_ref[head_rows(sets, 0, h), lanes] for h in range(heads)]

        def run(spans, carry):
            carry = list(carry)

            def first(item):
                h, begin, size, _ = item
                return jnp.dot(keys_ref[h, pl.ds(begin, size), :], queries[h], preferred_element_type=f32)

            def second(item, scores):
                h, _, size, diagonal = item
                peak, total, acc = carry[h]
                square = scores * scores + 1.0
                inverse = lax.rsqrt(square)
                reach = square * inverse
                if diagonal:
                    low = jnp.where(seen, reach[size - tile :], -1e30)
                    reach = low if size == tile else jnp.concatenate([reach[: size - tile], low], axis=0)
                top = jnp.maximum(peak, jnp.max(reach, axis=0, keepdims=True))
                shares = jnp.exp(reach - top)
                fade = jnp.exp(peak - top)
                total = total * fade + jnp.sum(shares, axis=0, keepdims=True)
                carry[h] = (top, total, acc)
                return (shares * (scores * inverse)).astype(bf16), fade

            def third(item, kept):
                h, begin, size, _ = item
                mixing, fade = kept
                top, total, acc = carry[h]
                values = sorted_ref[head_rows(sets, 2, h), pl.ds(begin, size)]
                carry[h] = (top, total, acc * fade + jnp.dot(values, mixing, preferred_element_type=f32))

            pipeline([(h,) + span for span in spans for h in range(heads)], first, second, third)
            return tuple(carry)

        here = i * tile // unit
        start = (jnp.ones((1, tile), f32), jnp.zeros((1, tile), f32), jnp.zeros((HEAD_DIM, tile), f32))
        carry = run(spans_to(here * unit, (i + 1) * tile, chunk), (start,) * heads)
        if here > 0:

            def earlier(k, carry):
                base = pl.multiple_of(k * unit, unit)
                return run([(base + o, chunk, False) for o in range(0, unit, chunk)], carry)

            carry = lax.fori_loop(here // doc_units * doc_units, here, earlier, carry)
        for h in range(heads):
            peak, total, acc = carry[h]
            rows = slice(h * HEAD_DIM, (h + 1) * HEAD_DIM)
            result = acc / total
            att_ref[rows, lanes] = result
            lse_ref[h : h + 1, lanes] = peak + jnp.log(total)
            low = result.astype(bf16)
            for part in range(tile // BLK):
                spot = meta_ref[i * (tile // BLK) + part]
                out_ref[spot // per_device, rows, lane_tile((spot % per_device) * BLK, BLK)] = low[:, part * BLK : (part + 1) * BLK]


def forward_attention(meta, qkv, sets, devices):
    row_len = qkv.shape[1]
    heads = sum(len(one) for one in sets)
    width = heads * HEAD_DIM
    whole = pl.BlockSpec(memory_space=pltpu.VMEM)
    return pl.pallas_call(
        functools.partial(forward_kernel, sets, 256, 512, SEQ_UNIT),
        out_shape=(
            jax.ShapeDtypeStruct((devices, width, row_len // devices), bf16),
            jax.ShapeDtypeStruct((width, row_len), f32),
            jax.ShapeDtypeStruct((8, row_len), f32),
        ),
        in_specs=[pl.BlockSpec(memory_space=pltpu.SMEM), whole],
        out_specs=(whole, whole, whole),
        scratch_shapes=[pltpu.VMEM((3 * width, row_len), bf16), pltpu.VMEM((heads, row_len, HEAD_DIM), bf16)],
        compiler_params=pltpu.CompilerParams(vmem_limit_bytes=40 * 2**20),
        cost_estimate=pl.CostEstimate(flops=7 * 10**9 * heads, bytes_accessed=10**6, transcendentals=0),
    )(meta, qkv)


def backward_kernel(
    sets, which, tile, chunk, unit, meta_ref, qkv_ref, up_ref, att_ref, lse_ref, grad_ref, sorted_ref, ups_ref, nat_ref, stat_ref, dq_ref, dkv_ref
):
    heads = sets[which]
    count = len(heads)
    row_len = qkv_ref.shape[1]
    width = count * HEAD_DIM
    blocks = row_len // BLK
    per_device = up_ref.shape[2] // BLK
    base_row = head_rows(sets, 0, heads[0]).start
    ups_rows = slice(heads[0] * HEAD_DIM, (heads[-1] + 1) * HEAD_DIM)
    for b in range(blocks):
        spot = slice(b * BLK, (b + 1) * BLK)
        sorted_ref[:, spot] = qkv_ref[base_row : base_row + 3 * width, lane_tile(meta_ref[b] * BLK, BLK)]
        ups_ref[:, spot] = up_ref[meta_ref[b] // per_device, ups_rows, lane_tile((meta_ref[b] % per_device) * BLK, BLK)]
    own = [slice(h * HEAD_DIM, (h + 1) * HEAD_DIM) for h in range(3 * count)]
    for h in range(count):
        for part in range(2):
            nat_ref[part * count + h] = sorted_ref[own[part * count + h], :].astype(f32).T.astype(bf16)
        upstream = ups_ref[own[h], :].astype(f32)
        nat_ref[2 * count + h] = upstream.T.astype(bf16)
        att = att_ref[heads[h] * HEAD_DIM : (heads[h] + 1) * HEAD_DIM, :]
        delta = jnp.sum(upstream * att, axis=0, keepdims=True)
        stats = [lse_ref[heads[h] : heads[h] + 1, :], delta, jnp.zeros((6, row_len), f32)]
        stat_ref[h] = jnp.concatenate(stats, axis=0).T
    dkv_ref[...] = jnp.zeros_like(dkv_ref)
    doc_units = jnp.maximum(meta_ref[blocks] // unit, 1)
    seen = lax.broadcasted_iota(jnp.int32, (tile, tile), 0) >= lax.broadcasted_iota(jnp.int32, (tile, tile), 1)
    for i in range(row_len // tile):
        at = slice(i * tile, (i + 1) * tile)

        def run(spans, carry):
            carry = list(carry)

            def first(item):
                h, begin, size, _ = item
                lanes = pl.ds(begin, size)
                scores = jnp.dot(nat_ref[h, at, :], sorted_ref[own[count + h], lanes], preferred_element_type=f32)
                effect = jnp.dot(nat_ref[2 * count + h, at, :], sorted_ref[own[2 * count + h], lanes], preferred_element_type=f32)
                return scores, effect

            def second(item, kept):
                h, _, size, diagonal = item
                scores, effect = kept
                square = scores * scores + 1.0
                inverse = lax.rsqrt(square)
                shares = jnp.exp(square * inverse - stat_ref[h, at, 0:1])
                if diagonal:
                    low = jnp.where(seen, shares[:, size - tile :], 0.0)
                    shares = low if size == tile else jnp.concatenate([shares[:, : size - tile], low], axis=1)
                sign = scores * inverse
                twice = inverse * inverse
                grad = shares * (effect * (1.0 - twice + twice * inverse) - stat_ref[h, at, 1:2] * sign)
                return grad.astype(bf16), (shares * sign).astype(bf16)

            def third(item, kept):
                h, begin, size, _ = item
                grad, mixing = kept
                lanes = pl.ds(begin, size)
                carry[h] = carry[h] + jnp.dot(grad, nat_ref[count + h, pl.ds(begin, size), :], preferred_element_type=f32)
                dkv_ref[own[h], lanes] += jnp.dot(sorted_ref[own[h], at], grad, preferred_element_type=f32)
                dkv_ref[own[count + h], lanes] += jnp.dot(ups_ref[own[h], at], mixing, preferred_element_type=f32)

            pipeline([(h,) + span for span in spans for h in range(count)], first, second, third)
            return tuple(carry)

        here = i * tile // unit
        carry = run(spans_to(here * unit, (i + 1) * tile, chunk), (jnp.zeros((tile, HEAD_DIM), f32),) * count)
        if here > 0:

            def earlier(k, carry):
                base = pl.multiple_of(k * unit, unit)
                return run([(base + o, chunk, False) for o in range(0, unit, chunk)], carry)

            carry = lax.fori_loop(here // doc_units * doc_units, here, earlier, carry)
        dq_ref[at, :] = carry[0] if count == 1 else jnp.concatenate(carry, axis=1)
    scale = HEAD_DIM**-0.5
    for b in range(blocks):
        here = slice(b * BLK, (b + 1) * BLK)
        both = jnp.concatenate([dq_ref[here, :] * scale, dkv_ref[:, here].T], axis=1)
        grad_ref[pl.ds(pl.multiple_of(meta_ref[b] * BLK, BLK), BLK), :] = both.astype(bf16)


def backward_attention(meta, qkv, upstream, att, lse, sets, which):
    row_len = qkv.shape[1]
    count = len(sets[which])
    width = count * HEAD_DIM
    whole = pl.BlockSpec(memory_space=pltpu.VMEM)
    return pl.pallas_call(
        functools.partial(backward_kernel, sets, which, 256, 256, SEQ_UNIT),
        out_shape=jax.ShapeDtypeStruct((row_len, 3 * width), bf16),
        in_specs=[pl.BlockSpec(memory_space=pltpu.SMEM)] + [whole] * 4,
        out_specs=whole,
        scratch_shapes=[
            pltpu.VMEM((3 * width, row_len), bf16),
            pltpu.VMEM((width, row_len), bf16),
            pltpu.VMEM((3 * count, row_len, HEAD_DIM), bf16),
            pltpu.VMEM((count, row_len, 8), f32),
            pltpu.VMEM((row_len, width), f32),
            pltpu.VMEM((2 * width, row_len), f32),
        ],
        compiler_params=pltpu.CompilerParams(vmem_limit_bytes=48 * 2**20),
        cost_estimate=pl.CostEstimate(flops=13 * 10**9 * count if which == 0 else 10**6, bytes_accessed=10**5, transcendentals=0),
    )(meta, qkv, upstream, att, lse)


def project_kernel(sets, gain_lane, count, *refs):
    weight_ref, h1_ref, qkv_ref, turned_ref, gain_ref = refs[count:]
    columns = qkv_ref.shape[0]

    @pl.when(pl.program_id(0) == 0)
    def _():
        turned = weight_ref[...].astype(f32).T
        gain_ref[...] = turned[gain_lane : gain_lane + 8]
        turned = turned[:columns]
        for one in sets:
            begin = head_rows(sets, 0, one[0]).start
            end = begin + len(one) * HEAD_DIM
            stop = begin + 3 * len(one) * HEAD_DIM
            turned_ref[begin:end] = (turned[begin:end] * HEAD_DIM**-0.5).astype(bf16)
            turned_ref[end:stop] = turned[end:stop].astype(bf16)

    for i in range(count):

        @pl.when(pl.program_id(0) == i)
        def _(tokens_ref=refs[i]):
            values = tokens_ref[...].astype(f32)
            centered = values - jnp.mean(values, axis=-1, keepdims=True)
            inverse = lax.rsqrt(jnp.mean(centered * centered, axis=-1, keepdims=True) + epsilon)
            h1 = (centered * inverse * gain_ref[0:1]).T.astype(bf16)
            h1_ref[...] = h1
            qkv_ref[...] = jnp.dot(turned_ref[...], h1, preferred_element_type=f32).astype(bf16)


def project(pieces, weight, sets):
    step, model = pieces[0].shape
    count = len(pieces)
    row_len = count * step
    columns = 3 * HEAD_DIM * sum(len(one) for one in sets)
    return pl.pallas_call(
        functools.partial(project_kernel, sets, columns, count),
        grid=(count,),
        out_shape=(jax.ShapeDtypeStruct((model, row_len), bf16), jax.ShapeDtypeStruct((columns, row_len), bf16)),
        in_specs=[pl.BlockSpec((step, model), lambda i: (0, 0))] * count + [pl.BlockSpec(weight.shape, lambda i: (0, 0))],
        out_specs=(pl.BlockSpec((model, step), lambda i: (0, i)), pl.BlockSpec((columns, step), lambda i: (0, i))),
        scratch_shapes=[pltpu.VMEM((columns, model), bf16), pltpu.VMEM((8, model), f32)],
        compiler_params=pltpu.CompilerParams(vmem_limit_bytes=40 * 2**20),
        cost_estimate=pl.CostEstimate(flops=10**6, bytes_accessed=10**5, transcendentals=0),
    )(*pieces, weight)


def rows_kernel(count, strides, more, me_ref, left_ref, right_ref, *refs):
    outs, total_ref = refs[:-1], refs[-1]
    cols = right_ref.shape[1]
    total_ref[:, :cols] = jnp.dot(left_ref[...], right_ref[...], preferred_element_type=f32)
    if more:
        total_ref[:, cols:] = refs[0][...].astype(f32)
        outs = outs[1:]
    outer = strides
    rows = outs[0].shape[-2]
    for r in range(count):
        entry = (me_ref[0] + count - r) % count
        for a in range(outer):
            at = pl.multiple_of((a * count + entry) * rows, 8)
            outs[r][a] = total_ref[pl.ds(at, rows), :].astype(bf16)


def split_product(grid, left, right, dim, more=None):
    rows_all, cols = left.shape[0], right.shape[1]
    operands = [left, right]
    if more is not None:
        operands.append(more)
        cols += more.shape[1]
    outer, count = grid.sizes["hi"], grid.sizes[dim]
    rows = rows_all // (outer * count)
    whole = pl.BlockSpec(memory_space=pltpu.VMEM)
    outs = pl.pallas_call(
        functools.partial(rows_kernel, count, outer, more is not None),
        out_shape=tuple(jax.ShapeDtypeStruct((outer, rows, cols), bf16) for _ in range(count)),
        in_specs=[pl.BlockSpec(memory_space=pltpu.SMEM)] + [whole] * len(operands),
        out_specs=(whole,) * count,
        scratch_shapes=[pltpu.VMEM((rows_all, cols), f32)],
        compiler_params=pltpu.CompilerParams(vmem_limit_bytes=48 * 2**20),
        cost_estimate=pl.CostEstimate(flops=10**6, bytes_accessed=10**5, transcendentals=0),
    )(grid.at[dim].reshape(1).astype(jnp.int32), *operands)
    return outs[0], list(outs[1:])


def back_kernel(bounds, count, *refs):
    parts, weight_ref, outs = refs[:count], refs[count], refs[count + 1 :]
    pieces, rows = outs[0].shape[0], outs[0].shape[1]
    for x in range(pieces):
        for c, out_ref in enumerate(outs):
            here = slice((x * len(outs) + c) * rows, (x * len(outs) + c + 1) * rows)
            total = 0.0
            for i in range(count):
                weight = weight_ref[:, bounds[i] : bounds[i + 1]]
                total = total + lax.dot_general(parts[i][here, :], weight, (((1,), (1,)), ((), ())), preferred_element_type=f32)
            out_ref[x] = total.astype(bf16)


def back_project(grid, parts, weight, bounds):
    nx, nc = grid.sizes["x"], grid.sizes["c"]
    rows = parts[0].shape[0] // (nx * nc)
    whole = pl.BlockSpec(memory_space=pltpu.VMEM)
    return pl.pallas_call(
        functools.partial(back_kernel, bounds, len(parts)),
        out_shape=tuple(jax.ShapeDtypeStruct((nx, rows, weight.shape[0]), bf16) for _ in range(nc)),
        in_specs=[whole] * (len(parts) + 1),
        out_specs=(whole,) * nc,
        compiler_params=pltpu.CompilerParams(vmem_limit_bytes=48 * 2**20),
        cost_estimate=pl.CostEstimate(flops=10**6, bytes_accessed=10**5, transcendentals=0),
    )(*parts, weight)


def hidden_kernel(counts, folds, up_at, down_at, *refs):
    up_refs, down_refs = refs[: counts[0]], refs[counts[0] : counts[0] + counts[1]]
    rest = refs[counts[0] + counts[1] :]
    h2_refs, cot_refs = rest[:2], rest[2:4]
    act_ref, pre_ref, own_ref, sent_ref, up_ref, down_ref, up_sem, down_sem = rest[4:]
    model = up_ref.shape[0]
    rows = up_refs[0].shape[1] // folds
    strip = down_refs[0].shape[1]
    copies, later = [], []
    for ref in up_refs:
        for i in range(ref.shape[0]):
            at = pl.multiple_of(up_at[len(copies) // folds] * rows, rows)
            for f in range(folds):
                piece = ref.at[i, pl.ds(f * rows, rows), :]
                spot = up_ref.at[pl.ds(at, rows), pl.ds(f * model, model)]
                copies.append(pltpu.make_async_copy(piece, spot, up_sem.at[len(copies)]))
    for ref in down_refs:
        for i in range(ref.shape[0]):
            at = pl.multiple_of(down_at[len(later)] * strip, strip)
            later.append(pltpu.make_async_copy(ref.at[i], down_ref.at[pl.ds(at, strip), :], down_sem.at[len(later)]))
    for copy in copies + later:
        copy.start()
    for copy in copies + later:
        copy.wait()
    half = h2_refs[0].shape[0]
    hidden = up_ref.shape[1]
    width = 256
    root = (2.0 / math.pi) ** 0.5

    def first(item):
        i, at = item
        pre = jnp.dot(h2_refs[i][...], up_ref[:, at : at + width], preferred_element_type=f32)
        back = lax.dot_general(cot_refs[i][...], down_ref[at : at + width, :], (((1,), (1,)), ((), ())), preferred_element_type=f32)
        return pre, back

    def second(item, kept):
        i, at = item
        pre, back = kept
        square = pre * pre
        slope = jnp.tanh(pre * (root + root * 0.044715 * square))
        side = 0.5 + 0.5 * slope
        act_ref[i * half : (i + 1) * half, at : at + width] = (pre * side).astype(bf16)
        steep = side + (0.5 * pre) * (1.0 - slope * slope) * (root + 3 * root * 0.044715 * square)
        pre_ref[i * half : (i + 1) * half, at : at + width] = (steep * back).astype(bf16)

    pipeline([(i, at) for i in range(2) for at in range(0, hidden, width)], first, second, lambda item, kept: None)
    for i, ref in enumerate((own_ref, sent_ref)):
        for at in range(0, half, 256):
            left = pre_ref[i * half + at : i * half + at + 256, :]
            total = lax.dot_general(left, up_ref[...], (((1,), (1,)), ((), ())), preferred_element_type=f32)
            ref[at : at + 256, :] = total.astype(ref.dtype)


def hidden_layer(up_stacks, up_at, down_stacks, down_at, h2_pair, cot_pair, folds):
    half, model = h2_pair[0].shape
    up_count, down_count = sum(one.shape[0] for one in up_stacks), sum(one.shape[0] for one in down_stacks)
    hidden = folds * model
    whole, smem, far = (pl.BlockSpec(memory_space=m) for m in (pltpu.VMEM, pltpu.SMEM, pl.ANY))
    return pl.pallas_call(
        functools.partial(hidden_kernel, (len(up_stacks), len(down_stacks)), folds),
        out_shape=(
            jax.ShapeDtypeStruct((2 * half, hidden), bf16),
            jax.ShapeDtypeStruct((2 * half, hidden), bf16),
            jax.ShapeDtypeStruct((half, model), f32),
            jax.ShapeDtypeStruct((half, model), bf16),
        ),
        in_specs=[smem, smem] + [far] * (len(up_stacks) + len(down_stacks)) + [whole] * 4,
        out_specs=(whole,) * 4,
        scratch_shapes=[
            pltpu.VMEM((model, hidden), bf16),
            pltpu.VMEM((hidden, model), bf16),
            pltpu.SemaphoreType.DMA((up_count * folds,)),
            pltpu.SemaphoreType.DMA((down_count,)),
        ],
        compiler_params=pltpu.CompilerParams(vmem_limit_bytes=50 * 2**20),
        cost_estimate=pl.CostEstimate(flops=14 * 10**9, bytes_accessed=10**6, transcendentals=0),
    )(up_at, down_at, *up_stacks, *down_stacks, *h2_pair, *cot_pair)


def norm_parts(values):
    centered = values - jnp.mean(values, axis=-1, keepdims=True)
    inverse = lax.rsqrt(jnp.mean(centered * centered, axis=-1, keepdims=True) + epsilon)
    return centered * inverse, inverse


def norm_back(normed, inverse, gain, grad):
    c = grad * gain
    return (c - jnp.mean(c, axis=-1, keepdims=True) - normed * jnp.mean(c * normed, axis=-1, keepdims=True)) * inverse


def mm(a, b, dims):
    return lax.dot_general(a, b, ((dims[:1], dims[1:]), ((), ())), preferred_element_type=f32)


def body(
    tokens,
    lengths,
    block_place,
    qkv_weight,
    out_weight,
    up_weight,
    down_weight,
    attn_gain,
    mlp_gain,
    cotangent,
):
    nb, nk = lax.axis_size("pb"), lax.axis_size("ka")
    grid = Grid(nb, nk)
    nx, nc = grid.sizes["x"], grid.sizes["c"]
    x_at, c_at = grid.at["x"], grid.at["c"]
    tok_rows, model = tokens.shape
    shard = qkv_weight.shape[0]
    chips = nb * nx
    heads = -(-HEADS // nk)
    width = heads * HEAD_DIM
    lanes = -(-(3 * width + 2) // BLK) * BLK
    rels = [(xr, cr) for xr in range(nx) for cr in range(nc)]

    def ka_of(xr, cr):
        return ((x_at + xr) % nx) * nc + (c_at + cr) % nc

    def exchange(parts):
        got = [parts(grid.ka)]
        for xr, cr in rels[1:]:
            got.append(grid.fetch(parts(ka_of(-xr, -cr)), x=xr, c=cr))
        return got

    cut = max(1, heads - 1)
    sets = [tuple(range(cut)), tuple(range(cut, heads))] if heads > 1 else [(0,)]
    bounds = [0]
    for one in sets:
        bounds.append(bounds[-1] + 3 * len(one) * HEAD_DIM)

    def head_groups(weight):
        split = weight.reshape(weight.shape[0], 3, HEADS, HEAD_DIM)
        if heads * nk != HEADS:
            split = jnp.pad(split, ((0, 0), (0, 0), (0, heads * nk - HEADS), (0, 0)))
        split = split.reshape(-1, 3, nk, heads, HEAD_DIM)
        chosen = [split[:, :, :, one[0] : one[-1] + 1].transpose(2, 0, 1, 3, 4).reshape(nk, weight.shape[0], -1) for one in sets]
        return jnp.concatenate(chosen, axis=2)

    gains = jnp.stack([attn_gain, mlp_gain], axis=1)
    gains = jnp.pad(gains, ((0, 0), (0, lanes - 3 * width - 2)))
    own_qkv = jnp.concatenate([head_groups(qkv_weight), jnp.broadcast_to(gains[None], (nk,) + gains.shape)], axis=2)
    got = exchange(lambda ka: lax.dynamic_index_in_dim(own_qkv, ka, 0, keepdims=False))
    group_qkv = jnp.concatenate(grid.group_in_order(got), axis=0)

    first_tokens = tie(tokens, *got)
    by_x = [tokens] + [grid.fetch(first_tokens, x=r) for r in range(1, nx)]
    strip = down_weight.shape[0]
    up_split = jnp.transpose(up_weight.reshape(shard, chips, nc, strip), (2, 0, 1, 3)).reshape(nc, shard, chips * strip)
    own, sends = grid.split(up_split, 0, "c")
    up_part = jnp.concatenate(grid.in_order([own] + grid.send(sends, "c"), "c"), axis=0)
    folds = chips * strip // model
    up_part = jnp.concatenate([up_part[:, i * model : (i + 1) * model] for i in range(folds)], axis=0)
    both = jnp.concatenate([up_part, down_weight], axis=0)
    group_qkv, both = together(group_qkv, both)
    got_hi = [grid.fetch(group_qkv[None], hi=r) for r in range(1, grid.sizes["hi"])]
    stack = tie(jnp.stack(by_x), *got_hi)
    from_c = [grid.fetch(stack, c=r) for r in range(1, nc)]
    by_c = [by_x] + [list(one) for one in from_c]
    row_tokens = [by_c[c][x] for x in range(nx) for c in range(nc)]
    qkv_stack = jnp.concatenate([group_qkv[None]] + got_hi, axis=0)
    full_qkv, _ = gather_rows(grid, None, ("lo",), {"place": row_tokens}, qkv_stack)

    full_out = lax.all_gather(tie(out_weight, *got_hi), ("pb", "ka"), axis=0, tiled=True)

    both = tie(both, qkv_stack, *from_c)
    both = grid.gather(both, "hi")

    slots = tok_rows // BLK
    holder = jnp.argsort(block_place[0]).astype(jnp.int32)
    holder_ka, holder_slot = holder // slots, holder % slots
    rel = ((holder_ka // nc - x_at) % nx) * nc + (holder_ka % nc - c_at) % nc
    meta = jnp.concatenate([rel * slots + holder_slot, lengths[0, :1]]).astype(jnp.int32)

    gain_one = full_qkv[:, 3 * width].astype(f32)
    gain_two = full_qkv[:, 3 * width + 1].astype(f32)
    inputs = tokens.astype(f32)
    h1, qkv = project(row_tokens, full_qkv, sets)
    row_len = h1.shape[1]
    up_rows = up_part.shape[0]
    up_stack, down_stack, _ = together(both[:, :up_rows], both[:, up_rows:], qkv)
    qkv = tie(qkv, up_stack, down_stack)
    up_stack = [up_stack] + [grid.fetch(up_stack, x=r) for r in range(1, nx)]
    down_stack = [down_stack] + [grid.fetch(down_stack, lo=r) for r in range(1, grid.sizes["lo"])]
    att_parts, att_row, lse = forward_attention(meta, qkv, sets, nk)
    att_parts, up_stack, down_stack = together(att_parts, up_stack, down_stack)
    up_stack, down_stack = jnp.concatenate(up_stack, axis=0), jnp.concatenate(down_stack, axis=0)
    up_stacks, up_at = gather_rows(grid, None, ("lo",), begun=up_stack, done=("hi", "x"), raw=True)
    down_stacks, down_at = gather_rows(grid, None, ("x",), begun=down_stack, done=("hi", "lo"), raw=True)
    got = [att_parts[0]]
    for xr, cr in rels[1:]:
        got.append(grid.fetch(att_parts[((-xr) % nx) * nc + (-cr) % nc], x=xr, c=cr))
    att = jnp.concatenate(grid.group_in_order(got), axis=0)[: HEADS * HEAD_DIM]

    late_cot = tie(cotangent, att_parts)
    cot_pair = [cotangent] + [grid.fetch(late_cot, c=r) for r in range(1, nc)]
    cots = jnp.concatenate(cot_pair, axis=0)
    att = tie(att, up_stack, down_stack)
    residual = inputs + mm(att, full_out, (0, 0))
    normed_two, inverse_two = norm_parts(residual)
    h2 = (normed_two * gain_two).astype(bf16)
    h2_pair = [h2] + [grid.fetch(h2, c=r) for r in range(1, nc)]
    h2s = jnp.concatenate(h2_pair, axis=0)

    def core_sum(part):
        pieces = part.reshape((nc, tok_rows) + part.shape[1:])
        total = pieces[0]
        for r in range(1, nc):
            total = total + grid.fetch(pieces[(nc - r) % nc].astype(bf16), c=r).astype(f32)
        return total

    if nc == 2 and strip % 16 == 0 and (nc * shard) % 16 == 0 and tok_rows % 256 == 0:
        hidden_low, grad_pre, grad_h2, grad_sent = hidden_layer(up_stacks, up_at, down_stacks, down_at, h2_pair, cot_pair, folds)
        grad_h2 = added(grad_h2, [grid.fetch(grad_sent, c=1)], True)
    else:
        full_up = put_in_place(up_stacks, up_at).reshape(chips, folds, nc * shard, model)
        full_up = jnp.transpose(full_up, (0, 2, 1, 3)).reshape(model, folds * model)
        hidden_act, gelu_back = jax.vjp(lambda v: jax.nn.gelu(v, approximate=True), mm(h2s, full_up, (1, 0)))
        hidden_low = hidden_act.astype(bf16)
        (grad_pre,) = gelu_back(mm(cots, put_in_place(down_stacks, down_at), (1, 1)))
        grad_pre = grad_pre.astype(bf16)
        grad_h2 = core_sum(mm(grad_pre, full_up, (1, 1)))
    grad_up = mm(h2s, grad_pre, (0, 0)).astype(bf16)
    grad_residual = cotangent.astype(f32) + norm_back(normed_two, inverse_two, gain_two, grad_h2)
    grad_res_low = grad_residual.astype(bf16)
    grad_att = mm(full_out, grad_res_low, (1, 1)).astype(bf16)
    if heads * nk != HEADS:
        grad_att = jnp.pad(grad_att, ((0, (heads * nk - HEADS) * HEAD_DIM), (0, 0)))
    grad_att = grad_att.reshape(nk, width, tok_rows)
    upstream = jnp.stack(exchange(lambda ka: lax.dynamic_index_in_dim(grad_att, ka, 0, keepdims=False)))
    late_low, late_res, _ = together(hidden_low, grad_res_low, grad_att)
    grad_down = mm(late_low, cots, (0, 0)).astype(bf16)
    grad_out = mm(att, late_res, (1, 0)).astype(bf16)

    n = grid.sizes

    def placed(grad):
        return grad.reshape(n["hi"], n["lo"], n["x"], -1, grad.shape[1])

    up_own, up_send = grid.split(placed(grad_up), 1, "lo")
    up_got = grid.send(up_send, "lo")
    down_own, down_send = grid.split(placed(grad_down), 2, "x")
    out_own, out_send = grid.split(grad_out.reshape(model, nc, model // nc), 1, "c")
    out_sum = added(out_own, grid.send(out_send, "c"))
    upstream, out_sum, down_send = together(upstream, out_sum, down_send)
    out_own, out_send = grid.split(out_sum.reshape(model, nx, model // nk), 1, "x")
    out_got = grid.send(out_send, "x")
    down_got = grid.send(down_send, "x")

    parts, qkv_rest, qkv_got = [], [], []
    last = len(sets) - 1
    for which in range(len(sets)):
        part = backward_attention(meta, qkv, upstream, att_row, lse, sets, which)
        if which == last:
            part, qkv_got, up_got = together(part, qkv_got, up_got)
        if which == 0:
            part, up_got, out_got = together(part, up_got, out_got)
            out_sum = added(out_own, out_got)
        parts.append(part)
        own, sends = split_product(grid, h1, part, "lo", out_sum if which == 0 else None)
        qkv_rest.append(own)
        qkv_got.append(grid.send(sends, "lo"))
        if which == 0:
            up_own, up_send = grid.halve(added(up_own, up_got), "hi", 0)
            up_got = [grid.swap(up_send, "hi", 0)]
            upstream, down_got, *_ = together(upstream, down_got, up_send, *sends)

    up_own, up_send = grid.halve(added(up_own, up_got), "hi", 1)
    down_own, down_send = grid.split(added(down_own, down_got), 1, "lo")
    up_got = [grid.swap(up_send, "hi", 1)]
    down_got = grid.send(down_send, "lo")
    late_part, *_ = together(parts[-1], *sends)
    grad_h1 = back_project(grid, parts[:-1] + [late_part], full_qkv, bounds)
    h1_got = grid.send([grad_h1[(nc - r) % nc] for r in range(1, nc)], "c")

    qkv_got, h1_got = together(qkv_got, h1_got)
    sums = [added(own, got) for own, got in zip(qkv_rest, qkv_got)]
    by_kind = []
    for kind in range(3):
        for i, one in enumerate(sets):
            begin = kind * len(one) * HEAD_DIM
            by_kind.append(sums[i][:, :, begin : begin + len(one) * HEAD_DIM])
    by_kind.append(sums[0][:, :, 3 * len(sets[0]) * HEAD_DIM :])
    qkv_own, qkv_send = grid.halve(jnp.concatenate(by_kind, axis=2), "hi", 0)
    qkv_got = [grid.swap(qkv_send, "hi", 0)]
    h1_own = added(grad_h1[0], h1_got)
    h1_got = grid.send([h1_own[(nx - r) % nx] for r in range(1, nx)], "x")

    qkv_got, up_got, down_got = together(qkv_got, up_got, down_got)
    qkv_own, qkv_send = grid.halve(added(qkv_own, qkv_got), "hi", 1)
    qkv_got = [grid.swap(qkv_send, "hi", 1)]
    up_own, up_send = grid.split(added(up_own, up_got)[0], 0, "x")
    up_got = grid.send(up_send, "x")
    down_own, down_send = grid.halve(added(down_own, down_got), "hi", 0)
    down_got = [grid.swap(down_send, "hi", 0)]

    low, stacks, _ = together(hidden_low, down_stacks, qkv_send)
    mixed = mm(low, put_in_place(stacks, down_at), (1, 0)).reshape(nc, tok_rows, model)
    mixed_got = [grid.fetch(mixed[(nc - r) % nc].astype(bf16), c=r) for r in range(1, nc)]
    mixed = (residual + added(mixed[0], mixed_got, True)).astype(bf16)

    qkv_got, h1_got, up_got, down_got = together(qkv_got, h1_got, up_got, down_got)
    group_grad = added(qkv_own, qkv_got, True).reshape(nx, nc, shard, -1)
    group_own, group_send = grid.split(group_grad, 0, "x")
    group_got = grid.send(group_send, "x")
    up_own, up_send = grid.split(added(up_own, up_got, True).reshape(nc, shard, -1), 0, "c")
    up_got = grid.send(up_send, "c")
    down_own, down_send = grid.halve(added(down_own, down_got), "hi", 1)
    down_got = [grid.swap(down_send, "hi", 1)]

    group_got, up_got = together(group_got, up_got)
    by_x = grid.in_order([group_own] + group_got, "x")
    group_own, group_send = grid.split(jnp.stack(by_x), 1, "c")
    by_c = grid.in_order([group_own] + grid.send(group_send, "c"), "c")
    got = [by_c[c][x] for x in range(nx) for c in range(nc)]
    sum_up = grid.in_order([up_own] + up_got, "c")

    sum_out = jnp.concatenate([got[x * nc + c][:, 3 * width :] for c in range(nc) for x in range(nx)], axis=1)
    kept = min(nk * width, HEADS * HEAD_DIM)
    sum_qkv = []
    for kind in range(3):
        for i, one in enumerate(got):
            size = min(width, kept - i * width)
            if size > 0:
                sum_qkv.append(one[:, kind * width : kind * width + size])
    sum_qkv = jnp.concatenate(sum_qkv, axis=1)
    sum_up = jnp.stack([one.reshape(shard, chips, strip) for one in sum_up], axis=2).reshape(shard, -1)
    sum_down = added(down_own, down_got, True)[0]
    normed_one, inverse_one = norm_parts(inputs)
    tokens_grad = added(h1_own[0], h1_got, True)
    tokens_grad = (grad_residual + norm_back(normed_one, inverse_one, gain_one, tokens_grad)).astype(bf16)

    grad_gain_one = jnp.sum(sum_qkv * qkv_weight.astype(f32), axis=1) / attn_gain.astype(f32)
    grad_gain_two = jnp.sum(sum_up * up_weight.astype(f32), axis=1) / mlp_gain.astype(f32)
    return (mixed, tokens_grad, sum_qkv, sum_out, sum_up, sum_down, grad_gain_one, grad_gain_two)


def solution(mesh):
    rows = P(("pb", "ka"), None)
    flat = P(("pb", "ka"))
    group = P("pb", None)
    return jax.shard_map(
        body,
        mesh=mesh,
        in_specs=(rows, group, group, rows, rows, rows, rows, flat, flat, rows),
        out_specs=(rows, rows, rows, rows, rows, rows, flat, flat),
        check_vma=False,
    )
```

```python
import functools
import math

import jax
import jax.numpy as jnp
from jax import lax
from jax.experimental import pallas as pl
from jax.experimental.pallas import tpu as pltpu
from jax.sharding import PartitionSpec as P

HEADS = 12
HEAD_DIM = 64
BLK = 128
SEQ_UNIT = 1024
epsilon = 1e-05
f32 = jnp.float32
bf16 = jnp.bfloat16


class Grid:
    def __init__(self, nb, nk):
        nhi = math.gcd(4, nb)
        nc = math.gcd(2, nk)
        self.sizes = {"hi": nhi, "lo": nb // nhi, "x": nk // nc, "c": nc}
        self.nb, self.nk = nb, nk
        pb, ka = lax.axis_index("pb"), lax.axis_index("ka")
        self.pb, self.ka = pb, ka
        self.at = {"hi": pb // self.sizes["lo"], "lo": pb % self.sizes["lo"], "x": ka // nc, "c": ka % nc}

    def fetch(self, value, flip=0, **steps):
        n = self.sizes
        pairs = []
        for hi in range(n["hi"]):
            for lo in range(n["lo"]):
                for x in range(n["x"]):
                    for c in range(n["c"]):
                        here = {"hi": hi, "lo": lo, "x": x, "c": c}
                        there = {d: here[d] ^ steps[d] if flip and d in steps else (here[d] + steps.get(d, 0)) % n[d] for d in here}
                        flat = [((p["hi"] * n["lo"] + p["lo"]) * n["x"] + p["x"]) * n["c"] + p["c"] for p in (there, here)]
                        pairs.append(tuple(flat))
        return lax.ppermute(value, ("pb", "ka"), pairs)

    def gather(self, value, dim):
        return jnp.stack([value] + [self.fetch(value, **{dim: r}) for r in range(1, self.sizes[dim])])

    def in_order(self, pieces, dim):
        n, me = self.sizes[dim], self.at[dim]
        if n == 1:
            return pieces
        if n == 2:
            return [jnp.where(me == 0, pieces[0], pieces[1]), jnp.where(me == 0, pieces[1], pieces[0])]
        stacked = jnp.stack(pieces)
        return [lax.dynamic_index_in_dim(stacked, (i - me) % n, 0, keepdims=False) for i in range(n)]

    def group_in_order(self, pieces):
        nx, nc = self.sizes["x"], self.sizes["c"]
        by_x = [self.in_order(pieces[i * nc : (i + 1) * nc], "c") for i in range(nx)]
        by_c = [self.in_order([row[c] for row in by_x], "x") for c in range(nc)]
        return [by_c[c][x] for x in range(nx) for c in range(nc)]

    def split(self, parts, axis, dim):
        n, me = self.sizes[dim], self.at[dim]
        own = lax.dynamic_index_in_dim(parts, me, axis, keepdims=False)
        return own, [lax.dynamic_index_in_dim(parts, (me - r) % n, axis, keepdims=False) for r in range(1, n)]

    def halve(self, parts, dim, bit):
        mine = (self.at[dim] >> bit) % 2
        parts = parts.reshape((-1, 2) + parts.shape[1:])
        kept = lax.dynamic_index_in_dim(parts, mine, 1, keepdims=False)
        return kept, lax.dynamic_index_in_dim(parts, 1 - mine, 1, keepdims=False)

    def swap(self, value, dim, bit):
        return self.fetch(value, 1, **{dim: 1 << bit})

    def send(self, sends, dim):
        return [self.fetch(sent, **{dim: r + 1}) for r, sent in enumerate(sends)]


def added(own, received, last=False):
    total = own.astype(f32)
    for one in received:
        total = total + one.astype(f32)
    return total if last else total.astype(own.dtype)


def together(*values):
    return lax.optimization_barrier(values)


def place_kernel(counts, rows, offs_ref, *refs):
    ins, out_ref, sems = refs[: len(counts)], refs[len(counts)], refs[len(counts) + 1]
    copies = []
    for ref, count in zip(ins, counts):
        for i in range(count):
            at = pl.multiple_of(offs_ref[len(copies)], rows)
            copies.append(pltpu.make_async_copy(ref.at[i], out_ref.at[pl.ds(at, rows), :], sems.at[len(copies)]))
    for copy in copies:
        copy.start()
    for copy in copies:
        copy.wait()


def place(stacks, offsets):
    rows, cols = stacks[0].shape[1:]
    counts = [s.shape[0] for s in stacks]
    total = sum(counts)
    return pl.pallas_call(
        functools.partial(place_kernel, counts, rows),
        out_shape=jax.ShapeDtypeStruct((total * rows, cols), stacks[0].dtype),
        in_specs=[pl.BlockSpec(memory_space=pltpu.SMEM)] + [pl.BlockSpec(memory_space=pl.ANY)] * len(stacks),
        out_specs=pl.BlockSpec(memory_space=pltpu.VMEM),
        scratch_shapes=[pltpu.SemaphoreType.DMA((total,))],
        compiler_params=pltpu.CompilerParams(vmem_limit_bytes=16 * 2**20),
        cost_estimate=pl.CostEstimate(flops=10**6, bytes_accessed=10**5, transcendentals=0),
    )(offsets.astype(jnp.int32), *stacks)


def tie(value, *before):
    return lax.optimization_barrier((value,) + before)[0]


def put_in_place(stacks, index):
    rows = stacks[0].shape[1]
    if rows % 16 == 0:
        return place(stacks, index * rows)
    order = jnp.argsort(index)
    out = jnp.concatenate(stacks, axis=0)
    return jnp.concatenate([lax.dynamic_index_in_dim(out, order[i], 0, keepdims=False) for i in range(index.shape[0])], axis=0)


def gather_rows(grid, piece, order, gates=None, begun=None, done=("hi",), raw=False):
    if begun is None:
        stack, steps = piece[None], [dict()]
    else:
        stack, steps = begun, [dict()]
        for dim in done:
            steps = steps + [{**s, dim: r} for r in range(1, grid.sizes[dim]) for s in steps]
        piece = stack[0]
    stacks = []
    received = {}
    for dim in order:
        if gates and dim in gates:
            stack = tie(stack, *gates[dim])
        got = [grid.fetch(stack, **{dim: r}) for r in range(1, grid.sizes[dim])]
        received[dim] = got
        steps = steps + [{**s, dim: r} for r in range(1, grid.sizes[dim]) for s in steps]
        if dim == order[-1]:
            stacks = [stack] + got
        else:
            stack = jnp.concatenate([stack] + got, axis=0)
    dims = [d for d in ("hi", "lo", "x") if d in order or (begun is not None and d in done)]
    rows = piece.shape[0]
    index = []
    for s in steps:
        at = 0
        for d in dims:
            at = at * grid.sizes[d] + (grid.at[d] + s.get(d, 0)) % grid.sizes[d]
        index.append(at)
    index = jnp.stack(index).astype(jnp.int32)
    if begun is not None and len(order) == 1 and raw:
        return stacks, index
    if gates and "place" in gates:
        stacks, _ = together(stacks, gates["place"])
    return put_in_place(stacks, index), received


def lane_tile(at, size):
    return pl.ds(pl.multiple_of(at, BLK), size)


def head_rows(sets, kind, head):
    at = 0
    for one in sets:
        if head in one:
            return slice(at + (kind * len(one) + one.index(head)) * HEAD_DIM, at + (kind * len(one) + one.index(head) + 1) * HEAD_DIM)
        at += 3 * len(one) * HEAD_DIM


def pipeline(work, first, second, third):
    held = {}
    for t in range(len(work) + 2):
        if t < len(work):
            held[t] = first(work[t])
        if 1 <= t <= len(work):
            held[t - 1] = second(work[t - 1], held[t - 1])
        if t >= 2:
            third(work[t - 2], held.pop(t - 2))


def spans_to(begin, end, chunk):
    spans = []
    while begin < end:
        size = min(chunk, end - begin)
        spans.append((begin, size, begin + size == end))
        begin += size
    return spans


def forward_kernel(sets, tile, chunk, unit, meta_ref, qkv_ref, out_ref, att_ref, lse_ref, sorted_ref, keys_ref):
    heads = sum(len(one) for one in sets)
    row_len = qkv_ref.shape[1]
    blocks = row_len // BLK
    per_device = out_ref.shape[2] // BLK
    for b in range(blocks):
        sorted_ref[:, b * BLK : (b + 1) * BLK] = qkv_ref[:, lane_tile(meta_ref[b] * BLK, BLK)]
    for h in range(heads):
        keys_ref[h] = sorted_ref[head_rows(sets, 1, h), :].astype(f32).T.astype(bf16)
    doc_units = jnp.maximum(meta_ref[blocks] // unit, 1)
    seen = lax.broadcasted_iota(jnp.int32, (tile, tile), 0) <= lax.broadcasted_iota(jnp.int32, (tile, tile), 1)
    lse_ref[...] = jnp.zeros_like(lse_ref)
    for i in range(row_len // tile):
        lanes = slice(i * tile, (i + 1) * tile)
        queries = [sorted_ref[head_rows(sets, 0, h), lanes] for h in range(heads)]

        def run(spans, carry):
            carry = list(carry)

            def first(item):
                h, begin, size, _ = item
                return jnp.dot(keys_ref[h, pl.ds(begin, size), :], queries[h], preferred_element_type=f32)

            def second(item, scores):
                h, _, size, diagonal = item
                peak, total, acc = carry[h]
                square = scores * scores + 1.0
                inverse = lax.rsqrt(square)
                reach = square * inverse
                if diagonal:
                    low = jnp.where(seen, reach[size - tile :], -1e30)
                    reach = low if size == tile else jnp.concatenate([reach[: size - tile], low], axis=0)
                top = jnp.maximum(peak, jnp.max(reach, axis=0, keepdims=True))
                shares = jnp.exp(reach - top)
                fade = jnp.exp(peak - top)
                total = total * fade + jnp.sum(shares, axis=0, keepdims=True)
                carry[h] = (top, total, acc)
                return (shares * (scores * inverse)).astype(bf16), fade

            def third(item, kept):
                h, begin, size, _ = item
                mixing, fade = kept
                top, total, acc = carry[h]
                values = sorted_ref[head_rows(sets, 2, h), pl.ds(begin, size)]
                carry[h] = (top, total, acc * fade + jnp.dot(values, mixing, preferred_element_type=f32))

            pipeline([(h,) + span for span in spans for h in range(heads)], first, second, third)
            return tuple(carry)

        here = i * tile // unit
        start = (jnp.ones((1, tile), f32), jnp.zeros((1, tile), f32), jnp.zeros((HEAD_DIM, tile), f32))
        carry = run(spans_to(here * unit, (i + 1) * tile, chunk), (start,) * heads)
        if here > 0:

            def earlier(k, carry):
                base = pl.multiple_of(k * unit, unit)
                return run([(base + o, chunk, False) for o in range(0, unit, chunk)], carry)

            carry = lax.fori_loop(here // doc_units * doc_units, here, earlier, carry)
        for h in range(heads):
            peak, total, acc = carry[h]
            rows = slice(h * HEAD_DIM, (h + 1) * HEAD_DIM)
            result = acc / total
            att_ref[rows, lanes] = result
            lse_ref[h : h + 1, lanes] = peak + jnp.log(total)
            low = result.astype(bf16)
            for part in range(tile // BLK):
                spot = meta_ref[i * (tile // BLK) + part]
                out_ref[spot // per_device, rows, lane_tile((spot % per_device) * BLK, BLK)] = low[:, part * BLK : (part + 1) * BLK]


def forward_attention(meta, qkv, sets, devices):
    row_len = qkv.shape[1]
    heads = sum(len(one) for one in sets)
    width = heads * HEAD_DIM
    whole = pl.BlockSpec(memory_space=pltpu.VMEM)
    return pl.pallas_call(
        functools.partial(forward_kernel, sets, 256, 512, SEQ_UNIT),
        out_shape=(
            jax.ShapeDtypeStruct((devices, width, row_len // devices), bf16),
            jax.ShapeDtypeStruct((width, row_len), f32),
            jax.ShapeDtypeStruct((8, row_len), f32),
        ),
        in_specs=[pl.BlockSpec(memory_space=pltpu.SMEM), whole],
        out_specs=(whole, whole, whole),
        scratch_shapes=[pltpu.VMEM((3 * width, row_len), bf16), pltpu.VMEM((heads, row_len, HEAD_DIM), bf16)],
        compiler_params=pltpu.CompilerParams(vmem_limit_bytes=40 * 2**20),
        cost_estimate=pl.CostEstimate(flops=7 * 10**9 * heads, bytes_accessed=10**6, transcendentals=0),
    )(meta, qkv)


def backward_kernel(
    sets, which, tile, chunk, unit, meta_ref, qkv_ref, up_ref, att_ref, lse_ref, grad_ref, sorted_ref, ups_ref, nat_ref, stat_ref, dq_ref, dkv_ref
):
    heads = sets[which]
    count = len(heads)
    row_len = qkv_ref.shape[1]
    width = count * HEAD_DIM
    blocks = row_len // BLK
    per_device = up_ref.shape[2] // BLK
    base_row = head_rows(sets, 0, heads[0]).start
    ups_rows = slice(heads[0] * HEAD_DIM, (heads[-1] + 1) * HEAD_DIM)
    for b in range(blocks):
        spot = slice(b * BLK, (b + 1) * BLK)
        sorted_ref[:, spot] = qkv_ref[base_row : base_row + 3 * width, lane_tile(meta_ref[b] * BLK, BLK)]
        ups_ref[:, spot] = up_ref[meta_ref[b] // per_device, ups_rows, lane_tile((meta_ref[b] % per_device) * BLK, BLK)]
    own = [slice(h * HEAD_DIM, (h + 1) * HEAD_DIM) for h in range(3 * count)]
    for h in range(count):
        for part in range(2):
            nat_ref[part * count + h] = sorted_ref[own[part * count + h], :].astype(f32).T.astype(bf16)
        upstream = ups_ref[own[h], :].astype(f32)
        nat_ref[2 * count + h] = upstream.T.astype(bf16)
        att = att_ref[heads[h] * HEAD_DIM : (heads[h] + 1) * HEAD_DIM, :]
        delta = jnp.sum(upstream * att, axis=0, keepdims=True)
        stats = [lse_ref[heads[h] : heads[h] + 1, :], delta, jnp.zeros((6, row_len), f32)]
        stat_ref[h] = jnp.concatenate(stats, axis=0).T
    dkv_ref[...] = jnp.zeros_like(dkv_ref)
    doc_units = jnp.maximum(meta_ref[blocks] // unit, 1)
    seen = lax.broadcasted_iota(jnp.int32, (tile, tile), 0) >= lax.broadcasted_iota(jnp.int32, (tile, tile), 1)
    for i in range(row_len // tile):
        at = slice(i * tile, (i + 1) * tile)

        def run(spans, carry):
            carry = list(carry)

            def first(item):
                h, begin, size, _ = item
                lanes = pl.ds(begin, size)
                scores = jnp.dot(nat_ref[h, at, :], sorted_ref[own[count + h], lanes], preferred_element_type=f32)
                effect = jnp.dot(nat_ref[2 * count + h, at, :], sorted_ref[own[2 * count + h], lanes], preferred_element_type=f32)
                return scores, effect

            def second(item, kept):
                h, _, size, diagonal = item
                scores, effect = kept
                square = scores * scores + 1.0
                inverse = lax.rsqrt(square)
                shares = jnp.exp(square * inverse - stat_ref[h, at, 0:1])
                if diagonal:
                    low = jnp.where(seen, shares[:, size - tile :], 0.0)
                    shares = low if size == tile else jnp.concatenate([shares[:, : size - tile], low], axis=1)
                sign = scores * inverse
                twice = inverse * inverse
                grad = shares * (effect * (1.0 - twice + twice * inverse) - stat_ref[h, at, 1:2] * sign)
                return grad.astype(bf16), (shares * sign).astype(bf16)

            def third(item, kept):
                h, begin, size, _ = item
                grad, mixing = kept
                lanes = pl.ds(begin, size)
                carry[h] = carry[h] + jnp.dot(grad, nat_ref[count + h, pl.ds(begin, size), :], preferred_element_type=f32)
                dkv_ref[own[h], lanes] += jnp.dot(sorted_ref[own[h], at], grad, preferred_element_type=f32)
                dkv_ref[own[count + h], lanes] += jnp.dot(ups_ref[own[h], at], mixing, preferred_element_type=f32)

            pipeline([(h,) + span for span in spans for h in range(count)], first, second, third)
            return tuple(carry)

        here = i * tile // unit
        carry = run(spans_to(here * unit, (i + 1) * tile, chunk), (jnp.zeros((tile, HEAD_DIM), f32),) * count)
        if here > 0:

            def earlier(k, carry):
                base = pl.multiple_of(k * unit, unit)
                return run([(base + o, chunk, False) for o in range(0, unit, chunk)], carry)

            carry = lax.fori_loop(here // doc_units * doc_units, here, earlier, carry)
        dq_ref[at, :] = carry[0] if count == 1 else jnp.concatenate(carry, axis=1)
    scale = HEAD_DIM**-0.5
    for b in range(blocks):
        here = slice(b * BLK, (b + 1) * BLK)
        both = jnp.concatenate([dq_ref[here, :] * scale, dkv_ref[:, here].T], axis=1)
        grad_ref[pl.ds(pl.multiple_of(meta_ref[b] * BLK, BLK), BLK), :] = both.astype(bf16)


def backward_attention(meta, qkv, upstream, att, lse, sets, which):
    row_len = qkv.shape[1]
    count = len(sets[which])
    width = count * HEAD_DIM
    whole = pl.BlockSpec(memory_space=pltpu.VMEM)
    return pl.pallas_call(
        functools.partial(backward_kernel, sets, which, 256, 256, SEQ_UNIT),
        out_shape=jax.ShapeDtypeStruct((row_len, 3 * width), bf16),
        in_specs=[pl.BlockSpec(memory_space=pltpu.SMEM)] + [whole] * 4,
        out_specs=whole,
        scratch_shapes=[
            pltpu.VMEM((3 * width, row_len), bf16),
            pltpu.VMEM((width, row_len), bf16),
            pltpu.VMEM((3 * count, row_len, HEAD_DIM), bf16),
            pltpu.VMEM((count, row_len, 8), f32),
            pltpu.VMEM((row_len, width), f32),
            pltpu.VMEM((2 * width, row_len), f32),
        ],
        compiler_params=pltpu.CompilerParams(vmem_limit_bytes=48 * 2**20),
        cost_estimate=pl.CostEstimate(flops=13 * 10**9 * count if which == 0 else 10**6, bytes_accessed=10**5, transcendentals=0),
    )(meta, qkv, upstream, att, lse)


def project_kernel(sets, gain_lane, count, *refs):
    weight_ref, h1_ref, qkv_ref, turned_ref, gain_ref = refs[count:]
    columns = qkv_ref.shape[0]

    @pl.when(pl.program_id(0) == 0)
    def _():
        turned = weight_ref[...].astype(f32).T
        gain_ref[...] = turned[gain_lane : gain_lane + 8]
        turned = turned[:columns]
        for one in sets:
            begin = head_rows(sets, 0, one[0]).start
            end = begin + len(one) * HEAD_DIM
            stop = begin + 3 * len(one) * HEAD_DIM
            turned_ref[begin:end] = (turned[begin:end] * HEAD_DIM**-0.5).astype(bf16)
            turned_ref[end:stop] = turned[end:stop].astype(bf16)

    for i in range(count):

        @pl.when(pl.program_id(0) == i)
        def _(tokens_ref=refs[i]):
            values = tokens_ref[...].astype(f32)
            centered = values - jnp.mean(values, axis=-1, keepdims=True)
            inverse = lax.rsqrt(jnp.mean(centered * centered, axis=-1, keepdims=True) + epsilon)
            h1 = (centered * inverse * gain_ref[0:1]).T.astype(bf16)
            h1_ref[...] = h1
            qkv_ref[...] = jnp.dot(turned_ref[...], h1, preferred_element_type=f32).astype(bf16)


def project(pieces, weight, sets):
    step, model = pieces[0].shape
    count = len(pieces)
    row_len = count * step
    columns = 3 * HEAD_DIM * sum(len(one) for one in sets)
    return pl.pallas_call(
        functools.partial(project_kernel, sets, columns, count),
        grid=(count,),
        out_shape=(jax.ShapeDtypeStruct((model, row_len), bf16), jax.ShapeDtypeStruct((columns, row_len), bf16)),
        in_specs=[pl.BlockSpec((step, model), lambda i: (0, 0))] * count + [pl.BlockSpec(weight.shape, lambda i: (0, 0))],
        out_specs=(pl.BlockSpec((model, step), lambda i: (0, i)), pl.BlockSpec((columns, step), lambda i: (0, i))),
        scratch_shapes=[pltpu.VMEM((columns, model), bf16), pltpu.VMEM((8, model), f32)],
        compiler_params=pltpu.CompilerParams(vmem_limit_bytes=40 * 2**20),
        cost_estimate=pl.CostEstimate(flops=10**6, bytes_accessed=10**5, transcendentals=0),
    )(*pieces, weight)


def rows_kernel(count, strides, more, me_ref, left_ref, right_ref, *refs):
    outs, total_ref = refs[:-1], refs[-1]
    cols = right_ref.shape[1]
    total_ref[:, :cols] = jnp.dot(left_ref[...], right_ref[...], preferred_element_type=f32)
    if more:
        total_ref[:, cols:] = refs[0][...].astype(f32)
        outs = outs[1:]
    outer = strides
    rows = outs[0].shape[-2]
    for r in range(count):
        entry = (me_ref[0] + count - r) % count
        for a in range(outer):
            at = pl.multiple_of((a * count + entry) * rows, 8)
            outs[r][a] = total_ref[pl.ds(at, rows), :].astype(bf16)


def split_product(grid, left, right, dim, more=None):
    rows_all, cols = left.shape[0], right.shape[1]
    operands = [left, right]
    if more is not None:
        operands.append(more)
        cols += more.shape[1]
    outer, count = grid.sizes["hi"], grid.sizes[dim]
    rows = rows_all // (outer * count)
    whole = pl.BlockSpec(memory_space=pltpu.VMEM)
    outs = pl.pallas_call(
        functools.partial(rows_kernel, count, outer, more is not None),
        out_shape=tuple(jax.ShapeDtypeStruct((outer, rows, cols), bf16) for _ in range(count)),
        in_specs=[pl.BlockSpec(memory_space=pltpu.SMEM)] + [whole] * len(operands),
        out_specs=(whole,) * count,
        scratch_shapes=[pltpu.VMEM((rows_all, cols), f32)],
        compiler_params=pltpu.CompilerParams(vmem_limit_bytes=48 * 2**20),
        cost_estimate=pl.CostEstimate(flops=10**6, bytes_accessed=10**5, transcendentals=0),
    )(grid.at[dim].reshape(1).astype(jnp.int32), *operands)
    return outs[0], list(outs[1:])


def back_kernel(bounds, count, *refs):
    parts, weight_ref, outs = refs[:count], refs[count], refs[count + 1 :]
    pieces, rows = outs[0].shape[0], outs[0].shape[1]
    for x in range(pieces):
        for c, out_ref in enumerate(outs):
            here = slice((x * len(outs) + c) * rows, (x * len(outs) + c + 1) * rows)
            total = 0.0
            for i in range(count):
                weight = weight_ref[:, bounds[i] : bounds[i + 1]]
                total = total + lax.dot_general(parts[i][here, :], weight, (((1,), (1,)), ((), ())), preferred_element_type=f32)
            out_ref[x] = total.astype(bf16)


def back_project(grid, parts, weight, bounds):
    nx, nc = grid.sizes["x"], grid.sizes["c"]
    rows = parts[0].shape[0] // (nx * nc)
    whole = pl.BlockSpec(memory_space=pltpu.VMEM)
    return pl.pallas_call(
        functools.partial(back_kernel, bounds, len(parts)),
        out_shape=tuple(jax.ShapeDtypeStruct((nx, rows, weight.shape[0]), bf16) for _ in range(nc)),
        in_specs=[whole] * (len(parts) + 1),
        out_specs=(whole,) * nc,
        compiler_params=pltpu.CompilerParams(vmem_limit_bytes=48 * 2**20),
        cost_estimate=pl.CostEstimate(flops=10**6, bytes_accessed=10**5, transcendentals=0),
    )(*parts, weight)


def hidden_kernel(counts, folds, up_at, down_at, *refs):
    up_refs, down_refs = refs[: counts[0]], refs[counts[0] : counts[0] + counts[1]]
    rest = refs[counts[0] + counts[1] :]
    h2_refs, cot_refs = rest[:2], rest[2:4]
    act_ref, pre_ref, own_ref, sent_ref, up_ref, down_ref, up_sem, down_sem = rest[4:]
    model = up_ref.shape[0]
    rows = up_refs[0].shape[1] // folds
    strip = down_refs[0].shape[1]
    copies, later = [], []
    for ref in up_refs:
        for i in range(ref.shape[0]):
            at = pl.multiple_of(up_at[len(copies) // folds] * rows, rows)
            for f in range(folds):
                piece = ref.at[i, pl.ds(f * rows, rows), :]
                spot = up_ref.at[pl.ds(at, rows), pl.ds(f * model, model)]
                copies.append(pltpu.make_async_copy(piece, spot, up_sem.at[len(copies)]))
    for ref in down_refs:
        for i in range(ref.shape[0]):
            at = pl.multiple_of(down_at[len(later)] * strip, strip)
            later.append(pltpu.make_async_copy(ref.at[i], down_ref.at[pl.ds(at, strip), :], down_sem.at[len(later)]))
    waiting = [copies[f::folds] for f in range(folds)]
    for copy in waiting[0] + later + [copy for fold in waiting[1:] for copy in fold]:
        copy.start()

    def arrive(group):
        while group:
            group.pop().wait()

    half = h2_refs[0].shape[0]
    hidden = up_ref.shape[1]
    width = 256
    root = (2.0 / math.pi) ** 0.5

    def before(item):
        i, at = item
        arrive(waiting[at // model])
        return jnp.dot(h2_refs[i][...], up_ref[:, at : at + width], preferred_element_type=f32)

    ahead = {(0, at): before((0, at)) for at in range(0, model, width)}
    arrive(later)

    def first(item):
        i, at = item
        pre = ahead.pop(item) if item in ahead else before(item)
        back = lax.dot_general(cot_refs[i][...], down_ref[at : at + width, :], (((1,), (1,)), ((), ())), preferred_element_type=f32)
        return pre, back

    def second(item, kept):
        i, at = item
        pre, back = kept
        square = pre * pre
        slope = jnp.tanh(pre * (root + root * 0.044715 * square))
        side = 0.5 + 0.5 * slope
        act_ref[i * half : (i + 1) * half, at : at + width] = (pre * side).astype(bf16)
        steep = side + (0.5 * pre) * (1.0 - slope * slope) * (root + 3 * root * 0.044715 * square)
        pre_ref[i * half : (i + 1) * half, at : at + width] = (steep * back).astype(bf16)

    pipeline([(i, at) for i in range(2) for at in range(0, hidden, width)], first, second, lambda item, kept: None)
    for i, ref in enumerate((own_ref, sent_ref)):
        for at in range(0, half, 256):
            left = pre_ref[i * half + at : i * half + at + 256, :]
            total = lax.dot_general(left, up_ref[...], (((1,), (1,)), ((), ())), preferred_element_type=f32)
            ref[at : at + 256, :] = total.astype(ref.dtype)


def hidden_layer(up_stacks, up_at, down_stacks, down_at, h2_pair, cot_pair, folds):
    half, model = h2_pair[0].shape
    up_count, down_count = sum(one.shape[0] for one in up_stacks), sum(one.shape[0] for one in down_stacks)
    hidden = folds * model
    whole, smem, far = (pl.BlockSpec(memory_space=m) for m in (pltpu.VMEM, pltpu.SMEM, pl.ANY))
    return pl.pallas_call(
        functools.partial(hidden_kernel, (len(up_stacks), len(down_stacks)), folds),
        out_shape=(
            jax.ShapeDtypeStruct((2 * half, hidden), bf16),
            jax.ShapeDtypeStruct((2 * half, hidden), bf16),
            jax.ShapeDtypeStruct((half, model), f32),
            jax.ShapeDtypeStruct((half, model), bf16),
        ),
        in_specs=[smem, smem] + [far] * (len(up_stacks) + len(down_stacks)) + [whole] * 4,
        out_specs=(whole,) * 4,
        scratch_shapes=[
            pltpu.VMEM((model, hidden), bf16),
            pltpu.VMEM((hidden, model), bf16),
            pltpu.SemaphoreType.DMA((up_count * folds,)),
            pltpu.SemaphoreType.DMA((down_count,)),
        ],
        compiler_params=pltpu.CompilerParams(vmem_limit_bytes=50 * 2**20),
        cost_estimate=pl.CostEstimate(flops=14 * 10**9, bytes_accessed=10**6, transcendentals=0),
    )(up_at, down_at, *up_stacks, *down_stacks, *h2_pair, *cot_pair)


def norm_parts(values):
    centered = values - jnp.mean(values, axis=-1, keepdims=True)
    inverse = lax.rsqrt(jnp.mean(centered * centered, axis=-1, keepdims=True) + epsilon)
    return centered * inverse, inverse


def norm_back(normed, inverse, gain, grad):
    c = grad * gain
    return (c - jnp.mean(c, axis=-1, keepdims=True) - normed * jnp.mean(c * normed, axis=-1, keepdims=True)) * inverse


def mm(a, b, dims):
    return lax.dot_general(a, b, ((dims[:1], dims[1:]), ((), ())), preferred_element_type=f32)


def body(
    tokens,
    lengths,
    block_place,
    qkv_weight,
    out_weight,
    up_weight,
    down_weight,
    attn_gain,
    mlp_gain,
    cotangent,
):
    nb, nk = lax.axis_size("pb"), lax.axis_size("ka")
    grid = Grid(nb, nk)
    nx, nc = grid.sizes["x"], grid.sizes["c"]
    x_at, c_at = grid.at["x"], grid.at["c"]
    tok_rows, model = tokens.shape
    shard = qkv_weight.shape[0]
    chips = nb * nx
    heads = -(-HEADS // nk)
    width = heads * HEAD_DIM
    lanes = -(-(3 * width + 2) // BLK) * BLK
    rels = [(xr, cr) for xr in range(nx) for cr in range(nc)]

    def ka_of(xr, cr):
        return ((x_at + xr) % nx) * nc + (c_at + cr) % nc

    def exchange(parts):
        got = [parts(grid.ka)]
        for xr, cr in rels[1:]:
            got.append(grid.fetch(parts(ka_of(-xr, -cr)), x=xr, c=cr))
        return got

    cut = max(1, heads - 1)
    sets = [tuple(range(cut)), tuple(range(cut, heads))] if heads > 1 else [(0,)]
    bounds = [0]
    for one in sets:
        bounds.append(bounds[-1] + 3 * len(one) * HEAD_DIM)

    def head_groups(weight):
        split = weight.reshape(weight.shape[0], 3, HEADS, HEAD_DIM)
        if heads * nk != HEADS:
            split = jnp.pad(split, ((0, 0), (0, 0), (0, heads * nk - HEADS), (0, 0)))
        split = split.reshape(-1, 3, nk, heads, HEAD_DIM)
        chosen = [split[:, :, :, one[0] : one[-1] + 1].transpose(2, 0, 1, 3, 4).reshape(nk, weight.shape[0], -1) for one in sets]
        return jnp.concatenate(chosen, axis=2)

    gains = jnp.stack([attn_gain, mlp_gain], axis=1)
    gains = jnp.pad(gains, ((0, 0), (0, lanes - 3 * width - 2)))
    own_qkv = jnp.concatenate([head_groups(qkv_weight), jnp.broadcast_to(gains[None], (nk,) + gains.shape)], axis=2)
    got = exchange(lambda ka: lax.dynamic_index_in_dim(own_qkv, ka, 0, keepdims=False))
    group_qkv = jnp.concatenate(grid.group_in_order(got), axis=0)

    first_tokens = tie(tokens, *got)
    by_x = [tokens] + [grid.fetch(first_tokens, x=r) for r in range(1, nx)]
    strip = down_weight.shape[0]
    up_split = jnp.transpose(up_weight.reshape(shard, chips, nc, strip), (2, 0, 1, 3)).reshape(nc, shard, chips * strip)
    own, sends = grid.split(up_split, 0, "c")
    up_part = jnp.concatenate(grid.in_order([own] + grid.send(sends, "c"), "c"), axis=0)
    folds = chips * strip // model
    up_part = jnp.concatenate([up_part[:, i * model : (i + 1) * model] for i in range(folds)], axis=0)
    both = jnp.concatenate([up_part, down_weight], axis=0)
    group_qkv, both = together(group_qkv, both)
    got_hi = [grid.fetch(group_qkv[None], hi=r) for r in range(1, grid.sizes["hi"])]
    stack = tie(jnp.stack(by_x), *got_hi)
    from_c = [grid.fetch(stack, c=r) for r in range(1, nc)]
    by_c = [by_x] + [list(one) for one in from_c]
    row_tokens = [by_c[c][x] for x in range(nx) for c in range(nc)]
    qkv_stack = jnp.concatenate([group_qkv[None]] + got_hi, axis=0)
    full_qkv, _ = gather_rows(grid, None, ("lo",), {"place": row_tokens}, qkv_stack)

    full_out = lax.all_gather(tie(out_weight, *got_hi), ("pb", "ka"), axis=0, tiled=True)

    both = tie(both, qkv_stack, *from_c)
    both = grid.gather(both, "hi")

    slots = tok_rows // BLK
    holder = jnp.argsort(block_place[0]).astype(jnp.int32)
    holder_ka, holder_slot = holder // slots, holder % slots
    rel = ((holder_ka // nc - x_at) % nx) * nc + (holder_ka % nc - c_at) % nc
    meta = jnp.concatenate([rel * slots + holder_slot, lengths[0, :1]]).astype(jnp.int32)

    gain_one = full_qkv[:, 3 * width].astype(f32)
    gain_two = full_qkv[:, 3 * width + 1].astype(f32)
    inputs = tokens.astype(f32)
    h1, qkv = project(row_tokens, full_qkv, sets)
    row_len = h1.shape[1]
    up_rows = up_part.shape[0]
    up_stack, down_stack, _ = together(both[:, :up_rows], both[:, up_rows:], qkv)
    qkv = tie(qkv, up_stack, down_stack)
    up_stack = [up_stack] + [grid.fetch(up_stack, x=r) for r in range(1, nx)]
    down_stack = [down_stack] + [grid.fetch(down_stack, lo=r) for r in range(1, grid.sizes["lo"])]
    att_parts, att_row, lse = forward_attention(meta, qkv, sets, nk)
    att_parts, up_stack, down_stack = together(att_parts, up_stack, down_stack)
    up_stack, down_stack = jnp.concatenate(up_stack, axis=0), jnp.concatenate(down_stack, axis=0)
    up_stacks, up_at = gather_rows(grid, None, ("lo",), begun=up_stack, done=("hi", "x"), raw=True)
    down_stacks, down_at = gather_rows(grid, None, ("x",), begun=down_stack, done=("hi", "lo"), raw=True)
    got = [att_parts[0]]
    for xr, cr in rels[1:]:
        got.append(grid.fetch(att_parts[((-xr) % nx) * nc + (-cr) % nc], x=xr, c=cr))
    att = jnp.concatenate(grid.group_in_order(got), axis=0)[: HEADS * HEAD_DIM]

    late_cot = tie(cotangent, att_parts)
    cot_pair = [cotangent] + [grid.fetch(late_cot, c=r) for r in range(1, nc)]
    cots = jnp.concatenate(cot_pair, axis=0)
    att = tie(att, up_stack, down_stack)
    residual = inputs + mm(att, full_out, (0, 0))
    normed_two, inverse_two = norm_parts(residual)
    h2 = (normed_two * gain_two).astype(bf16)
    h2_pair = [h2] + [grid.fetch(h2, c=r) for r in range(1, nc)]
    h2s = jnp.concatenate(h2_pair, axis=0)

    def core_sum(part):
        pieces = part.reshape((nc, tok_rows) + part.shape[1:])
        total = pieces[0]
        for r in range(1, nc):
            total = total + grid.fetch(pieces[(nc - r) % nc].astype(bf16), c=r).astype(f32)
        return total

    if nc == 2 and strip % 16 == 0 and (nc * shard) % 16 == 0 and tok_rows % 256 == 0:
        hidden_low, grad_pre, grad_h2, grad_sent = hidden_layer(up_stacks, up_at, down_stacks, down_at, h2_pair, cot_pair, folds)
        grad_h2 = added(grad_h2, [grid.fetch(grad_sent, c=1)], True)
    else:
        full_up = put_in_place(up_stacks, up_at).reshape(chips, folds, nc * shard, model)
        full_up = jnp.transpose(full_up, (0, 2, 1, 3)).reshape(model, folds * model)
        hidden_act, gelu_back = jax.vjp(lambda v: jax.nn.gelu(v, approximate=True), mm(h2s, full_up, (1, 0)))
        hidden_low = hidden_act.astype(bf16)
        (grad_pre,) = gelu_back(mm(cots, put_in_place(down_stacks, down_at), (1, 1)))
        grad_pre = grad_pre.astype(bf16)
        grad_h2 = core_sum(mm(grad_pre, full_up, (1, 1)))
    grad_up = mm(h2s, grad_pre, (0, 0)).astype(bf16)
    grad_residual = cotangent.astype(f32) + norm_back(normed_two, inverse_two, gain_two, grad_h2)
    grad_res_low = grad_residual.astype(bf16)
    grad_att = mm(full_out, grad_res_low, (1, 1)).astype(bf16)
    if heads * nk != HEADS:
        grad_att = jnp.pad(grad_att, ((0, (heads * nk - HEADS) * HEAD_DIM), (0, 0)))
    grad_att = grad_att.reshape(nk, width, tok_rows)
    upstream = jnp.stack(exchange(lambda ka: lax.dynamic_index_in_dim(grad_att, ka, 0, keepdims=False)))
    late_low, late_res, _ = together(hidden_low, grad_res_low, grad_att)
    grad_down = mm(late_low, cots, (0, 0)).astype(bf16)
    grad_out = mm(att, late_res, (1, 0)).astype(bf16)

    n = grid.sizes

    def placed(grad):
        return grad.reshape(n["hi"], n["lo"], n["x"], -1, grad.shape[1])

    up_own, up_send = grid.split(placed(grad_up), 1, "lo")
    up_got = grid.send(up_send, "lo")
    down_own, down_send = grid.split(placed(grad_down), 2, "x")
    out_own, out_send = grid.split(grad_out.reshape(model, nc, model // nc), 1, "c")
    out_sum = added(out_own, grid.send(out_send, "c"))
    upstream, out_sum, down_send = together(upstream, out_sum, down_send)
    out_own, out_send = grid.split(out_sum.reshape(model, nx, model // nk), 1, "x")
    out_got = grid.send(out_send, "x")
    down_got = grid.send(down_send, "x")

    parts, qkv_rest, qkv_got = [], [], []
    last = len(sets) - 1
    for which in range(len(sets)):
        part = backward_attention(meta, qkv, upstream, att_row, lse, sets, which)
        if which == last:
            part, qkv_got, up_got = together(part, qkv_got, up_got)
        if which == 0:
            part, up_got, out_got = together(part, up_got, out_got)
            out_sum = added(out_own, out_got)
        parts.append(part)
        own, sends = split_product(grid, h1, part, "lo", out_sum if which == 0 else None)
        qkv_rest.append(own)
        qkv_got.append(grid.send(sends, "lo"))
        if which == 0:
            up_own, up_send = grid.halve(added(up_own, up_got), "hi", 0)
            up_got = [grid.swap(up_send, "hi", 0)]
            upstream, down_got, *_ = together(upstream, down_got, up_send, *sends)

    up_own, up_send = grid.halve(added(up_own, up_got), "hi", 1)
    down_own, down_send = grid.split(added(down_own, down_got), 1, "lo")
    up_got = [grid.swap(up_send, "hi", 1)]
    down_got = grid.send(down_send, "lo")
    late_part, *_ = together(parts[-1], *sends)
    grad_h1 = back_project(grid, parts[:-1] + [late_part], full_qkv, bounds)
    h1_got = grid.send([grad_h1[(nc - r) % nc] for r in range(1, nc)], "c")

    qkv_got, h1_got = together(qkv_got, h1_got)
    sums = [added(own, got) for own, got in zip(qkv_rest, qkv_got)]
    by_kind = []
    for kind in range(3):
        for i, one in enumerate(sets):
            begin = kind * len(one) * HEAD_DIM
            by_kind.append(sums[i][:, :, begin : begin + len(one) * HEAD_DIM])
    by_kind.append(sums[0][:, :, 3 * len(sets[0]) * HEAD_DIM :])
    qkv_own, qkv_send = grid.halve(jnp.concatenate(by_kind, axis=2), "hi", 0)
    qkv_got = [grid.swap(qkv_send, "hi", 0)]
    h1_own = added(grad_h1[0], h1_got)
    h1_got = grid.send([h1_own[(nx - r) % nx] for r in range(1, nx)], "x")

    qkv_got, up_got, down_got = together(qkv_got, up_got, down_got)
    qkv_own, qkv_send = grid.halve(added(qkv_own, qkv_got), "hi", 1)
    qkv_got = [grid.swap(qkv_send, "hi", 1)]
    up_own, up_send = grid.split(added(up_own, up_got)[0], 0, "x")
    up_got = grid.send(up_send, "x")
    down_own, down_send = grid.halve(added(down_own, down_got), "hi", 0)
    down_got = [grid.swap(down_send, "hi", 0)]

    low, stacks, _ = together(hidden_low, down_stacks, qkv_send)
    mixed = mm(low, put_in_place(stacks, down_at), (1, 0)).reshape(nc, tok_rows, model)
    mixed_got = [grid.fetch(mixed[(nc - r) % nc].astype(bf16), c=r) for r in range(1, nc)]
    mixed = (residual + added(mixed[0], mixed_got, True)).astype(bf16)

    qkv_got, h1_got, up_got, down_got = together(qkv_got, h1_got, up_got, down_got)
    group_grad = added(qkv_own, qkv_got, True).reshape(nx, nc, shard, -1)
    group_own, group_send = grid.split(group_grad, 0, "x")
    group_got = grid.send(group_send, "x")
    up_own, up_send = grid.split(added(up_own, up_got, True).reshape(nc, shard, -1), 0, "c")
    up_got = grid.send(up_send, "c")
    down_own, down_send = grid.halve(added(down_own, down_got), "hi", 1)
    down_got = [grid.swap(down_send, "hi", 1)]

    group_got, up_got = together(group_got, up_got)
    by_x = grid.in_order([group_own] + group_got, "x")
    group_own, group_send = grid.split(jnp.stack(by_x), 1, "c")
    by_c = grid.in_order([group_own] + grid.send(group_send, "c"), "c")
    got = [by_c[c][x] for x in range(nx) for c in range(nc)]
    sum_up = grid.in_order([up_own] + up_got, "c")

    sum_out = jnp.concatenate([got[x * nc + c][:, 3 * width :] for c in range(nc) for x in range(nx)], axis=1)
    kept = min(nk * width, HEADS * HEAD_DIM)
    sum_qkv = []
    for kind in range(3):
        for i, one in enumerate(got):
            size = min(width, kept - i * width)
            if size > 0:
                sum_qkv.append(one[:, kind * width : kind * width + size])
    sum_qkv = jnp.concatenate(sum_qkv, axis=1)
    sum_up = jnp.stack([one.reshape(shard, chips, strip) for one in sum_up], axis=2).reshape(shard, -1)
    sum_down = added(down_own, down_got, True)[0]
    normed_one, inverse_one = norm_parts(inputs)
    tokens_grad = added(h1_own[0], h1_got, True)
    tokens_grad = (grad_residual + norm_back(normed_one, inverse_one, gain_one, tokens_grad)).astype(bf16)

    grad_gain_one = jnp.sum(sum_qkv * qkv_weight.astype(f32), axis=1) / attn_gain.astype(f32)
    grad_gain_two = jnp.sum(sum_up * up_weight.astype(f32), axis=1) / mlp_gain.astype(f32)
    return (mixed, tokens_grad, sum_qkv, sum_out, sum_up, sum_down, grad_gain_one, grad_gain_two)


def solution(mesh):
    rows = P(("pb", "ka"), None)
    flat = P(("pb", "ka"))
    group = P("pb", None)
    return jax.shard_map(
        body,
        mesh=mesh,
        in_specs=(rows, group, group, rows, rows, rows, rows, flat, flat, rows),
        out_specs=(rows, rows, rows, rows, rows, rows, flat, flat),
        check_vma=False,
    )
```
